32 devices in a mesh: ax: 4 (over y, x), circ: 8 (over z, core).
Axes of the slice: x: 2, y: 2, z: 4, core: 2. Of those that a mesh axis runs over, the one named last changes fastest.
Arguments:
- displace: float32 [3, 512, 16384], P(None, 'ax', 'circ'), may hold values from -6 to 6
- load: float32 [3, 512, 16384], P(None, 'ax', 'circ'), may hold values from -6 to 6
- history: float32 [9, 512, 16384], P(None, 'ax', 'circ'), may hold values from -4 to 4
- stiffen: float32 [512, 16384], P('ax', 'circ'), may hold values from 0.2 to 4
- modulus: float32 [9, 9], replicated, may hold values from -2 to 2
- radial_slope: float32 [32, 32], replicated, may hold values from -1 to 1
- radial_basis: float32 [32, 32], replicated, may hold values from -1 to 1
- axial_eig: float32 [512], replicated, may hold values from 0.05 to 4
- cycle_eig: float32 [512], replicated, may hold values from 0.05 to 4
- radial_eig: float32 [32], replicated, may hold values from 0.05 to 4
Outputs:
- precond: float32 [3, 512, 16384], P(None, ('ax', 'circ'))
The draws below stay inside these ranges and needn't reach their ends.
All inputs are finite; a program needn't handle non-finite values.
Results may differ from the reference program's by a relative error of at most 0.000092.
Values sent between devices are 32-bit elements; how exact they have to be, the bound alone decides.
No kernel may reach another device: no remote copies, remote signals or barrier semaphores. Data moves between devices by JAX's collectives and lax.ppermute only.
A program may use at most 128 MiB of HBM per device.

```python
import math
import jax
import jax.numpy as jnp
from jax import lax

NA = 512
NC = 512
R = 32


def block_levels(rng, shape, split, smallest, high):
    level, own = 1.0, jax.random.fold_in(rng, 6)
    for dim, parts in split:
        heights = jnp.exp(jax.random.uniform(jax.random.fold_in(own, dim), (parts,), jnp.float32, smallest / len(split), high / len(split)))
        level = level * jnp.repeat(heights, shape[dim] // parts).reshape([-1 if axis == dim else 1 for axis in range(len(shape))])
    return level


def normal_values(rng, extent, deviation, reach, shards=(), held_as=jnp.bfloat16):
    values = deviation * jax.random.normal(rng, extent, jnp.float32)
    if shards:
        values = values * block_levels(rng, extent, shards, -0.22, 0.18)
    return jnp.clip(values, -reach, reach).astype(held_as)


def setup_inputs(seed: int = 0) -> dict:
    streams_of = jax.random.split(jax.random.key(seed), 11)
    displace = normal_values(streams_of[0], (3, NA, NC * R), 1.0, 6.0, ((1, 4), (2, 8)), jnp.float32)
    load = normal_values(streams_of[1], (3, NA, NC * R), 1.0, 6.0, ((1, 4), (2, 8)), jnp.float32)
    history = normal_values(streams_of[2], (9, NA, NC * R), 0.5, 4.0, ((1, 4), (2, 8)), jnp.float32)
    stiffen = jnp.clip(jnp.exp(math.log(4.0) - 2.9957323 * jax.random.uniform(streams_of[3], (NA, NC * R), jnp.float32) ** block_levels(streams_of[3], (NA, NC * R), ((0, 4), (1, 8)), -0.2, 0.2)), 0.2, 4.0)
    modulus = normal_values(streams_of[4], (9, 9), 9 ** -0.5, 2.0, (), jnp.float32)
    radial_slope = normal_values(streams_of[5], (R, R), R ** -0.5, 1.0, (), jnp.float32)
    radial_basis = normal_values(streams_of[6], (R, R), R ** -0.5, 1.0, (), jnp.float32)
    axial_eig = jnp.clip(jnp.exp(jax.random.uniform(streams_of[7], (NA,), jnp.float32, math.log(0.05), math.log(4.0))), 0.05, 4.0)
    cycle_eig = jnp.clip(jnp.exp(jax.random.uniform(streams_of[8], (NC,), jnp.float32, math.log(0.05), math.log(4.0))), 0.05, 4.0)
    radial_eig = jnp.clip(jnp.exp(jax.random.uniform(streams_of[9], (R,), jnp.float32, math.log(0.05), math.log(4.0))), 0.05, 4.0)
    return dict(displace=displace, load=load, history=history, stiffen=stiffen, modulus=modulus, radial_slope=radial_slope, radial_basis=radial_basis, axial_eig=axial_eig, cycle_eig=cycle_eig, radial_eig=radial_eig)


def cycle_table(count):
    col = jnp.arange(count, dtype=jnp.int32)[:, None]
    mode = jnp.arange(count, dtype=jnp.int32)[None, :]
    half = count // 2
    folded = jnp.where(mode <= half, mode, mode - half)
    shift = jnp.where(mode <= half, 0.0, 0.5 * math.pi).astype(jnp.float32)
    scale_ends = jnp.where((mode == 0) | (mode == half), math.sqrt(1.0 / count), math.sqrt(2.0 / count)).astype(jnp.float32)
    phase = (col * folded % count).astype(jnp.float32) * (2.0 * math.pi / count)
    return jnp.cos(phase - shift) * scale_ends

def axial_table(rows, count):
    first = (rows + 1)[:, None]
    mode = jnp.arange(count, dtype=jnp.int32)[None, :] + 1
    phase = (first * mode % (2 * (count + 1))).astype(jnp.float32) * (math.pi / (count + 1))
    return jnp.sin(phase) * math.sqrt(2.0 / (count + 1))

def cycle_parts(field):
    left = jnp.roll(field, 1, axis=2)
    right = jnp.roll(field, -1, axis=2)
    return ((left + 4.0 * field + right) / 6.0, (right - left) * 0.5)

def row_smooth(field):
    padded = jnp.pad(field, ((0, 0), (1, 1), (0, 0), (0, 0)))
    return (padded[:, :-2] + 4.0 * padded[:, 1:-1] + padded[:, 2:]) / 6.0

def row_slope(field):
    padded = jnp.pad(field, ((0, 0), (1, 1), (0, 0), (0, 0)))
    return (padded[:, 2:] - padded[:, :-2]) * 0.5

def reference(displace, load, history, stiffen, modulus, radial_slope, radial_basis, axial_eig, cycle_eig, radial_eig):
    high = lax.Precision.HIGHEST
    shape4 = (NA, NC, R)
    field = displace.reshape((3,) + shape4)
    cycle_v, cycle_d = cycle_parts(field)
    smooth_v = row_smooth(cycle_v)
    radial_part = jnp.einsum('iacq,rq->iacr', smooth_v, radial_slope, precision=high)
    grads = jnp.concatenate([row_slope(cycle_v), row_smooth(cycle_d), radial_part], axis=0)
    mixed = jnp.einsum('mn,nacr->macr', modulus, grads, precision=high)
    stress = (1.0 + stiffen.reshape(shape4))[None] * mixed + history.reshape((9,) + shape4)
    first_v, unused_d = cycle_parts(stress[0:3])
    unused_v, second_d = cycle_parts(stress[3:6])
    third_v, unused_e = cycle_parts(stress[6:9])
    third = jnp.einsum('iacr,rq->iacq', row_smooth(third_v), radial_slope, precision=high)
    pull = -row_slope(first_v) - row_smooth(second_d) + third
    resid = load.reshape((3,) + shape4) - pull
    table_cycle = cycle_table(NC)
    table_axial = axial_table(jnp.arange(NA, dtype=jnp.int32), NA)
    spec = jnp.einsum('iacr,ck->iakr', resid, table_cycle, precision=high)
    spec = jnp.einsum('iakr,rm->iakm', spec, radial_basis, precision=high)
    spec = jnp.einsum('iakm,ab->ibkm', spec, table_axial, precision=high)
    denom = axial_eig[:, None, None] + cycle_eig[None, :, None] + radial_eig[None, None, :]
    scaled = spec / denom[None]
    back = jnp.einsum('ibkm,ab->iakm', scaled, table_axial, precision=high)
    back = jnp.einsum('iakm,rm->iakr', back, radial_basis, precision=high)
    back = jnp.einsum('iakr,ck->iacr', back, table_cycle, precision=high)
    return back.reshape(3, NA, NC * R)
```

```python
import math

import functools

import jax
import jax.numpy as jnp
import ml_dtypes
import numpy as np
from jax import lax
from jax.experimental import pallas as pl
from jax.experimental.pallas import tpu as pltpu
from jax.sharding import PartitionSpec as P

NA = 512
NC = 512
R = 32


def with_halo(block, sides, width, periodic):
    for axis, dim in sides:
        count = lax.axis_size(axis)
        forward = [(i, i + 1) for i in range(count - 1)]
        if periodic:
            forward.append((count - 1, 0))
        backward = [(target, source) for source, target in forward]
        low = lax.ppermute(
            lax.slice_in_dim(block, block.shape[dim] - width, None, axis=dim), axis, forward
        )
        high = lax.ppermute(lax.slice_in_dim(block, 0, width, axis=dim), axis, backward)
        block = jnp.concatenate([low, block, high], axis=dim)
    return block


def cycle_table(count):
    col = jnp.arange(count, dtype=jnp.int32)[:, None]
    mode = jnp.arange(count, dtype=jnp.int32)[None, :]
    half = count // 2
    folded = jnp.where(mode <= half, mode, mode - half)
    shift = jnp.where(mode <= half, 0.0, 0.5 * math.pi).astype(jnp.float32)
    scale_ends = jnp.where(
        (mode == 0) | (mode == half), math.sqrt(1.0 / count), math.sqrt(2.0 / count)
    ).astype(jnp.float32)
    phase = (col * folded % count).astype(jnp.float32) * (2.0 * math.pi / count)
    return jnp.cos(phase - shift) * scale_ends


def axial_table(rows, count):
    first = (rows + 1)[:, None]
    mode = jnp.arange(count, dtype=jnp.int32)[None, :] + 1
    phase = (first * mode % (2 * (count + 1))).astype(jnp.float32) * (math.pi / (count + 1))
    return jnp.sin(phase) * math.sqrt(2.0 / (count + 1))


def extend(field):
    rows = with_halo(field, (("ax", 1),), 1, False)
    return with_halo(rows, (("circ", 2),), R, True)


def cycle_parts(ext):
    span = ext.shape[2] - 2 * R
    left = ext[:, :, :span]
    middle = ext[:, :, R : R + span]
    right = ext[:, :, 2 * R :]
    return ((left + 4.0 * middle + right) / 6.0, (right - left) * 0.5)


def row_smooth(field):
    return (field[:, :-2] + 4.0 * field[:, 1:-1] + field[:, 2:]) / 6.0


def row_slope(field):
    return (field[:, 2:] - field[:, :-2]) * 0.5


def radial_mix(field, matrix, form):
    count, rows, flat = field.shape
    cube = field.reshape(count, rows, flat // R, R)
    mixed = jnp.einsum(form, cube, matrix, precision=lax.Precision.HIGHEST)
    return mixed.reshape(count, rows, flat)


def into_cycles(field):
    return lax.all_to_all(field, "circ", split_axis=1, concat_axis=2, tiled=True)


def cycle_forward(field, table, basis):
    count, rows, flat = field.shape
    cube = field.reshape(count * rows, NC, R)
    cube = jnp.einsum("bcr,ck->bkr", cube, table, precision=lax.Precision.HIGHEST)
    cube = jnp.einsum("bkr,rm->bkm", cube, basis, precision=lax.Precision.HIGHEST)
    return cube.reshape(count, rows, flat)


def cycle_inverse(field, table, basis):
    count, rows, flat = field.shape
    cube = field.reshape(count * rows, NC, R)
    cube = jnp.einsum("bkm,rm->bkr", cube, basis, precision=lax.Precision.HIGHEST)
    cube = jnp.einsum("bkr,ck->bcr", cube, table, precision=lax.Precision.HIGHEST)
    return cube.reshape(count, rows, flat)


def axial_solve(lines, forward_table, inverse_table, weights):
    modes = jnp.einsum("pk,cps->cks", forward_table, lines, precision=lax.Precision.HIGHEST)
    return jnp.einsum(
        "ak,cks->cas", inverse_table, modes * weights[None], precision=lax.Precision.HIGHEST
    )


def plain_body(
    displace,
    load,
    history,
    stiffen,
    modulus,
    radial_slope,
    radial_basis,
    axial_eig,
    cycle_eig,
    radial_eig,
):
    ext = extend(displace)
    cycle_v, cycle_d = cycle_parts(ext)
    smooth_v = row_smooth(cycle_v)
    radial_part = radial_mix(smooth_v, radial_slope, "iacq,rq->iacr")
    grads = jnp.concatenate([row_slope(cycle_v), row_smooth(cycle_d), radial_part], axis=0)
    mixed = jnp.einsum("mn,nac->mac", modulus, grads, precision=lax.Precision.HIGHEST)
    stress = (1.0 + stiffen)[None] * mixed + history
    ext_stress = extend(stress)
    first_v, unused_d = cycle_parts(ext_stress[0:3])
    unused_v, second_d = cycle_parts(ext_stress[3:6])
    third_v, unused_e = cycle_parts(ext_stress[6:9])
    third = radial_mix(row_smooth(third_v), radial_slope, "iacr,rq->iacq")
    pull = -row_slope(first_v) - row_smooth(second_d) + third
    resid = load - pull
    a_dev = displace.shape[1]
    flat_dev = displace.shape[2]
    n_ax = lax.axis_size("ax")
    n_circ = lax.axis_size("circ")
    piece = flat_dev // n_ax
    rows_cycle = a_dev // n_circ
    table_cycle = cycle_table(NC)
    spec = cycle_forward(into_cycles(resid), table_cycle, radial_basis)
    start = lax.axis_index("circ") * flat_dev + lax.axis_index("ax") * piece
    index_flat = start + jnp.arange(piece, dtype=jnp.int32)
    denom = (
        axial_eig[:, None]
        + jnp.take(cycle_eig, index_flat // R)[None, :]
        + jnp.take(radial_eig, index_flat % R)[None, :]
    )
    weights = 1.0 / denom
    natural_rows = jnp.arange(NA, dtype=jnp.int32)
    inverse_table = axial_table(natural_rows, NA)
    cube = spec.reshape(3, rows_cycle, n_circ, flat_dev)
    lines = lax.all_to_all(
        lax.all_to_all(cube, "ax", split_axis=3, concat_axis=1, tiled=True),
        "circ",
        split_axis=2,
        concat_axis=1,
        tiled=True,
    ).reshape(3, NA, piece)
    group = n_ax * rows_cycle
    outer = natural_rows // group
    inner = natural_rows % group
    source_rows = inner // rows_cycle * a_dev + outer * rows_cycle + inner % rows_cycle
    forward_table = axial_table(source_rows, NA)
    solved = axial_solve(lines, forward_table, inverse_table, weights)
    cycles_back = lax.all_to_all(
        lax.all_to_all(solved, "ax", split_axis=1, concat_axis=2, tiled=True),
        "circ",
        split_axis=1,
        concat_axis=2,
        tiled=True,
    )
    return cycle_inverse(cycles_back, table_cycle, radial_basis)


BF = jnp.bfloat16
F32 = jnp.float32
VMEM = pl.BlockSpec(memory_space=pltpu.VMEM)
SMEM = pl.BlockSpec(memory_space=pltpu.SMEM)
ANY = pl.BlockSpec(memory_space=pl.ANY)
HALO = 8
LANES = 128


def params():
    return pltpu.CompilerParams(vmem_limit_bytes=48 * 1024 * 1024)


def cost(flops, read):
    return pl.CostEstimate(flops=int(flops), bytes_accessed=int(read), transcendentals=0)


def split(x):
    hi = x.astype(BF)
    return hi, (x - hi.astype(F32)).astype(BF)


def dot(a, b, transposed=False):
    dims = (((1,), (1 if transposed else 0,)), ((), ()))
    return lax.dot_general(a, b, dims, preferred_element_type=F32)


def dot3(ah, al, bh, bl, transposed=False):
    return dot(ah, bh, transposed) + (dot(ah, bl, transposed) + dot(al, bh, transposed))


def exact(a, b, transposed=False):
    dims = (((1,), (1 if transposed else 0,)), ((), ()))
    return lax.dot_general(
        a, b, dims, precision=lax.Precision.HIGHEST, preferred_element_type=F32
    )


def host_split(table):
    hi = table.astype(np.float32).astype(ml_dtypes.bfloat16)
    lo = (table - hi.astype(np.float64)).astype(np.float32).astype(ml_dtypes.bfloat16)
    return jnp.asarray(hi), jnp.asarray(lo)


def host_cycle(count):
    col = np.arange(count)[None, :]
    mode = np.arange(count)[:, None]
    half = count // 2
    folded = np.where(mode <= half, mode, mode - half)
    phase = 2.0 * np.pi * ((col * folded) % count) / count
    scale = np.where((mode == 0) | (mode == half), math.sqrt(1.0 / count), math.sqrt(2.0 / count))
    return np.where(mode <= half, np.cos(phase), np.sin(phase)) * scale


def host_axial(count):
    first = np.arange(1, count + 1)
    phase = np.pi * (np.outer(first, first) % (2 * (count + 1))) / (count + 1)
    return np.sin(phase) * math.sqrt(2.0 / (count + 1))


def host_weave(mp):
    table = np.zeros((mp * LANES, mp * LANES), np.float32)
    for m in range(mp):
        for c in range(LANES):
            table[m * LANES + c, c * mp + m] = 1.0
    return jnp.asarray(table.astype(ml_dtypes.bfloat16))


def iota(shape, dim):
    return lax.broadcasted_iota(jnp.int32, shape, dim)


def onehot(condition):
    return jnp.where(condition, 1.0, 0.0).astype(F32)


def write_split(hi_ref, lo_ref, value):
    hi, lo = split(value)
    hi_ref[...] = hi
    lo_ref[...] = lo


def front_tables_kernel(mp, me_ref, slope_ref, basis_ref, krh, krl, kbh, kbl, kwh, kwl):
    me = me_ref[0]
    slope = slope_ref[...]
    basis = basis_ref[...]
    side = LANES
    row = iota((side, R), 0)
    col = iota((side, R), 1)
    pick = onehot(row % R == col)
    mask = iota((side, side), 0) // R == iota((side, side), 1) // R
    value = exact(exact(pick, slope, True), pick, True)
    write_split(krh, krl, jnp.where(mask, value, 0.0))
    side = 8 * R
    row = iota((side, R), 0)
    col = iota((side, R), 1)
    pick = onehot(row % R == col)
    block = mp * 8
    peer = jnp.bitwise_xor(row // block, me)
    mode = onehot(peer * mp + (row % block) // 8 == col)
    mask = iota((side, side), 0) % 8 == iota((side, side), 1) // R
    value = exact(exact(mode, basis, True), pick, True)
    write_split(kbh, kbl, jnp.where(mask, value, 0.0))
    both = exact(slope, basis)
    value = exact(exact(mode, both, True), pick, True)
    write_split(kwh, kwl, jnp.where(mask, -value, 0.0))


def front_tables(me, slope, basis, mp):
    one = jax.ShapeDtypeStruct((LANES, LANES), BF)
    two = jax.ShapeDtypeStruct((8 * R, 8 * R), BF)
    return pl.pallas_call(
        functools.partial(front_tables_kernel, mp),
        out_shape=(one, one, two, two, two, two),
        in_specs=[SMEM, VMEM, VMEM],
        out_specs=(VMEM,) * 6,
        compiler_params=params(),
        name="front_tables",
    )(me, slope, basis)


def back_tables_kernel(mp, me_ref, basis_ref, hi_ref, lo_ref):
    me = me_ref[0]
    rows, cols = hi_ref.shape
    span = LANES // mp
    row = iota((rows, R), 0)
    col = iota((rows, R), 1)
    peer = jnp.bitwise_xor(row // LANES, me)
    mode = onehot(peer * mp + row % mp == col)
    pick = onehot(iota((cols, R), 0) % R == iota((cols, R), 1))
    value = exact(exact(mode, basis_ref[...], True), pick, True)
    mask = (iota((rows, cols), 0) % LANES) // mp == iota((rows, cols), 1) // R
    write_split(hi_ref, lo_ref, jnp.where(mask, value, 0.0))


def back_tables(me, basis, mp, peers):
    shape = jax.ShapeDtypeStruct((peers * LANES, LANES // mp * R), BF)
    return pl.pallas_call(
        functools.partial(back_tables_kernel, mp),
        out_shape=(shape, shape),
        in_specs=[SMEM, VMEM],
        out_specs=(VMEM, VMEM),
        compiler_params=params(),
        name="back_tables",
    )(me, basis)


def pack_rows_kernel(d_top, d_bot, h_top, h_bot, s_top, s_bot, up_ref, down_ref):
    for i in range(3):
        up_ref[2 * i : 2 * i + 2, :] = d_top[i, 0:2, :]
        down_ref[2 * i : 2 * i + 2, :] = d_bot[i, 6:8, :]
    for n in range(9):
        up_ref[6 + n : 7 + n, :] = h_top[n, 0:1, :]
        down_ref[6 + n : 7 + n, :] = h_bot[n, 7:8, :]
    up_ref[15:16, :] = 1.0 + s_top[0:1, :]
    down_ref[15:16, :] = 1.0 + s_bot[7:8, :]


def pack_rows(displace, history, stiffen):
    rows, flat = stiffen.shape
    last = rows // 8 - 1
    shape = jax.ShapeDtypeStruct((16, flat), F32)
    return pl.pallas_call(
        pack_rows_kernel,
        out_shape=(shape, shape),
        grid=(1,),
        in_specs=[
            pl.BlockSpec((3, 8, flat), lambda g: (0, 0, 0)),
            pl.BlockSpec((3, 8, flat), lambda g: (0, last, 0)),
            pl.BlockSpec((9, 8, flat), lambda g: (0, 0, 0)),
            pl.BlockSpec((9, 8, flat), lambda g: (0, last, 0)),
            pl.BlockSpec((8, flat), lambda g: (0, 0)),
            pl.BlockSpec((8, flat), lambda g: (last, 0)),
        ],
        out_specs=(pl.BlockSpec((16, flat), lambda g: (0, 0)),) * 2,
        compiler_params=params(),
        name="pack_rows",
    )(displace, displace, history, history, stiffen, stiffen)


def pack_cols_kernel(dl, dr, hl, hr, sl, sr, tl, tr, bl, br, left_ref, right_ref, tall):
    rows = sl.shape[0]
    lane = iota((rows + HALO, LANES), 1)

    def column(field, top, bottom, first, count):
        tall[0:rows, :] = field
        tall[rows : rows + HALO, :] = jnp.zeros((HALO, LANES), F32)
        tall[rows : rows + count, :] = bottom[first : first + count, :]
        tall[rows + HALO - count : rows + HALO, :] = top[first : first + count, :]
        return tall[...]

    def place(value, source, target):
        shift = (target - source) % LANES
        return pltpu.roll(value, shift, 1) if shift else value

    for out, d, h, s, top, bottom, wide, slim in (
        (left_ref, dl, hl, sl, tl, bl, 0, 0),
        (right_ref, dr, hr, sr, tr, br, LANES - 2 * R, LANES - R),
    ):
        pieces = [(64 * i, 64, wide, column(d[i], top, bottom, 2 * i, 2)) for i in range(3)]
        pieces += [(192 + 32 * n, 32, slim, column(h[n], top, bottom, 6 + n, 1)) for n in range(9)]
        pieces += [(480, 32, slim, column(1.0 + s[...], top, bottom, 15, 1))]
        for tile in range(4):
            value = None
            for at, width, source, piece in pieces:
                if at // LANES == tile:
                    moved = place(piece, source, at % LANES)
                    if value is None:
                        value = moved
                    else:
                        value = jnp.where(lane >= at % LANES, moved, value)
            out[:, tile * LANES : (tile + 1) * LANES] = value


def pack_cols(displace, history, stiffen, top, bottom):
    rows, flat = stiffen.shape
    last = flat // LANES - 1
    shape = jax.ShapeDtypeStruct((rows + HALO, 4 * LANES), F32)

    def three(count, at):
        return pl.BlockSpec((count, rows, LANES), lambda g: (0, 0, at))

    def two(height, at):
        return pl.BlockSpec((height, LANES), lambda g: (0, at))

    return pl.pallas_call(
        pack_cols_kernel,
        out_shape=(shape, shape),
        grid=(1,),
        in_specs=[
            three(3, 0),
            three(3, last),
            three(9, 0),
            three(9, last),
            two(rows, 0),
            two(rows, last),
            two(16, 0),
            two(16, last),
            two(16, 0),
            two(16, last),
        ],
        out_specs=(pl.BlockSpec((rows + HALO, 4 * LANES), lambda g: (0, 0)),) * 2,
        scratch_shapes=[pltpu.VMEM((rows + HALO, LANES), F32)],
        compiler_params=params(),
        name="pack_cols",
    )(displace, displace, history, history, stiffen, stiffen, top, top, bottom, bottom)


def stencil_kernel(
    comp,
    mp,
    peers,
    modulus,
    displace,
    load,
    history,
    stiffen,
    top,
    bottom,
    left,
    right,
    krh,
    krl,
    kbh,
    kbl,
    kwh,
    kwl,
    *rest,
):
    outs = rest[:peers]
    xd, hx, sx, ld, st, uh, ul, wh, wl, sems = rest[peers:]
    rows, flat = stiffen.shape
    tall = rows + HALO
    tiles = flat // LANES
    center = (slice(0, rows), slice(0, flat))
    copies = [
        pltpu.make_async_copy(displace.at[i], xd.at[(i,) + center], sems.at[i]) for i in range(3)
    ]
    copies += [
        pltpu.make_async_copy(history.at[comp + 3 * k], hx.at[(k,) + center], sems.at[3 + k])
        for k in range(3)
    ]
    copies += [pltpu.make_async_copy(stiffen, sx.at[center], sems.at[6])]
    copies += [pltpu.make_async_copy(load.at[comp], ld, sems.at[7])]
    for copy in copies:
        copy.start()
    lane = iota((tall, LANES), 1)

    def tile_of(ref, at, target):
        value = ref[:, at // LANES * LANES : (at // LANES + 1) * LANES]
        shift = (target - at) % LANES
        return pltpu.roll(value, shift, 1) if shift else value

    halo_rows = slice(rows, tall)
    zeros = jnp.zeros((HALO, flat), F32)
    for i in range(3):
        xd[i, halo_rows, 0:flat] = zeros
        xd[i, rows : rows + 2, 0:flat] = bottom[2 * i : 2 * i + 2, :]
        xd[i, tall - 2 : tall, 0:flat] = top[2 * i : 2 * i + 2, :]
        xd[i, :, flat:] = jnp.where(
            lane < 64, tile_of(right, 64 * i, 0), tile_of(left, 64 * i, 64)
        )
    for k in range(3):
        n = comp + 3 * k
        at = 192 + 32 * n
        hx[k, halo_rows, 0:flat] = zeros
        hx[k, rows : rows + 1, 0:flat] = bottom[6 + n : 7 + n, :]
        hx[k, tall - 1 : tall, 0:flat] = top[6 + n : 7 + n, :]
        hx[k, :, flat:] = jnp.where(lane < 64, tile_of(right, at, 0), tile_of(left, at, 96))
    sx[halo_rows, 0:flat] = zeros
    sx[rows : rows + 1, 0:flat] = bottom[15:16, :] - 1.0
    sx[tall - 1 : tall, 0:flat] = top[15:16, :] - 1.0
    sx[:, flat:] = jnp.where(lane < 64, tile_of(right, 480, 0), tile_of(left, 480, 96)) - 1.0
    for copy in copies:
        copy.wait()

    def lanes(t):
        return pl.ds(pl.multiple_of(t * LANES, LANES), LANES)

    def beside(ref, k, t):
        now = ref[k, :, lanes(t)]
        before = ref[k, :, lanes(lax.rem(t + tiles, tiles + 1))]
        after = ref[k, :, lanes(lax.rem(t + 1, tiles + 1))]
        low = jnp.where(lane < R, pltpu.roll(before, R, 1), pltpu.roll(now, R, 1))
        high = jnp.where(
            lane >= LANES - R, pltpu.roll(after, LANES - R, 1), pltpu.roll(now, LANES - R, 1)
        )
        return low, now, high

    def up(x):
        return pltpu.roll(x, 1, 0)

    def down(x):
        return pltpu.roll(x, tall - 1, 0)

    def stress_step(t, carry):
        total = [None] * 3
        for i in range(3):
            low, now, high = beside(xd, i, t)
            smooth = (low + 4.0 * now + high) * (1.0 / 6.0)
            slope = (high - low) * 0.5
            above, below = up(smooth), down(smooth)
            first = (below - above) * 0.5
            second = (up(slope) + 4.0 * slope + down(slope)) * (1.0 / 6.0)
            both = (above + 4.0 * smooth + below) * (1.0 / 6.0)
            bh, bl = split(both)
            third = dot3(bh, bl, krh[...], krl[...])
            for k in range(3):
                m = comp + 3 * k
                part = (
                    modulus[m, i] * first + modulus[m, 3 + i] * second + modulus[m, 6 + i] * third
                )
                total[k] = part if total[k] is None else total[k] + part
        factor = 1.0 + sx[:, lanes(t)]
        for k in range(3):
            st[k, :, lanes(t)] = factor * total[k] + hx[k, :, lanes(t)]
        return carry

    lax.fori_loop(0, tiles + 1, stress_step, 0)

    def pull_step(t, carry):
        low, now, high = beside(st, 0, t)
        first = (low + 4.0 * now + high) * (1.0 / 12.0)
        low, now, high = beside(st, 1, t)
        second = (high - low) * (1.0 / 12.0)
        mixed = up(second - first) + down(second + first) + 4.0 * second
        u = ld[:, lanes(t)] + mixed[0:rows]
        hi, lo = split(u)
        uh[:, lanes(t)] = hi
        ul[:, lanes(t)] = lo
        low, now, high = beside(st, 2, t)
        third = (low + 4.0 * now + high) * (1.0 / 36.0)
        w = (up(third) + 4.0 * third + down(third))[0:rows]
        hi, lo = split(w)
        wh[:, lanes(t)] = hi
        wl[:, lanes(t)] = lo
        return carry

    lax.fori_loop(0, tiles, pull_step, 0)

    def message_step(t, carry):
        at = pl.ds(pl.multiple_of(t * 2 * LANES, 2 * LANES), 2 * LANES)
        value = dot3(kbh[...], kbl[...], uh[:, at], ul[:, at], True)
        value = value + dot3(kwh[...], kwl[...], wh[:, at], wl[:, at], True)
        here = pl.ds(pl.multiple_of(t * 8, 8), 8)
        for peer in range(peers):
            for m in range(mp):
                row = (peer * mp + m) * 8
                outs[peer][here, m * rows : (m + 1) * rows] = value[row : row + 8, :]
        return carry

    lax.fori_loop(0, tiles // 2, message_step, 0)


def stencil(comp, mp, peers, modulus, displace, load, history, stiffen, halos, tables):
    rows, flat = stiffen.shape
    tall = rows + HALO
    wide = flat + LANES
    shape = jax.ShapeDtypeStruct((flat // R, mp * rows), F32)
    return pl.pallas_call(
        functools.partial(stencil_kernel, comp, mp, peers),
        out_shape=(shape,) * peers,
        in_specs=[SMEM] + [ANY] * 4 + [VMEM] * 10,
        out_specs=(VMEM,) * peers,
        scratch_shapes=[
            pltpu.VMEM((3, tall, wide), F32),
            pltpu.VMEM((3, tall, wide), F32),
            pltpu.VMEM((tall, wide), F32),
            pltpu.VMEM((rows, flat), F32),
            pltpu.VMEM((3, tall, wide), F32),
            pltpu.VMEM((rows, flat), BF),
            pltpu.VMEM((rows, flat), BF),
            pltpu.VMEM((rows, flat), BF),
            pltpu.VMEM((rows, flat), BF),
            pltpu.SemaphoreType.DMA((8,)),
        ],
        compiler_params=params(),
        cost_estimate=cost(2e9, 10 << 20),
        name="stencil",
    )(modulus, displace, load, history, stiffen, *halos, *tables)


def cycle_kernel(peers, parts, ids, *refs):
    ins = refs[:peers]
    th, tl = refs[peers : peers + 2]
    outs = refs[peers + 2 : peers + 2 + parts]
    xh, xl = refs[peers + 2 + parts :]
    height = ins[0].shape[0]
    for j in range(peers):
        source = jnp.bitwise_xor(ids[0], j)
        at = pl.ds(pl.multiple_of(source * height, height), height)
        hi, lo = split(ins[j][...])
        xh[at, :] = hi
        xl[at, :] = lo
    block = outs[0].shape[0]
    for d in range(parts):
        target = jnp.bitwise_xor(ids[1], d)
        at = pl.ds(pl.multiple_of(target * block, block), block)
        outs[d][...] = dot3(th[at, :], tl[at, :], xh[...], xl[...])


def cycle_stage(ids, pieces, table, parts):
    peers = len(pieces)
    height, width = pieces[0].shape
    count = peers * height
    shape = jax.ShapeDtypeStruct((count // parts, width), F32)
    return pl.pallas_call(
        functools.partial(cycle_kernel, peers, parts),
        out_shape=(shape,) * parts,
        in_specs=[SMEM] + [VMEM] * (peers + 2),
        out_specs=(VMEM,) * parts,
        scratch_shapes=[pltpu.VMEM((count, width), BF)] * 2,
        compiler_params=params(),
        cost_estimate=cost(6 * count * count * width, 5 << 20),
        name="cycle_stage",
    )(ids, *pieces, *table)


def axial_kernel(mp, parts, ids, radial, cyc, axial, *refs):
    ins = refs[:parts]
    th, tl = refs[parts : parts + 2]
    outs = refs[parts + 2 : 2 * parts + 2]
    xh, xl = refs[2 * parts + 2 :]
    kc, width = ins[0].shape
    rows = width // mp
    for j in range(parts):
        source = jnp.bitwise_xor(ids[1], j)
        at = pl.ds(pl.multiple_of(source * rows, rows), rows)
        for m in range(mp):
            hi, lo = split(ins[j][:, m * rows : (m + 1) * rows])
            xh[m * kc : (m + 1) * kc, at] = hi
            xl[m * kc : (m + 1) * kc, at] = lo
    mine = cyc[pl.ds(pl.multiple_of(ids[1] * kc, kc), kc), :]
    base = axial[...] + mine
    for m in range(mp):
        part = slice(m * kc, (m + 1) * kc)
        value = dot3(xh[part, :], xl[part, :], th[...], tl[...])
        value = value / (base + radial[ids[0] * mp + m])
        hi, lo = split(value)
        xh[part, :] = hi
        xl[part, :] = lo
    for d in range(parts):
        target = jnp.bitwise_xor(ids[1], d)
        at = pl.ds(pl.multiple_of(target * rows, rows), rows)
        outs[d][...] = dot3(th[at, :], tl[at, :], xh[...], xl[...], True)


def axial_stage(ids, radial, cyc, axial, pieces, table, mp):
    parts = len(pieces)
    kc, width = pieces[0].shape
    rows = width // mp
    shape = jax.ShapeDtypeStruct((rows, mp * kc), F32)
    return pl.pallas_call(
        functools.partial(axial_kernel, mp, parts),
        out_shape=(shape,) * parts,
        in_specs=[SMEM, SMEM] + [VMEM] * (parts + 4),
        out_specs=(VMEM,) * parts,
        scratch_shapes=[pltpu.VMEM((mp * kc, parts * rows), BF)] * 2,
        compiler_params=params(),
        cost_estimate=cost(12 * parts * rows * parts * rows * mp * kc, 5 << 20),
        name="axial_stage",
    )(ids, radial, cyc, axial, *pieces, *table)


def uncycle_kernel(mp, parts, peers, ids, *refs):
    ins = refs[:parts]
    th, tl, weave = refs[parts : parts + 3]
    outs = refs[parts + 3 : parts + 3 + peers]
    xh, xl, full = refs[parts + 3 + peers :]
    rows, width = ins[0].shape
    kc = width // mp
    count = th.shape[1]
    for j in range(parts):
        source = jnp.bitwise_xor(ids[1], j)
        at = pl.ds(pl.multiple_of(source * kc, kc), kc)
        for m in range(mp):
            hi, lo = split(ins[j][:, m * kc : (m + 1) * kc])
            xh[m * rows : (m + 1) * rows, at] = hi
            xl[m * rows : (m + 1) * rows, at] = lo
    value = dot3(xh[...], xl[...], th[...], tl[...])
    hi, lo = split(value)
    span = mp * LANES
    for t in range(count // LANES):
        columns = slice(t * LANES, (t + 1) * LANES)

        def gather(x):
            return jnp.concatenate(
                [x[m * rows : (m + 1) * rows, columns] for m in range(mp)], axis=1
            )

        full[:, t * span : (t + 1) * span] = dot(gather(hi), weave[...]) + dot(
            gather(lo), weave[...]
        )
    few = outs[0].shape[0]
    for d in range(peers):
        target = jnp.bitwise_xor(ids[0], d)
        outs[d][...] = full[pl.ds(pl.multiple_of(target * few, few), few), :]


def uncycle_stage(ids, pieces, table, weave, mp, peers):
    parts = len(pieces)
    rows, width = pieces[0].shape
    count = table[0].shape[0]
    shape = jax.ShapeDtypeStruct((rows // peers, mp * count), F32)
    return pl.pallas_call(
        functools.partial(uncycle_kernel, mp, parts, peers),
        out_shape=(shape,) * peers,
        in_specs=[SMEM] + [VMEM] * (parts + 3),
        out_specs=(VMEM,) * peers,
        scratch_shapes=[
            pltpu.VMEM((mp * rows, count), BF),
            pltpu.VMEM((mp * rows, count), BF),
            pltpu.VMEM((rows, mp * count), F32),
        ],
        compiler_params=params(),
        cost_estimate=cost(8 * mp * rows * count * count, 5 << 20),
        name="uncycle_stage",
    )(ids, *pieces, *table, weave)


def radial_kernel(comp, peers, *refs):
    ins = refs[:peers]
    th, tl = refs[peers : peers + 2]
    out, xh, xl = refs[-3:]
    few, width = ins[0].shape
    groups = width // LANES
    span = th.shape[1]
    for j in range(peers):
        for g in range(groups):
            hi, lo = split(ins[j][:, g * LANES : (g + 1) * LANES])
            xh[g * few : (g + 1) * few, j * LANES : (j + 1) * LANES] = hi
            xl[g * few : (g + 1) * few, j * LANES : (j + 1) * LANES] = lo
    value = dot3(xh[...], xl[...], th[...], tl[...])
    for g in range(groups):
        out[0, :, g * span : (g + 1) * span] = value[g * few : (g + 1) * few, :]


def radial_stage(comp, pieces, table, carried):
    peers = len(pieces)
    few, width = pieces[0].shape
    groups = width // LANES
    depth, span = table[0].shape
    shape = jax.ShapeDtypeStruct((3, few, groups * span), F32)
    extra = [] if carried is None else [carried]
    return pl.pallas_call(
        functools.partial(radial_kernel, comp, peers),
        out_shape=shape,
        grid=(1,),
        in_specs=[VMEM] * (peers + 2) + [ANY] * len(extra),
        out_specs=pl.BlockSpec((1, few, groups * span), lambda g: (comp, 0, 0)),
        scratch_shapes=[pltpu.VMEM((groups * few, depth), BF)] * 2,
        input_output_aliases={peers + 2: 0} if extra else {},
        compiler_params=params(),
        cost_estimate=cost(6 * groups * few * depth * span, 6 << 20),
        name="radial_stage",
    )(*pieces, *table, *extra)


def swap(pieces, axis):
    count = len(pieces)
    return [pieces[0]] + [
        lax.ppermute(pieces[d], axis, [(i, i ^ d) for i in range(count)]) for d in range(1, count)
    ]


def body(
    displace,
    load,
    history,
    stiffen,
    modulus,
    radial_slope,
    radial_basis,
    axial_eig,
    cycle_eig,
    radial_eig,
):
    parts = lax.axis_size("ax")
    peers = lax.axis_size("circ")
    mp = R // peers
    rows, flat = stiffen.shape
    count_a = parts * rows
    count_c = peers * flat // R
    me = lax.axis_index("circ").astype(jnp.int32)
    pe = lax.axis_index("ax").astype(jnp.int32)
    ids = jnp.stack([me, pe])

    upward, downward = pack_rows(displace, history, stiffen)
    ahead = [(i, i + 1) for i in range(parts - 1)]
    bottom = lax.ppermute(upward, "ax", [(j, i) for i, j in ahead])
    top = lax.ppermute(downward, "ax", ahead)
    front = front_tables(ids, radial_slope, radial_basis, mp)
    to_left, to_right = pack_cols(displace, history, stiffen, top, bottom)
    around = [(i, (i + 1) % peers) for i in range(peers)]
    right = lax.ppermute(to_left, "circ", [(j, i) for i, j in around])
    left = lax.ppermute(to_right, "circ", around)
    back = back_tables(ids, radial_basis, mp, peers)
    halos = (top, bottom, left, right)

    cycle_table_parts = host_split(host_cycle(count_c))
    axial_table_parts = host_split(host_axial(count_a))
    weave = host_weave(mp)
    cyc = cycle_eig[:, None]
    axial = axial_eig[None, :]

    out = None
    lines = []
    for i in range(3):
        sent = stencil(
            i, mp, peers, modulus, displace, load, history, stiffen, halos, front
        )
        lines.append(swap(list(sent), "circ"))
    lines = [swap(list(cycle_stage(ids, x, cycle_table_parts, parts)), "ax") for x in lines]
    lines = [
        swap(list(axial_stage(ids, radial_eig, cyc, axial, x, axial_table_parts, mp)), "ax")
        for x in lines
    ]
    lines = [
        swap(list(uncycle_stage(ids, x, cycle_table_parts, weave, mp, peers)), "circ")
        for x in lines
    ]
    for i in range(3):
        out = radial_stage(i, lines[i], back, out)
    return out


def tiled(mesh):
    parts, peers = mesh.shape["ax"], mesh.shape["circ"]
    rows, flat = NA // parts, NC // peers * R
    return (
        parts & (parts - 1) == 0
        and peers & (peers - 1) == 0
        and R == 32
        and R % peers == 0
        and peers * (R // peers) * 8 == 8 * R
        and rows % LANES == 0
        and (NC // parts) % LANES == 0
        and flat % (2 * LANES) == 0
        and (NC // peers) % 16 == 0
        and (rows // peers) % 16 == 0
    )


def solution(mesh):
    return jax.shard_map(
        body if tiled(mesh) else plain_body,
        mesh=mesh,
        in_specs=(
            P(None, "ax", "circ"),
            P(None, "ax", "circ"),
            P(None, "ax", "circ"),
            P("ax", "circ"),
            P(),
            P(),
            P(),
            P(),
            P(),
            P(),
        ),
        out_specs=P(None, ("ax", "circ"), None),
        check_vma=False,
    )
```

```python
import math

import functools

import jax
import jax.numpy as jnp
import ml_dtypes
import numpy as np
from jax import lax
from jax.experimental import pallas as pl
from jax.experimental.pallas import tpu as pltpu
from jax.sharding import PartitionSpec as P

NA = 512
NC = 512
R = 32


def with_halo(block, sides, width, periodic):
    for axis, dim in sides:
        count = lax.axis_size(axis)
        forward = [(i, i + 1) for i in range(count - 1)]
        if periodic:
            forward.append((count - 1, 0))
        backward = [(target, source) for source, target in forward]
        low = lax.ppermute(
            lax.slice_in_dim(block, block.shape[dim] - width, None, axis=dim), axis, forward
        )
        high = lax.ppermute(lax.slice_in_dim(block, 0, width, axis=dim), axis, backward)
        block = jnp.concatenate([low, block, high], axis=dim)
    return block


def cycle_table(count):
    col = jnp.arange(count, dtype=jnp.int32)[:, None]
    mode = jnp.arange(count, dtype=jnp.int32)[None, :]
    half = count // 2
    folded = jnp.where(mode <= half, mode, mode - half)
    shift = jnp.where(mode <= half, 0.0, 0.5 * math.pi).astype(jnp.float32)
    scale_ends = jnp.where(
        (mode == 0) | (mode == half), math.sqrt(1.0 / count), math.sqrt(2.0 / count)
    ).astype(jnp.float32)
    phase = (col * folded % count).astype(jnp.float32) * (2.0 * math.pi / count)
    return jnp.cos(phase - shift) * scale_ends


def axial_table(rows, count):
    first = (rows + 1)[:, None]
    mode = jnp.arange(count, dtype=jnp.int32)[None, :] + 1
    phase = (first * mode % (2 * (count + 1))).astype(jnp.float32) * (math.pi / (count + 1))
    return jnp.sin(phase) * math.sqrt(2.0 / (count + 1))


def extend(field):
    rows = with_halo(field, (("ax", 1),), 1, False)
    return with_halo(rows, (("circ", 2),), R, True)


def cycle_parts(ext):
    span = ext.shape[2] - 2 * R
    left = ext[:, :, :span]
    middle = ext[:, :, R : R + span]
    right = ext[:, :, 2 * R :]
    return ((left + 4.0 * middle + right) / 6.0, (right - left) * 0.5)


def row_smooth(field):
    return (field[:, :-2] + 4.0 * field[:, 1:-1] + field[:, 2:]) / 6.0


def row_slope(field):
    return (field[:, 2:] - field[:, :-2]) * 0.5


def radial_mix(field, matrix, form):
    count, rows, flat = field.shape
    cube = field.reshape(count, rows, flat // R, R)
    mixed = jnp.einsum(form, cube, matrix, precision=lax.Precision.HIGHEST)
    return mixed.reshape(count, rows, flat)


def into_cycles(field):
    return lax.all_to_all(field, "circ", split_axis=1, concat_axis=2, tiled=True)


def cycle_forward(field, table, basis):
    count, rows, flat = field.shape
    cube = field.reshape(count * rows, NC, R)
    cube = jnp.einsum("bcr,ck->bkr", cube, table, precision=lax.Precision.HIGHEST)
    cube = jnp.einsum("bkr,rm->bkm", cube, basis, precision=lax.Precision.HIGHEST)
    return cube.reshape(count, rows, flat)


def cycle_inverse(field, table, basis):
    count, rows, flat = field.shape
    cube = field.reshape(count * rows, NC, R)
    cube = jnp.einsum("bkm,rm->bkr", cube, basis, precision=lax.Precision.HIGHEST)
    cube = jnp.einsum("bkr,ck->bcr", cube, table, precision=lax.Precision.HIGHEST)
    return cube.reshape(count, rows, flat)


def axial_solve(lines, forward_table, inverse_table, weights):
    modes = jnp.einsum("pk,cps->cks", forward_table, lines, precision=lax.Precision.HIGHEST)
    return jnp.einsum(
        "ak,cks->cas", inverse_table, modes * weights[None], precision=lax.Precision.HIGHEST
    )


def plain_body(
    displace,
    load,
    history,
    stiffen,
    modulus,
    radial_slope,
    radial_basis,
    axial_eig,
    cycle_eig,
    radial_eig,
):
    ext = extend(displace)
    cycle_v, cycle_d = cycle_parts(ext)
    smooth_v = row_smooth(cycle_v)
    radial_part = radial_mix(smooth_v, radial_slope, "iacq,rq->iacr")
    grads = jnp.concatenate([row_slope(cycle_v), row_smooth(cycle_d), radial_part], axis=0)
    mixed = jnp.einsum("mn,nac->mac", modulus, grads, precision=lax.Precision.HIGHEST)
    stress = (1.0 + stiffen)[None] * mixed + history
    ext_stress = extend(stress)
    first_v, unused_d = cycle_parts(ext_stress[0:3])
    unused_v, second_d = cycle_parts(ext_stress[3:6])
    third_v, unused_e = cycle_parts(ext_stress[6:9])
    third = radial_mix(row_smooth(third_v), radial_slope, "iacr,rq->iacq")
    pull = -row_slope(first_v) - row_smooth(second_d) + third
    resid = load - pull
    a_dev = displace.shape[1]
    flat_dev = displace.shape[2]
    n_ax = lax.axis_size("ax")
    n_circ = lax.axis_size("circ")
    piece = flat_dev // n_ax
    rows_cycle = a_dev // n_circ
    table_cycle = cycle_table(NC)
    spec = cycle_forward(into_cycles(resid), table_cycle, radial_basis)
    start = lax.axis_index("circ") * flat_dev + lax.axis_index("ax") * piece
    index_flat = start + jnp.arange(piece, dtype=jnp.int32)
    denom = (
        axial_eig[:, None]
        + jnp.take(cycle_eig, index_flat // R)[None, :]
        + jnp.take(radial_eig, index_flat % R)[None, :]
    )
    weights = 1.0 / denom
    natural_rows = jnp.arange(NA, dtype=jnp.int32)
    inverse_table = axial_table(natural_rows, NA)
    cube = spec.reshape(3, rows_cycle, n_circ, flat_dev)
    lines = lax.all_to_all(
        lax.all_to_all(cube, "ax", split_axis=3, concat_axis=1, tiled=True),
        "circ",
        split_axis=2,
        concat_axis=1,
        tiled=True,
    ).reshape(3, NA, piece)
    group = n_ax * rows_cycle
    outer = natural_rows // group
    inner = natural_rows % group
    source_rows = inner // rows_cycle * a_dev + outer * rows_cycle + inner % rows_cycle
    forward_table = axial_table(source_rows, NA)
    solved = axial_solve(lines, forward_table, inverse_table, weights)
    cycles_back = lax.all_to_all(
        lax.all_to_all(solved, "ax", split_axis=1, concat_axis=2, tiled=True),
        "circ",
        split_axis=1,
        concat_axis=2,
        tiled=True,
    )
    return cycle_inverse(cycles_back, table_cycle, radial_basis)


BF = jnp.bfloat16
F32 = jnp.float32
VMEM = pl.BlockSpec(memory_space=pltpu.VMEM)
SMEM = pl.BlockSpec(memory_space=pltpu.SMEM)
HBM = pl.BlockSpec(memory_space=pltpu.HBM)
HALO = 8
PAD = 8
LANES = 128


def params(mebibytes=24):
    return pltpu.CompilerParams(vmem_limit_bytes=mebibytes << 20)


def cost(microseconds):
    return pl.CostEstimate(flops=1, bytes_accessed=int(microseconds * 3.6e6) + 1, transcendentals=0)


def split(x):
    hi = x.astype(BF)
    return hi, (x - hi.astype(F32)).astype(BF)


def dot(a, b, transposed=False):
    dims = (((1,), (1 if transposed else 0,)), ((), ()))
    return lax.dot_general(a, b, dims, preferred_element_type=F32)


def dot3(ah, al, bh, bl, transposed=False):
    return dot(ah, bh, transposed) + (dot(ah, bl, transposed) + dot(al, bh, transposed))


def exact(a, b, transposed=False):
    dims = (((1,), (1 if transposed else 0,)), ((), ()))
    return lax.dot_general(
        a, b, dims, precision=lax.Precision.HIGHEST, preferred_element_type=F32
    )


def host_split(table):
    hi = table.astype(np.float32).astype(ml_dtypes.bfloat16)
    lo = (table - hi.astype(np.float64)).astype(np.float32).astype(ml_dtypes.bfloat16)
    return jnp.asarray(hi), jnp.asarray(lo)


def host_cycle(count):
    col = np.arange(count)[None, :]
    mode = np.arange(count)[:, None]
    half = count // 2
    folded = np.where(mode <= half, mode, mode - half)
    phase = 2.0 * np.pi * ((col * folded) % count) / count
    scale = np.where((mode == 0) | (mode == half), math.sqrt(1.0 / count), math.sqrt(2.0 / count))
    return np.where(mode <= half, np.cos(phase), np.sin(phase)) * scale


def host_axial(count):
    first = np.arange(1, count + 1)
    phase = np.pi * (np.outer(first, first) % (2 * (count + 1))) / (count + 1)
    return np.sin(phase) * math.sqrt(2.0 / (count + 1))


def host_weave(mp):
    table = np.zeros((mp * LANES, mp * LANES), np.float32)
    for m in range(mp):
        for c in range(LANES):
            table[m * LANES + c, c * mp + m] = 1.0
    return jnp.asarray(table.astype(ml_dtypes.bfloat16))


def iota(shape, dim):
    return lax.broadcasted_iota(jnp.int32, shape, dim)


def onehot(condition):
    return jnp.where(condition, 1.0, 0.0).astype(F32)


def write_split(hi_ref, lo_ref, value):
    hi, lo = split(value)
    hi_ref[...] = hi
    lo_ref[...] = lo


TOKEN = jax.ShapeDtypeStruct((8, LANES), F32)


def fetch(sources, targets, sems):
    copies = [
        pltpu.make_async_copy(source, target, sems.at[k])
        for k, (source, target) in enumerate(zip(sources, targets, strict=True))
    ]
    for copy in copies:
        copy.start()
    return copies


def front_tables_kernel(mp, slope_ref, basis_ref, krh, krl, kbh, kbl, kwh, kwl):
    slope = slope_ref[...]
    basis = basis_ref[...]
    side = LANES
    row = iota((side, R), 0)
    col = iota((side, R), 1)
    pick = onehot(row % R == col)
    mask = iota((side, side), 0) // R == iota((side, side), 1) // R
    value = exact(exact(pick, slope, True), pick, True)
    write_split(krh, krl, jnp.where(mask, value * (1.0 / 36.0), 0.0))
    side = 8 * R
    row = iota((side, R), 0)
    col = iota((side, R), 1)
    pick = onehot(row % R == col)
    block = mp * 8
    mode = onehot(row // block * mp + (row % block) // 8 == col)
    mask = iota((side, side), 0) % 8 == iota((side, side), 1) // R
    value = exact(exact(mode, basis, True), pick, True)
    write_split(kbh, kbl, jnp.where(mask, value, 0.0))
    both = exact(slope, basis)
    value = exact(exact(mode, both, True), pick, True)
    write_split(kwh, kwl, jnp.where(mask, value * (-1.0 / 36.0), 0.0))


def front_tables(slope, basis, mp):
    one = jax.ShapeDtypeStruct((LANES, LANES), BF)
    two = jax.ShapeDtypeStruct((8 * R, 8 * R), BF)
    return pl.pallas_call(
        functools.partial(front_tables_kernel, mp),
        out_shape=(one, one, two, two, two, two),
        in_specs=[VMEM, VMEM],
        out_specs=(VMEM,) * 6,
        compiler_params=params(),
        name="front_tables",
    )(slope, basis)


def back_tables_kernel(mp, basis_ref, hi_ref, lo_ref):
    rows, cols = hi_ref.shape
    row = iota((rows, R), 0)
    col = iota((rows, R), 1)
    mode = onehot(row // LANES * mp + row % mp == col)
    pick = onehot(iota((cols, R), 0) % R == iota((cols, R), 1))
    value = exact(exact(mode, basis_ref[...], True), pick, True)
    mask = (iota((rows, cols), 0) % LANES) // mp == iota((rows, cols), 1) // R
    write_split(hi_ref, lo_ref, jnp.where(mask, value, 0.0))


def back_tables(basis, mp, peers):
    shape = jax.ShapeDtypeStruct((peers * LANES, LANES // mp * R), BF)
    return pl.pallas_call(
        functools.partial(back_tables_kernel, mp),
        out_shape=(shape, shape),
        in_specs=[VMEM],
        out_specs=(VMEM, VMEM),
        compiler_params=params(),
        name="back_tables",
    )(basis)


def pack_columns(out, lane, wide, slim, pieces):
    for tile in range(4):
        value = None
        for index, piece in enumerate(pieces):
            at = 64 * index if index < 3 else 96 + 32 * index
            if at // LANES == tile:
                shift = (at - (wide if index < 3 else slim)) % LANES
                moved = pltpu.roll(piece, shift, 1) if shift else piece
                value = moved if value is None else jnp.where(lane >= at % LANES, moved, value)
        out[:, tile * LANES : (tile + 1) * LANES] = value


def pack_kernel(
    displace, history, stiffen, up_ref, down_ref, left_ref, right_ref, d, h, s, dc, hc, sc, sems
):
    rows, flat = stiffen.shape
    sources, targets = [], []
    for k, at in enumerate((slice(0, 8), slice(rows - 8, rows))):
        sources += [displace.at[:, at, :], history.at[:, at, :], stiffen.at[at, :]]
        targets += [d.at[k], h.at[k], s.at[k]]
    for k, at in enumerate((slice(0, LANES), slice(flat - LANES, flat))):
        sources += [displace.at[:, :, at], history.at[:, :, at], stiffen.at[:, at]]
        targets += [dc.at[k], hc.at[k], sc.at[k]]
    copies = fetch(sources, targets, sems)
    for copy in copies[:6]:
        copy.wait()
    for k, first, last, out in ((0, 0, 0, up_ref), (1, 6, 7, down_ref)):
        for i in range(3):
            out[2 * i : 2 * i + 2, :] = d[k, i, first : first + 2, :]
        for n in range(9):
            out[6 + n : 7 + n, :] = h[k, n, last : last + 1, :]
        out[15:16, :] = 1.0 + s[k, last : last + 1, :]
    for copy in copies[6:]:
        copy.wait()
    lane = iota((rows, LANES), 1)
    for k, out, wide, slim in ((0, left_ref, 0, 0), (1, right_ref, LANES - 2 * R, LANES - R)):
        pieces = [dc[k, i] for i in range(3)] + [hc[k, n] for n in range(9)] + [1.0 + sc[k]]
        pack_columns(out, lane, wide, slim, pieces)


def pack(displace, history, stiffen):
    rows, flat = stiffen.shape
    row = jax.ShapeDtypeStruct((16, flat), F32)
    column = jax.ShapeDtypeStruct((rows, 4 * LANES), F32)
    return pl.pallas_call(
        pack_kernel,
        out_shape=(row, row, column, column),
        in_specs=[HBM] * 3,
        out_specs=(VMEM,) * 4,
        scratch_shapes=[
            pltpu.VMEM((2, 3, 8, flat), F32),
            pltpu.VMEM((2, 9, 8, flat), F32),
            pltpu.VMEM((2, 8, flat), F32),
            pltpu.VMEM((2, 3, rows, LANES), F32),
            pltpu.VMEM((2, 9, rows, LANES), F32),
            pltpu.VMEM((2, rows, LANES), F32),
            pltpu.SemaphoreType.DMA((12,)),
        ],
        compiler_params=params(60),
        cost_estimate=cost(0),
        name="pack",
    )(displace, history, stiffen)


def corners_kernel(top, bottom, left_ref, right_ref, tall):
    flat = top.shape[1]
    lane = iota((HALO, LANES), 1)
    tall[...] = jnp.zeros_like(tall)
    for out, at, wide, slim in (
        (left_ref, slice(0, LANES), 0, 0),
        (right_ref, slice(flat - LANES, flat), LANES - 2 * R, LANES - R),
    ):
        pieces = []
        for index in range(13):
            first, count = (2 * index, 2) if index < 3 else (3 + index, 1)
            tall[index, 0:count, :] = bottom[first : first + count, at]
            tall[index, HALO - count : HALO, :] = top[first : first + count, at]
            pieces.append(tall[index])
        pack_columns(out, lane, wide, slim, pieces)


def corners(top, bottom):
    shape = jax.ShapeDtypeStruct((HALO, 4 * LANES), F32)
    return pl.pallas_call(
        corners_kernel,
        out_shape=(shape, shape),
        in_specs=[VMEM] * 2,
        out_specs=(VMEM, VMEM),
        scratch_shapes=[pltpu.VMEM((13, HALO, LANES), F32)],
        compiler_params=params(),
        cost_estimate=cost(0),
        name="corners",
    )(top, bottom)


def stencil_kernel(
    comps,
    mp,
    peers,
    modulus,
    displace,
    load,
    history,
    stiffen,
    top,
    bottom,
    left,
    left_corner,
    right,
    right_corner,
    krh,
    krl,
    kbh,
    kbl,
    kwh,
    kwl,
    after,
    *rest,
):
    n = len(comps)
    outs = rest[:n]
    token, xd, hx, sx, ld, st, sums, diffs, made, sems = rest[n:]
    token[...] = jnp.zeros_like(token)
    rows, flat = stiffen.shape
    tall = rows + HALO
    tiles = flat // LANES
    entries = [comp + 3 * k for comp in comps for k in range(3)]
    center = (slice(0, rows), slice(0, flat))

    def displace_copy(i, t):
        return pltpu.make_async_copy(
            displace.at[i, :, t * LANES : (t + 1) * LANES],
            xd.at[i, t, PAD : PAD + rows, :],
            sems.at[i * tiles + t],
        )

    moves = [displace_copy(i, t) for t in range(tiles) for i in range(3)]
    base = 3 * tiles
    late = [pltpu.make_async_copy(stiffen, sx.at[center], sems.at[base])]
    late += [
        pltpu.make_async_copy(history.at[m], hx.at[(k,) + center], sems.at[base + 1 + k])
        for k, m in enumerate(entries)
    ]
    final = [
        pltpu.make_async_copy(load.at[comp], ld.at[k], sems.at[base + 1 + 3 * n + k])
        for k, comp in enumerate(comps)
    ]
    for copy in moves + late + final:
        copy.start()
    left = (left, left_corner)
    right = (right, right_corner)
    lane = iota((tall, LANES), 1)
    short = iota((rows, LANES), 1)

    def tile_of(refs, at, target):
        part = slice(at // LANES * LANES, (at // LANES + 1) * LANES)
        value = jnp.concatenate([ref[:, part] for ref in refs], axis=0)
        shift = (target - at) % LANES
        return pltpu.roll(value, shift, 1) if shift else value

    for i in range(3):
        tile = jnp.where(lane < 64, tile_of(right, 64 * i, 0), tile_of(left, 64 * i, 64))
        xd[i, tiles, PAD : PAD + tall, :] = tile
        xd[i, tiles, PAD - 1 : PAD, :] = tile[tall - 1 : tall]
        xd[i, tiles, PAD + tall : PAD + tall + 1, :] = tile[0:1]
        for t in range(tiles):
            part = slice(t * LANES, (t + 1) * LANES)
            above = top[2 * i : 2 * i + 2, part]
            xd[i, t, PAD + rows : PAD + rows + 2, :] = bottom[2 * i : 2 * i + 2, part]
            xd[i, t, PAD + tall - 2 : PAD + tall, :] = above
            xd[i, t, PAD - 1 : PAD, :] = above[1:2]
    zeros = jnp.zeros((HALO, flat), F32)
    for k, m in enumerate(entries):
        at = 192 + 32 * m
        hx[k, rows:tall, 0:flat] = zeros
        hx[k, rows : rows + 1, 0:flat] = bottom[6 + m : 7 + m, :]
        hx[k, tall - 1 : tall, 0:flat] = top[6 + m : 7 + m, :]
        hx[k, :, flat:] = jnp.where(lane < 64, tile_of(right, at, 0), tile_of(left, at, 96))
    sx[rows:tall, 0:flat] = zeros
    sx[rows : rows + 1, 0:flat] = bottom[15:16, :] - 1.0
    sx[tall - 1 : tall, 0:flat] = top[15:16, :] - 1.0
    sx[:, flat:] = jnp.where(lane < 64, tile_of(right, 480, 0), tile_of(left, 480, 96)) - 1.0

    def lanes(t):
        return pl.ds(pl.multiple_of(t * LANES, LANES), LANES)

    def previous(t):
        return lax.rem(t + tiles, tiles + 1)

    def following(t):
        return lax.rem(t + 1, tiles + 1)

    def rolled(value, amount):
        return pltpu.roll(value, amount % LANES, 1)

    def lower(ref, k, t, height, mask):
        return jnp.where(mask < R, ref[k, previous(t), 0:height, :], ref[k, t, 0:height, :])

    def higher(ref, k, t, height, mask):
        return jnp.where(
            mask >= LANES - R, ref[k, following(t), 0:height, :], ref[k, t, 0:height, :]
        )

    for copy in moves:
        copy.wait()

    def rows_step(t, carry):
        for i in range(3):
            xd[i, t, PAD + tall : PAD + tall + 1, :] = xd[i, t, PAD : PAD + 1, :]
            above = xd[i, t, PAD - 1 : PAD - 1 + tall, :]
            below = xd[i, t, PAD + 1 : PAD + 1 + tall, :]
            total = above + 4.0 * xd[i, t, PAD : PAD + tall, :] + below
            change = below - above
            sums[3 * i, t] = total
            sums[3 * i + 1, t] = rolled(total, R)
            sums[3 * i + 2, t] = rolled(total, -R)
            diffs[3 * i, t] = change
            diffs[3 * i + 1, t] = rolled(change, R)
            diffs[3 * i + 2, t] = rolled(change, -R)
        return carry

    lax.fori_loop(0, tiles + 1, rows_step, 0)
    for copy in late:
        copy.wait()

    def stress_step(t, carry):
        total = [None] * len(entries)
        for i in range(3):
            low = lower(sums, 3 * i + 1, t, tall, lane)
            high = higher(sums, 3 * i + 2, t, tall, lane)
            second = high - low
            both = low + high + 4.0 * sums[3 * i, t]
            low = lower(diffs, 3 * i + 1, t, tall, lane)
            high = higher(diffs, 3 * i + 2, t, tall, lane)
            first = low + high + 4.0 * diffs[3 * i, t]
            bh, bl = split(both)
            third = dot3(bh, bl, krh[...], krl[...])
            for k, m in enumerate(entries):
                part = (
                    (modulus[m, i] * (1.0 / 12.0)) * first
                    + (modulus[m, 3 + i] * (1.0 / 12.0)) * second
                    + modulus[m, 6 + i] * third
                )
                total[k] = part if total[k] is None else total[k] + part
        factor = 1.0 + sx[:, lanes(t)]
        for k in range(len(entries)):
            value = factor * total[k] + hx[k, :, lanes(t)]
            st[k, t, PAD : PAD + tall, :] = value
            st[k, t, PAD - 1 : PAD, :] = value[tall - 1 : tall]
        return carry

    lax.fori_loop(0, tiles + 1, stress_step, 0)
    for copy in final:
        copy.wait()

    sent = []
    for index in range(n):
        first_entry = 3 * index
        out = made.at[index]

        def pull_rows(t, carry):
            def around(k):
                field = first_entry + k
                return (
                    st[field, t, PAD - 1 : PAD - 1 + rows, :],
                    st[field, t, PAD : PAD + rows, :],
                    st[field, t, PAD + 1 : PAD + 1 + rows, :],
                )

            above, _, below = around(0)
            p = below - above
            above, now, below = around(1)
            q = above + 4.0 * now + below
            above, now, below = around(2)
            w = above + 4.0 * now + below
            sums[0, t, 0:rows, :] = 4.0 * p
            sums[1, t, 0:rows, :] = rolled(p - q, R)
            sums[2, t, 0:rows, :] = rolled(p + q, -R)
            sums[3, t, 0:rows, :] = 4.0 * w
            sums[4, t, 0:rows, :] = rolled(w, R)
            sums[5, t, 0:rows, :] = rolled(w, -R)
            return carry

        lax.fori_loop(0, tiles + 1, pull_rows, 0)

        def message_step(s, carry):
            us, ws = [], []
            for half in range(2):
                t = 2 * s + half
                pull = sums[0, t, 0:rows, :] + lower(sums, 1, t, rows, short)
                pull = pull + higher(sums, 2, t, rows, short)
                us.append(ld[index, :, lanes(t)] + pull * (1.0 / 12.0))
                w = sums[3, t, 0:rows, :] + lower(sums, 4, t, rows, short)
                ws.append(w + higher(sums, 5, t, rows, short))
            uh, ul = split(jnp.concatenate(us, axis=1))
            wh, wl = split(jnp.concatenate(ws, axis=1))
            value = dot3(kbh[...], kbl[...], uh, ul, True)
            value = value + dot3(kwh[...], kwl[...], wh, wl, True)
            here = pl.ds(pl.multiple_of(s * 8, 8), 8)
            for peer in range(peers):
                for m in range(mp):
                    row = (peer * mp + m) * 8
                    out[peer, here, m * rows : (m + 1) * rows] = value[row : row + 8, :]
            return carry

        lax.fori_loop(0, tiles // 2, message_step, 0)
        sent += [pltpu.make_async_copy(out, outs[index], sems.at[base + 1 + 4 * n + index])]
        sent[-1].start()
    for copy in sent:
        copy.wait()


def stencil(comps, mp, peers, modulus, displace, load, history, stiffen, halos, tables, after):
    rows, flat = stiffen.shape
    tall = rows + HALO
    wide = flat + LANES
    tiles = flat // LANES
    n = len(comps)
    shape = jax.ShapeDtypeStruct((peers, flat // R, mp * rows), F32)
    return pl.pallas_call(
        functools.partial(stencil_kernel, comps, mp, peers),
        out_shape=(shape,) * n + (TOKEN,),
        in_specs=[SMEM] + [HBM] * 4 + [VMEM] * 12 + [HBM],
        out_specs=(HBM,) * n + (VMEM,),
        scratch_shapes=[
            pltpu.VMEM((3, tiles + 1, PAD + tall + HALO, LANES), F32),
            pltpu.VMEM((3 * n, tall, wide), F32),
            pltpu.VMEM((tall, wide), F32),
            pltpu.VMEM((n, rows, flat), F32),
            pltpu.VMEM((3 * n, tiles + 1, PAD + tall, LANES), F32),
            pltpu.VMEM((9, tiles + 1, tall, LANES), F32),
            pltpu.VMEM((9, tiles + 1, tall, LANES), F32),
            pltpu.VMEM((n,) + shape.shape, F32),
            pltpu.SemaphoreType.DMA((3 * tiles + 1 + 5 * n,)),
        ],
        compiler_params=params(56),
        cost_estimate=cost(13 + 8 * n),
        name="stencil",
    )(modulus, displace, load, history, stiffen, *halos, *tables, after)


def cycle_kernel(parts, ids, piece, th_ref, tl_ref, after, *refs):
    outs = refs[:parts]
    token, xh, xl, raw, th, tl, sems = refs[parts:]
    token[...] = jnp.zeros_like(token)
    copies = fetch((piece, th_ref, tl_ref), (raw, th, tl), sems)
    copies[0].wait()
    hi, lo = split(raw[...])
    xh[...] = hi
    xl[...] = lo
    copies[1].wait()
    copies[2].wait()
    block = outs[0].shape[0]
    for d in range(parts):
        target = jnp.bitwise_xor(ids[1], d)
        at = pl.ds(pl.multiple_of(target * block, block), block)
        outs[d][...] = dot3(th[at, :], tl[at, :], xh[...], xl[...])


def cycle_stage(ids, piece, table, parts, after):
    count, width = piece.shape
    shape = jax.ShapeDtypeStruct((count // parts, width), F32)
    return pl.pallas_call(
        functools.partial(cycle_kernel, parts),
        out_shape=(shape,) * parts + (TOKEN,),
        in_specs=[SMEM] + [HBM] * 4,
        out_specs=(VMEM,) * (parts + 1),
        scratch_shapes=[
            pltpu.VMEM((count, width), BF),
            pltpu.VMEM((count, width), BF),
            pltpu.VMEM((count, width), F32),
            pltpu.VMEM((count, count), BF),
            pltpu.VMEM((count, count), BF),
            pltpu.SemaphoreType.DMA((3,)),
        ],
        compiler_params=params(),
        cost_estimate=cost(0),
        name="cycle_stage",
    )(ids, piece, *table, after)


def axial_kernel(mp, parts, ids, radial, cyc, axial, *refs):
    ins = refs[:parts]
    th_ref, tl_ref, after = refs[parts : parts + 3]
    outs = refs[parts + 3 : 2 * parts + 3]
    token, xh, xl, raw, th, tl, sems = refs[2 * parts + 3 :]
    token[...] = jnp.zeros_like(token)
    kc, width = ins[0].shape
    rows = width // mp
    copies = fetch([*ins, th_ref, tl_ref], [raw.at[j] for j in range(parts)] + [th, tl], sems)
    for j in range(parts):
        source = jnp.bitwise_xor(ids[1], j)
        at = pl.ds(pl.multiple_of(source * rows, rows), rows)
        copies[j].wait()
        for m in range(mp):
            hi, lo = split(raw[j, :, m * rows : (m + 1) * rows])
            xh[m * kc : (m + 1) * kc, at] = hi
            xl[m * kc : (m + 1) * kc, at] = lo
    copies[parts].wait()
    copies[parts + 1].wait()
    mine = cyc[pl.ds(pl.multiple_of(ids[1] * kc, kc), kc), :]
    base = axial[...] + mine
    for m in range(mp):
        part = slice(m * kc, (m + 1) * kc)
        value = dot3(xh[part, :], xl[part, :], th[...], tl[...])
        value = value / (base + radial[ids[0] * mp + m])
        hi, lo = split(value)
        xh[part, :] = hi
        xl[part, :] = lo
    for d in range(parts):
        target = jnp.bitwise_xor(ids[1], d)
        at = pl.ds(pl.multiple_of(target * rows, rows), rows)
        outs[d][...] = dot3(th[at, :], tl[at, :], xh[...], xl[...], True)


def axial_stage(ids, radial, cyc, axial, pieces, table, mp, after):
    parts = len(pieces)
    kc, width = pieces[0].shape
    rows = width // mp
    shape = jax.ShapeDtypeStruct((rows, mp * kc), F32)
    return pl.pallas_call(
        functools.partial(axial_kernel, mp, parts),
        out_shape=(shape,) * parts + (TOKEN,),
        in_specs=[SMEM, SMEM, VMEM, VMEM] + [HBM] * (parts + 3),
        out_specs=(VMEM,) * (parts + 1),
        scratch_shapes=[
            pltpu.VMEM((mp * kc, parts * rows), BF),
            pltpu.VMEM((mp * kc, parts * rows), BF),
            pltpu.VMEM((parts, kc, width), F32),
            pltpu.VMEM((parts * rows, parts * rows), BF),
            pltpu.VMEM((parts * rows, parts * rows), BF),
            pltpu.SemaphoreType.DMA((parts + 2,)),
        ],
        compiler_params=params(),
        cost_estimate=cost(0),
        name="axial_stage",
    )(ids, radial, cyc, axial, *pieces, *table, after)


def uncycle_kernel(mp, parts, ids, *refs):
    ins = refs[:parts]
    th_ref, tl_ref, weave_ref, after, out = refs[parts : parts + 5]
    token, xh, xl, raw, th, tl, weave, full, sems = refs[parts + 5 :]
    token[...] = jnp.zeros_like(token)
    rows, width = ins[0].shape
    kc = width // mp
    count = th.shape[1]
    copies = fetch(
        [*ins, th_ref, tl_ref, weave_ref],
        [raw.at[j] for j in range(parts)] + [th, tl, weave],
        sems,
    )
    for j in range(parts):
        source = jnp.bitwise_xor(ids[1], j)
        at = pl.ds(pl.multiple_of(source * kc, kc), kc)
        copies[j].wait()
        for m in range(mp):
            hi, lo = split(raw[j, :, m * kc : (m + 1) * kc])
            xh[m * rows : (m + 1) * rows, at] = hi
            xl[m * rows : (m + 1) * rows, at] = lo
    for copy in copies[parts:]:
        copy.wait()
    value = dot3(xh[...], xl[...], th[...], tl[...])
    hi, lo = split(value)
    span = mp * LANES
    sent = []
    for t in range(count // LANES):
        columns = slice(t * LANES, (t + 1) * LANES)

        def gather(x):
            return jnp.concatenate(
                [x[m * rows : (m + 1) * rows, columns] for m in range(mp)], axis=1
            )

        wide = slice(t * span, (t + 1) * span)
        full[:, wide] = dot(gather(hi), weave[...]) + dot(gather(lo), weave[...])
        sent += [pltpu.make_async_copy(full.at[:, wide], out.at[:, wide], sems.at[parts + 3 + t])]
        sent[-1].start()
    for copy in sent:
        copy.wait()


def uncycle_stage(ids, pieces, table, weave, mp, after):
    parts = len(pieces)
    rows, width = pieces[0].shape
    count = table[0].shape[0]
    shape = jax.ShapeDtypeStruct((rows, mp * count), F32)
    return pl.pallas_call(
        functools.partial(uncycle_kernel, mp, parts),
        out_shape=(shape, TOKEN),
        in_specs=[SMEM] + [HBM] * (parts + 4),
        out_specs=(HBM, VMEM),
        scratch_shapes=[
            pltpu.VMEM((mp * rows, count), BF),
            pltpu.VMEM((mp * rows, count), BF),
            pltpu.VMEM((parts, rows, width), F32),
            pltpu.VMEM((count, count), BF),
            pltpu.VMEM((count, count), BF),
            pltpu.VMEM(weave.shape, BF),
            pltpu.VMEM((rows, mp * count), F32),
            pltpu.SemaphoreType.DMA((parts + 3 + count // LANES,)),
        ],
        compiler_params=params(),
        cost_estimate=cost(0),
        name="uncycle_stage",
    )(ids, *pieces, *table, weave, after)


def radial_kernel(comp, piece, th_ref, tl_ref, *refs):
    out, token, xh, xl, raw, th, tl, sems = refs[-8:]
    token[...] = jnp.zeros_like(token)
    peers, few, width = piece.shape
    groups = width // LANES
    span = th.shape[1]
    copies = fetch(
        [piece.at[j] for j in range(peers)] + [th_ref, tl_ref],
        [raw.at[j] for j in range(peers)] + [th, tl],
        sems,
    )
    for j in range(peers):
        copies[j].wait()
        for g in range(groups):
            hi, lo = split(raw[j, :, g * LANES : (g + 1) * LANES])
            xh[g * few : (g + 1) * few, j * LANES : (j + 1) * LANES] = hi
            xl[g * few : (g + 1) * few, j * LANES : (j + 1) * LANES] = lo
    copies[peers].wait()
    copies[peers + 1].wait()
    value = dot3(xh[...], xl[...], th[...], tl[...])
    for g in range(groups):
        out[0, :, g * span : (g + 1) * span] = value[g * few : (g + 1) * few, :]


def radial_stage(comp, piece, table, carried, after):
    peers, few, width = piece.shape
    groups = width // LANES
    depth, span = table[0].shape
    shape = jax.ShapeDtypeStruct((3, few, groups * span), F32)
    extra = [after] if carried is None else [after, carried]
    return pl.pallas_call(
        functools.partial(radial_kernel, comp),
        out_shape=(shape, TOKEN),
        grid=(1,),
        in_specs=[HBM] * (3 + len(extra)),
        out_specs=(pl.BlockSpec((1, few, groups * span), lambda g: (comp, 0, 0)), VMEM),
        scratch_shapes=[
            pltpu.VMEM((groups * few, depth), BF),
            pltpu.VMEM((groups * few, depth), BF),
            pltpu.VMEM((peers, few, width), F32),
            pltpu.VMEM((depth, span), BF),
            pltpu.VMEM((depth, span), BF),
            pltpu.SemaphoreType.DMA((peers + 2,)),
        ],
        input_output_aliases={4: 0} if carried is not None else {},
        compiler_params=params(),
        cost_estimate=cost(0),
        name="radial_stage",
    )(piece, *table, *extra)


def gate_kernel(block, after, out):
    del block, after, out


def gate(block, after):
    return pl.pallas_call(
        gate_kernel,
        out_shape=jax.ShapeDtypeStruct(block.shape, block.dtype),
        in_specs=[HBM, HBM],
        out_specs=HBM,
        input_output_aliases={0: 0},
        compiler_params=params(),
        cost_estimate=cost(0),
        name="gate",
    )(block, after)


def across(block, axis):
    return lax.all_to_all(block, axis, split_axis=0, concat_axis=0, tiled=True)


def swap(pieces, axis):
    count = len(pieces)
    return [pieces[0]] + [
        lax.ppermute(pieces[d], axis, [(i, i ^ d) for i in range(count)]) for d in range(1, count)
    ]


ORDER = (
    ("stencil", (0,)),
    ("send", 0),
    ("stencil", (1, 2)),
    ("send", 1),
    ("cycle", 0),
    ("axial", 0),
    ("send", 2),
    ("cycle", 1),
    ("axial", 1),
    ("uncycle", 0),
    ("cycle", 2),
    ("axial", 2),
    ("uncycle", 1),
    ("radial", 0),
    ("uncycle", 2),
    ("radial", 1),
    ("radial", 2),
)


def body(
    displace,
    load,
    history,
    stiffen,
    modulus,
    radial_slope,
    radial_basis,
    axial_eig,
    cycle_eig,
    radial_eig,
):
    parts = lax.axis_size("ax")
    peers = lax.axis_size("circ")
    mp = R // peers
    rows, flat = stiffen.shape
    count_a = parts * rows
    count_c = peers * flat // R
    me = lax.axis_index("circ").astype(jnp.int32)
    pe = lax.axis_index("ax").astype(jnp.int32)
    ids = jnp.stack([me, pe])

    upward, downward, leftward, rightward = pack(displace, history, stiffen)
    ahead = [(i, i + 1) for i in range(parts - 1)]
    back_ahead = [(j, i) for i, j in ahead]
    around = [(i, (i + 1) % peers) for i in range(peers)]
    back_around = [(j, i) for i, j in around]
    bottom = lax.ppermute(upward, "ax", back_ahead)
    top = lax.ppermute(downward, "ax", ahead)
    right = lax.ppermute(leftward, "circ", back_around)
    left = lax.ppermute(rightward, "circ", around)
    to_left, to_right = corners(top, bottom)
    right_corner = lax.ppermute(to_left, "circ", back_around)
    left_corner = lax.ppermute(to_right, "circ", around)
    front = front_tables(radial_slope, radial_basis, mp)
    back = back_tables(radial_basis, mp, peers)
    halos = (top, bottom, left, left_corner, right, right_corner)

    cycle_table_parts = host_split(host_cycle(count_c))
    axial_table_parts = host_split(host_axial(count_a))
    weave = host_weave(mp)
    cyc = cycle_eig[:, None]
    axial = axial_eig[None, :]

    lines = [None] * 3
    out, token = None, ids
    for step in ORDER:
        kind, i = step
        if kind == "stencil":
            *sent, token = stencil(
                i, mp, peers, modulus, displace, load, history, stiffen, halos, front, token
            )
            for comp, block in zip(i, sent, strict=True):
                lines[comp] = block
        elif kind == "send":
            block = lines[i] if i < 2 else gate(lines[i], token)
            lines[i] = across(block, "circ").reshape(count_c, mp * rows)
        elif kind == "cycle":
            *sent, token = cycle_stage(ids, lines[i], cycle_table_parts, parts, token)
            lines[i] = swap(sent, "ax")
        elif kind == "axial":
            *sent, token = axial_stage(
                ids, radial_eig, cyc, axial, lines[i], axial_table_parts, mp, token
            )
            lines[i] = swap(sent, "ax")
        elif kind == "uncycle":
            sent, token = uncycle_stage(ids, lines[i], cycle_table_parts, weave, mp, token)
            lines[i] = across(sent.reshape(peers, rows // peers, mp * count_c), "circ")
        else:
            out, token = radial_stage(i, lines[i], back, out, token)
    return out


def tiled(mesh):
    parts, peers = mesh.shape["ax"], mesh.shape["circ"]
    rows, flat = NA // parts, NC // peers * R
    return (
        parts & (parts - 1) == 0
        and peers & (peers - 1) == 0
        and R == 32
        and R % peers == 0
        and peers * (R // peers) * 8 == 8 * R
        and rows % LANES == 0
        and (NC // parts) % LANES == 0
        and flat % (2 * LANES) == 0
        and (NC // peers) % 16 == 0
        and (rows // peers) % 16 == 0
    )


def solution(mesh):
    return jax.shard_map(
        body if tiled(mesh) else plain_body,
        mesh=mesh,
        in_specs=(
            P(None, "ax", "circ"),
            P(None, "ax", "circ"),
            P(None, "ax", "circ"),
            P("ax", "circ"),
            P(),
            P(),
            P(),
            P(),
            P(),
            P(),
        ),
        out_specs=P(None, ("ax", "circ"), None),
        check_vma=False,
    )
```

```python
import math

import functools

import jax
import jax.numpy as jnp
import ml_dtypes
import numpy as np
from jax import lax
from jax.experimental import pallas as pl
from jax.experimental.pallas import tpu as pltpu
from jax.sharding import PartitionSpec as P

NA = 512
NC = 512
R = 32


def with_halo(block, sides, width, periodic):
    for axis, dim in sides:
        count = lax.axis_size(axis)
        forward = [(i, i + 1) for i in range(count - 1)]
        if periodic:
            forward.append((count - 1, 0))
        backward = [(target, source) for source, target in forward]
        low = lax.ppermute(
            lax.slice_in_dim(block, block.shape[dim] - width, None, axis=dim), axis, forward
        )
        high = lax.ppermute(lax.slice_in_dim(block, 0, width, axis=dim), axis, backward)
        block = jnp.concatenate([low, block, high], axis=dim)
    return block


def cycle_table(count):
    col = jnp.arange(count, dtype=jnp.int32)[:, None]
    mode = jnp.arange(count, dtype=jnp.int32)[None, :]
    half = count // 2
    folded = jnp.where(mode <= half, mode, mode - half)
    shift = jnp.where(mode <= half, 0.0, 0.5 * math.pi).astype(jnp.float32)
    scale_ends = jnp.where(
        (mode == 0) | (mode == half), math.sqrt(1.0 / count), math.sqrt(2.0 / count)
    ).astype(jnp.float32)
    phase = (col * folded % count).astype(jnp.float32) * (2.0 * math.pi / count)
    return jnp.cos(phase - shift) * scale_ends


def axial_table(rows, count):
    first = (rows + 1)[:, None]
    mode = jnp.arange(count, dtype=jnp.int32)[None, :] + 1
    phase = (first * mode % (2 * (count + 1))).astype(jnp.float32) * (math.pi / (count + 1))
    return jnp.sin(phase) * math.sqrt(2.0 / (count + 1))


def extend(field):
    rows = with_halo(field, (("ax", 1),), 1, False)
    return with_halo(rows, (("circ", 2),), R, True)


def cycle_parts(ext):
    span = ext.shape[2] - 2 * R
    left = ext[:, :, :span]
    middle = ext[:, :, R : R + span]
    right = ext[:, :, 2 * R :]
    return ((left + 4.0 * middle + right) / 6.0, (right - left) * 0.5)


def row_smooth(field):
    return (field[:, :-2] + 4.0 * field[:, 1:-1] + field[:, 2:]) / 6.0


def row_slope(field):
    return (field[:, 2:] - field[:, :-2]) * 0.5


def radial_mix(field, matrix, form):
    count, rows, flat = field.shape
    cube = field.reshape(count, rows, flat // R, R)
    mixed = jnp.einsum(form, cube, matrix, precision=lax.Precision.HIGHEST)
    return mixed.reshape(count, rows, flat)


def into_cycles(field):
    return lax.all_to_all(field, "circ", split_axis=1, concat_axis=2, tiled=True)


def cycle_forward(field, table, basis):
    count, rows, flat = field.shape
    cube = field.reshape(count * rows, NC, R)
    cube = jnp.einsum("bcr,ck->bkr", cube, table, precision=lax.Precision.HIGHEST)
    cube = jnp.einsum("bkr,rm->bkm", cube, basis, precision=lax.Precision.HIGHEST)
    return cube.reshape(count, rows, flat)


def cycle_inverse(field, table, basis):
    count, rows, flat = field.shape
    cube = field.reshape(count * rows, NC, R)
    cube = jnp.einsum("bkm,rm->bkr", cube, basis, precision=lax.Precision.HIGHEST)
    cube = jnp.einsum("bkr,ck->bcr", cube, table, precision=lax.Precision.HIGHEST)
    return cube.reshape(count, rows, flat)


def axial_solve(lines, forward_table, inverse_table, weights):
    modes = jnp.einsum("pk,cps->cks", forward_table, lines, precision=lax.Precision.HIGHEST)
    return jnp.einsum(
        "ak,cks->cas", inverse_table, modes * weights[None], precision=lax.Precision.HIGHEST
    )


def plain_body(
    displace,
    load,
    history,
    stiffen,
    modulus,
    radial_slope,
    radial_basis,
    axial_eig,
    cycle_eig,
    radial_eig,
):
    ext = extend(displace)
    cycle_v, cycle_d = cycle_parts(ext)
    smooth_v = row_smooth(cycle_v)
    radial_part = radial_mix(smooth_v, radial_slope, "iacq,rq->iacr")
    grads = jnp.concatenate([row_slope(cycle_v), row_smooth(cycle_d), radial_part], axis=0)
    mixed = jnp.einsum("mn,nac->mac", modulus, grads, precision=lax.Precision.HIGHEST)
    stress = (1.0 + stiffen)[None] * mixed + history
    ext_stress = extend(stress)
    first_v, unused_d = cycle_parts(ext_stress[0:3])
    unused_v, second_d = cycle_parts(ext_stress[3:6])
    third_v, unused_e = cycle_parts(ext_stress[6:9])
    third = radial_mix(row_smooth(third_v), radial_slope, "iacr,rq->iacq")
    pull = -row_slope(first_v) - row_smooth(second_d) + third
    resid = load - pull
    a_dev = displace.shape[1]
    flat_dev = displace.shape[2]
    n_ax = lax.axis_size("ax")
    n_circ = lax.axis_size("circ")
    piece = flat_dev // n_ax
    rows_cycle = a_dev // n_circ
    table_cycle = cycle_table(NC)
    spec = cycle_forward(into_cycles(resid), table_cycle, radial_basis)
    start = lax.axis_index("circ") * flat_dev + lax.axis_index("ax") * piece
    index_flat = start + jnp.arange(piece, dtype=jnp.int32)
    denom = (
        axial_eig[:, None]
        + jnp.take(cycle_eig, index_flat // R)[None, :]
        + jnp.take(radial_eig, index_flat % R)[None, :]
    )
    weights = 1.0 / denom
    natural_rows = jnp.arange(NA, dtype=jnp.int32)
    inverse_table = axial_table(natural_rows, NA)
    cube = spec.reshape(3, rows_cycle, n_circ, flat_dev)
    lines = lax.all_to_all(
        lax.all_to_all(cube, "ax", split_axis=3, concat_axis=1, tiled=True),
        "circ",
        split_axis=2,
        concat_axis=1,
        tiled=True,
    ).reshape(3, NA, piece)
    group = n_ax * rows_cycle
    outer = natural_rows // group
    inner = natural_rows % group
    source_rows = inner // rows_cycle * a_dev + outer * rows_cycle + inner % rows_cycle
    forward_table = axial_table(source_rows, NA)
    solved = axial_solve(lines, forward_table, inverse_table, weights)
    cycles_back = lax.all_to_all(
        lax.all_to_all(solved, "ax", split_axis=1, concat_axis=2, tiled=True),
        "circ",
        split_axis=1,
        concat_axis=2,
        tiled=True,
    )
    return cycle_inverse(cycles_back, table_cycle, radial_basis)


BF = jnp.bfloat16
F32 = jnp.float32
VMEM = pl.BlockSpec(memory_space=pltpu.VMEM)
SMEM = pl.BlockSpec(memory_space=pltpu.SMEM)
HBM = pl.BlockSpec(memory_space=pltpu.HBM)
HALO = 8
PAD = 8
LANES = 128


def params(mebibytes=60):
    return pltpu.CompilerParams(vmem_limit_bytes=mebibytes << 20)


def cost(microseconds):
    return pl.CostEstimate(flops=1, bytes_accessed=int(microseconds * 3.6e6) + 1, transcendentals=0)


def split(x):
    hi = x.astype(BF)
    return hi, (x - hi.astype(F32)).astype(BF)


def dot(a, b, transposed=False):
    dims = (((1,), (1 if transposed else 0,)), ((), ()))
    return lax.dot_general(a, b, dims, preferred_element_type=F32)


def dot3(ah, al, bh, bl, transposed=False):
    return dot(ah, bh, transposed) + (dot(ah, bl, transposed) + dot(al, bh, transposed))


def stacked3(both, bh, bl, transposed=False):
    rows = both.shape[0] // 2
    upper = dot(both[...], bh, transposed)
    return upper[:rows] + (upper[rows:] + dot(both[0:rows, :], bl, transposed))


def exact(a, b, transposed=False):
    dims = (((1,), (1 if transposed else 0,)), ((), ()))
    return lax.dot_general(
        a, b, dims, precision=lax.Precision.HIGHEST, preferred_element_type=F32
    )


def host_split(table):
    hi = table.astype(np.float32).astype(ml_dtypes.bfloat16)
    lo = (table - hi.astype(np.float64)).astype(np.float32).astype(ml_dtypes.bfloat16)
    return jnp.asarray(np.concatenate([hi, lo], axis=0))


def host_cycle(count):
    col = np.arange(count)[None, :]
    mode = np.arange(count)[:, None]
    half = count // 2
    folded = np.where(mode <= half, mode, mode - half)
    phase = 2.0 * np.pi * ((col * folded) % count) / count
    scale = np.where((mode == 0) | (mode == half), math.sqrt(1.0 / count), math.sqrt(2.0 / count))
    return np.where(mode <= half, np.cos(phase), np.sin(phase)) * scale


def host_axial(count):
    first = np.arange(1, count + 1)
    phase = np.pi * (np.outer(first, first) % (2 * (count + 1))) / (count + 1)
    return np.sin(phase) * math.sqrt(2.0 / (count + 1))


def host_weave(mp):
    table = np.zeros((mp * LANES, mp * LANES), np.float32)
    for m in range(mp):
        for c in range(LANES):
            table[m * LANES + c, c * mp + m] = 1.0
    return jnp.asarray(table.astype(ml_dtypes.bfloat16))


def iota(shape, dim):
    return lax.broadcasted_iota(jnp.int32, shape, dim)


def onehot(condition):
    return jnp.where(condition, 1.0, 0.0).astype(F32)


def write_split(hi_ref, lo_ref, value):
    hi, lo = split(value)
    hi_ref[...] = hi
    lo_ref[...] = lo


def fetch(sources, targets, sems):
    copies = [
        pltpu.make_async_copy(source, target, sems.at[k])
        for k, (source, target) in enumerate(zip(sources, targets, strict=True))
    ]
    for copy in copies:
        copy.start()
    return copies


def write_stack(ref, value):
    rows = value.shape[0]
    hi, lo = split(value)
    ref[0:rows, :] = hi
    ref[rows:, :] = lo


def fetch(sources, targets, sems):
    copies = [
        pltpu.make_async_copy(source, target, sems.at[k])
        for k, (source, target) in enumerate(zip(sources, targets, strict=True))
    ]
    for copy in copies:
        copy.start()
    return copies


def front_tables_kernel(mp, slope_ref, basis_ref, *refs):
    outs, made, sems = refs[:6], refs[6:12], refs[12]
    krh, krl, kbh, kbl, kwh, kwl = made
    slope = slope_ref[...]
    basis = basis_ref[...]
    side = LANES
    row = iota((side, R), 0)
    col = iota((side, R), 1)
    pick = onehot(row % R == col)
    mask = iota((side, side), 0) // R == iota((side, side), 1) // R
    value = exact(exact(pick, slope, True), pick, True)
    write_split(krh, krl, jnp.where(mask, value * (1.0 / 36.0), 0.0))
    side = 8 * R
    row = iota((side, R), 0)
    col = iota((side, R), 1)
    pick = onehot(row % R == col)
    block = mp * 8
    mode = onehot(row // block * mp + (row % block) // 8 == col)
    mask = iota((side, side), 0) % 8 == iota((side, side), 1) // R
    value = exact(exact(mode, basis, True), pick, True)
    write_split(kbh, kbl, jnp.where(mask, value, 0.0))
    both = exact(slope, basis)
    value = exact(exact(mode, both, True), pick, True)
    write_split(kwh, kwl, jnp.where(mask, value * (-1.0 / 36.0), 0.0))
    for copy in fetch(made, outs, sems):
        copy.wait()


def front_tables(slope, basis, mp):
    one = jax.ShapeDtypeStruct((LANES, LANES), BF)
    two = jax.ShapeDtypeStruct((8 * R, 8 * R), BF)
    return pl.pallas_call(
        functools.partial(front_tables_kernel, mp),
        out_shape=(one, one, two, two, two, two),
        in_specs=[VMEM, VMEM],
        out_specs=(HBM,) * 6,
        scratch_shapes=[pltpu.VMEM(x.shape, BF) for x in (one, one, two, two, two, two)]
        + [pltpu.SemaphoreType.DMA((6,))],
        compiler_params=params(),
        name="front_tables",
    )(slope, basis)


def back_tables_kernel(mp, basis_ref, after, out, made, sem):
    del after
    rows, cols = made.shape[0] // 2, made.shape[1]
    row = iota((rows, R), 0)
    col = iota((rows, R), 1)
    mode = onehot(row // LANES * mp + row % mp == col)
    pick = onehot(iota((cols, R), 0) % R == iota((cols, R), 1))
    value = exact(exact(mode, basis_ref[...], True), pick, True)
    mask = (iota((rows, cols), 0) % LANES) // mp == iota((rows, cols), 1) // R
    write_stack(made, jnp.where(mask, value, 0.0))
    copy = pltpu.make_async_copy(made, out, sem)
    copy.start()
    copy.wait()


def back_tables(basis, mp, peers, after):
    shape = jax.ShapeDtypeStruct((2 * peers * LANES, LANES // mp * R), BF)
    return pl.pallas_call(
        functools.partial(back_tables_kernel, mp),
        out_shape=shape,
        in_specs=[VMEM, HBM],
        out_specs=HBM,
        scratch_shapes=[pltpu.VMEM(shape.shape, BF), pltpu.SemaphoreType.DMA],
        compiler_params=params(24),
        name="back_tables",
    )(basis, after)


def pack_columns(out, lane, wide, slim, pieces):
    for tile in range(4):
        value = None
        for index, piece in enumerate(pieces):
            at = 64 * index if index < 3 else 96 + 32 * index
            if at // LANES == tile:
                shift = (at - (wide if index < 3 else slim)) % LANES
                moved = pltpu.roll(piece, shift, 1) if shift else piece
                value = moved if value is None else jnp.where(lane >= at % LANES, moved, value)
        out[:, tile * LANES : (tile + 1) * LANES] = value


def pack_kernel(
    displace, history, stiffen, up_ref, down_ref, left_ref, right_ref, d, h, s, dc, hc, sc, sems
):
    rows, flat = stiffen.shape
    sources, targets = [], []
    for k, at in enumerate((slice(0, 8), slice(rows - 8, rows))):
        sources += [displace.at[:, at, :], history.at[:, at, :], stiffen.at[at, :]]
        targets += [d.at[k], h.at[k], s.at[k]]
    for k, at in enumerate((slice(0, LANES), slice(flat - LANES, flat))):
        sources += [displace.at[:, :, at], history.at[:, :, at], stiffen.at[:, at]]
        targets += [dc.at[k], hc.at[k], sc.at[k]]
    copies = fetch(sources, targets, sems)
    for copy in copies[:6]:
        copy.wait()
    for k, first, last, out in ((0, 0, 0, up_ref), (1, 6, 7, down_ref)):
        for i in range(3):
            out[2 * i : 2 * i + 2, :] = d[k, i, first : first + 2, :]
        for n in range(9):
            out[6 + n : 7 + n, :] = h[k, n, last : last + 1, :]
        out[15:16, :] = 1.0 + s[k, last : last + 1, :]
    for copy in copies[6:]:
        copy.wait()
    lane = iota((rows, LANES), 1)
    for k, out, wide, slim in ((0, left_ref, 0, 0), (1, right_ref, LANES - 2 * R, LANES - R)):
        pieces = [dc[k, i] for i in range(3)] + [hc[k, n] for n in range(9)] + [1.0 + sc[k]]
        pack_columns(out, lane, wide, slim, pieces)


def pack(displace, history, stiffen):
    rows, flat = stiffen.shape
    row = jax.ShapeDtypeStruct((16, flat), F32)
    column = jax.ShapeDtypeStruct((rows, 4 * LANES), F32)
    return pl.pallas_call(
        pack_kernel,
        out_shape=(row, row, column, column),
        in_specs=[HBM] * 3,
        out_specs=(VMEM,) * 4,
        scratch_shapes=[
            pltpu.VMEM((2, 3, 8, flat), F32),
            pltpu.VMEM((2, 9, 8, flat), F32),
            pltpu.VMEM((2, 8, flat), F32),
            pltpu.VMEM((2, 3, rows, LANES), F32),
            pltpu.VMEM((2, 9, rows, LANES), F32),
            pltpu.VMEM((2, rows, LANES), F32),
            pltpu.SemaphoreType.DMA((12,)),
        ],
        compiler_params=params(60),
        cost_estimate=cost(0),
        name="pack",
    )(displace, history, stiffen)


def corners_kernel(top, bottom, left_ref, right_ref, tall):
    flat = top.shape[1]
    lane = iota((HALO, LANES), 1)
    tall[...] = jnp.zeros_like(tall)
    for out, at, wide, slim in (
        (left_ref, slice(0, LANES), 0, 0),
        (right_ref, slice(flat - LANES, flat), LANES - 2 * R, LANES - R),
    ):
        pieces = []
        for index in range(13):
            first, count = (2 * index, 2) if index < 3 else (3 + index, 1)
            tall[index, 0:count, :] = bottom[first : first + count, at]
            tall[index, HALO - count : HALO, :] = top[first : first + count, at]
            pieces.append(tall[index])
        pack_columns(out, lane, wide, slim, pieces)


def corners(top, bottom):
    shape = jax.ShapeDtypeStruct((HALO, 4 * LANES), F32)
    return pl.pallas_call(
        corners_kernel,
        out_shape=(shape, shape),
        in_specs=[VMEM] * 2,
        out_specs=(VMEM, VMEM),
        scratch_shapes=[pltpu.VMEM((13, HALO, LANES), F32)],
        compiler_params=params(),
        cost_estimate=cost(0),
        name="corners",
    )(top, bottom)


def stencil_kernel(
    comps,
    mp,
    peers,
    modulus,
    displace,
    load,
    history,
    stiffen,
    top,
    bottom,
    left,
    left_corner,
    right,
    right_corner,
    *rest,
):
    n = len(comps)
    out, xd, hx, sx, ld, st, sums, diffs, made, krh, krl, kbh, kbl, kwh, kwl, sems = rest[7:]
    rows, flat = stiffen.shape
    tall = rows + HALO
    tiles = flat // LANES
    entries = [comp + 3 * k for comp in comps for k in range(3)]
    center = (slice(0, rows), slice(0, flat))

    def displace_copy(i, t):
        return pltpu.make_async_copy(
            displace.at[i, :, t * LANES : (t + 1) * LANES],
            xd.at[i, t, PAD : PAD + rows, :],
            sems.at[i * tiles + t],
        )

    moves = [displace_copy(i, t) for t in range(tiles) for i in range(3)]
    base = 3 * tiles
    late = [pltpu.make_async_copy(stiffen, sx.at[center], sems.at[base])]
    late += [
        pltpu.make_async_copy(history.at[m], hx.at[(k,) + center], sems.at[base + 1 + k])
        for k, m in enumerate(entries)
    ]
    final = [
        pltpu.make_async_copy(load.at[comp], ld.at[k], sems.at[base + 1 + 3 * n + k])
        for k, comp in enumerate(comps)
    ]
    tables = [
        pltpu.make_async_copy(source, target, sems.at[base + 1 + 5 * n + k])
        for k, (source, target) in enumerate(
            zip(rest[:6], (krh, krl, kbh, kbl, kwh, kwl), strict=True)
        )
    ]
    late += tables[:2]
    final += tables[2:]
    for copy in moves + late + final:
        copy.start()
    left = (left, left_corner)
    right = (right, right_corner)
    lane = iota((tall, LANES), 1)
    short = iota((rows, LANES), 1)

    def tile_of(refs, at, target):
        part = slice(at // LANES * LANES, (at // LANES + 1) * LANES)
        value = jnp.concatenate([ref[:, part] for ref in refs], axis=0)
        shift = (target - at) % LANES
        return pltpu.roll(value, shift, 1) if shift else value

    for i in range(3):
        tile = jnp.where(lane < 64, tile_of(right, 64 * i, 0), tile_of(left, 64 * i, 64))
        xd[i, tiles, PAD : PAD + tall, :] = tile
        xd[i, tiles, PAD - 1 : PAD, :] = tile[tall - 1 : tall]
        xd[i, tiles, PAD + tall : PAD + tall + 1, :] = tile[0:1]
        for t in range(tiles):
            part = slice(t * LANES, (t + 1) * LANES)
            above = top[2 * i : 2 * i + 2, part]
            xd[i, t, PAD + rows : PAD + rows + 2, :] = bottom[2 * i : 2 * i + 2, part]
            xd[i, t, PAD + tall - 2 : PAD + tall, :] = above
            xd[i, t, PAD - 1 : PAD, :] = above[1:2]
    zeros = jnp.zeros((HALO, flat), F32)
    for k, m in enumerate(entries):
        at = 192 + 32 * m
        hx[k, rows:tall, 0:flat] = zeros
        hx[k, rows : rows + 1, 0:flat] = bottom[6 + m : 7 + m, :]
        hx[k, tall - 1 : tall, 0:flat] = top[6 + m : 7 + m, :]
        hx[k, :, flat:] = jnp.where(lane < 64, tile_of(right, at, 0), tile_of(left, at, 96))
    sx[rows:tall, 0:flat] = zeros
    sx[rows : rows + 1, 0:flat] = bottom[15:16, :] - 1.0
    sx[tall - 1 : tall, 0:flat] = top[15:16, :] - 1.0
    sx[:, flat:] = jnp.where(lane < 64, tile_of(right, 480, 0), tile_of(left, 480, 96)) - 1.0

    def lanes(t):
        return pl.ds(pl.multiple_of(t * LANES, LANES), LANES)

    def previous(t):
        return lax.rem(t + tiles, tiles + 1)

    def following(t):
        return lax.rem(t + 1, tiles + 1)

    def rolled(value, amount):
        return pltpu.roll(value, amount % LANES, 1)

    def lower(ref, k, t, height, mask):
        return jnp.where(mask < R, ref[k, previous(t), 0:height, :], ref[k, t, 0:height, :])

    def higher(ref, k, t, height, mask):
        return jnp.where(
            mask >= LANES - R, ref[k, following(t), 0:height, :], ref[k, t, 0:height, :]
        )

    for copy in moves:
        copy.wait()

    def rows_step(t, carry):
        for i in range(3):
            xd[i, t, PAD + tall : PAD + tall + 1, :] = xd[i, t, PAD : PAD + 1, :]
            above = xd[i, t, PAD - 1 : PAD - 1 + tall, :]
            below = xd[i, t, PAD + 1 : PAD + 1 + tall, :]
            total = above + 4.0 * xd[i, t, PAD : PAD + tall, :] + below
            change = below - above
            sums[3 * i, t] = total
            sums[3 * i + 1, t] = rolled(total, R)
            sums[3 * i + 2, t] = rolled(total, -R)
            diffs[3 * i, t] = change
            diffs[3 * i + 1, t] = rolled(change, R)
            diffs[3 * i + 2, t] = rolled(change, -R)
        return carry

    lax.fori_loop(0, tiles + 1, rows_step, 0)
    for copy in late:
        copy.wait()

    def stress_step(t, carry):
        total = [None] * len(entries)
        for i in range(3):
            low = lower(sums, 3 * i + 1, t, tall, lane)
            high = higher(sums, 3 * i + 2, t, tall, lane)
            second = high - low
            both = low + high + 4.0 * sums[3 * i, t]
            low = lower(diffs, 3 * i + 1, t, tall, lane)
            high = higher(diffs, 3 * i + 2, t, tall, lane)
            first = low + high + 4.0 * diffs[3 * i, t]
            bh, bl = split(both)
            third = dot3(bh, bl, krh[...], krl[...])
            for k, m in enumerate(entries):
                part = (
                    (modulus[m, i] * (1.0 / 12.0)) * first
                    + (modulus[m, 3 + i] * (1.0 / 12.0)) * second
                    + modulus[m, 6 + i] * third
                )
                total[k] = part if total[k] is None else total[k] + part
        factor = 1.0 + sx[:, lanes(t)]
        for k in range(len(entries)):
            value = factor * total[k] + hx[k, :, lanes(t)]
            st[k, t, PAD : PAD + tall, :] = value
            st[k, t, PAD - 1 : PAD, :] = value[tall - 1 : tall]
        return carry

    lax.fori_loop(0, tiles + 1, stress_step, 0)
    for copy in final:
        copy.wait()

    sent = []
    for index in range(n):
        first_entry = 3 * index
        message = made.at[index]

        def pull_rows(t, carry):
            def around(k):
                field = first_entry + k
                return (
                    st[field, t, PAD - 1 : PAD - 1 + rows, :],
                    st[field, t, PAD : PAD + rows, :],
                    st[field, t, PAD + 1 : PAD + 1 + rows, :],
                )

            above, _, below = around(0)
            p = below - above
            above, now, below = around(1)
            q = above + 4.0 * now + below
            above, now, below = around(2)
            w = above + 4.0 * now + below
            sums[0, t, 0:rows, :] = 4.0 * p
            sums[1, t, 0:rows, :] = rolled(p - q, R)
            sums[2, t, 0:rows, :] = rolled(p + q, -R)
            sums[3, t, 0:rows, :] = 4.0 * w
            sums[4, t, 0:rows, :] = rolled(w, R)
            sums[5, t, 0:rows, :] = rolled(w, -R)
            return carry

        lax.fori_loop(0, tiles + 1, pull_rows, 0)

        def message_step(s, carry):
            us, ws = [], []
            for half in range(2):
                t = 2 * s + half
                pull = sums[0, t, 0:rows, :] + lower(sums, 1, t, rows, short)
                pull = pull + higher(sums, 2, t, rows, short)
                us.append(ld[index, :, lanes(t)] + pull * (1.0 / 12.0))
                w = sums[3, t, 0:rows, :] + lower(sums, 4, t, rows, short)
                ws.append(w + higher(sums, 5, t, rows, short))
            uh, ul = split(jnp.concatenate(us, axis=1))
            wh, wl = split(jnp.concatenate(ws, axis=1))
            value = dot3(kbh[...], kbl[...], uh, ul, True)
            value = value + dot3(kwh[...], kwl[...], wh, wl, True)
            here = pl.ds(pl.multiple_of(s * 8, 8), 8)
            for peer in range(peers):
                for m in range(mp):
                    row = (peer * mp + m) * 8
                    message[peer, here, m * rows : (m + 1) * rows] = value[row : row + 8, :]
            return carry

        lax.fori_loop(0, tiles // 2, message_step, 0)
        sent += [pltpu.make_async_copy(message, out.at[:, index], sems.at[base + 1 + 4 * n + index])]
        sent[-1].start()
    for copy in sent:
        copy.wait()


def stencil(comps, mp, peers, modulus, displace, load, history, stiffen, halos, tables, after):
    rows, flat = stiffen.shape
    tall = rows + HALO
    wide = flat + LANES
    tiles = flat // LANES
    n = len(comps)
    block = (flat // R, mp * rows)
    return pl.pallas_call(
        functools.partial(stencil_kernel, comps, mp, peers),
        out_shape=jax.ShapeDtypeStruct((peers, n) + block, F32),
        in_specs=[SMEM] + [HBM] * 4 + [VMEM] * 6 + [HBM] * 7,
        out_specs=HBM,
        scratch_shapes=[
            pltpu.VMEM((3, tiles + 1, PAD + tall + HALO, LANES), F32),
            pltpu.VMEM((3 * n, tall, wide), F32),
            pltpu.VMEM((tall, wide), F32),
            pltpu.VMEM((n, rows, flat), F32),
            pltpu.VMEM((3 * n, tiles + 1, PAD + tall, LANES), F32),
            pltpu.VMEM((9, tiles + 1, tall, LANES), F32),
            pltpu.VMEM((9, tiles + 1, tall, LANES), F32),
            pltpu.VMEM((n, peers) + block, F32),
            *(pltpu.VMEM(table.shape, BF) for table in tables),
            pltpu.SemaphoreType.DMA((3 * tiles + 7 + 5 * n,)),
        ],
        compiler_params=params(),
        cost_estimate=cost(13 + 8 * n),
        name="stencil",
    )(modulus, displace, load, history, stiffen, *halos, *tables, after)


def cycle_kernel(index, parts, ids, piece, table_ref, after, *refs):
    del after
    outs = refs[:parts]
    xh, xl, raw, table, made, sems = refs[parts:]
    peers, _, height, _ = piece.shape
    copies = fetch(
        [piece.at[j, index] for j in range(peers)] + [table_ref],
        [raw.at[j] for j in range(peers)] + [table],
        sems,
    )
    for j in range(peers):
        copies[j].wait()
        at = slice(j * height, (j + 1) * height)
        hi, lo = split(raw[j])
        xh[at, :] = hi
        xl[at, :] = lo
    copies[peers].wait()
    value = stacked3(table, xh[...], xl[...])
    block = outs[0].shape[0]
    for b in range(parts):
        made[jnp.bitwise_xor(ids[1], b)] = value[b * block : (b + 1) * block]
    sent = fetch([made.at[d] for d in range(parts)], outs, sems.at[pl.ds(peers + 1, parts)])
    for copy in sent:
        copy.wait()


def cycle_stage(index, ids, piece, table, parts, after):
    peers, _, height, width = piece.shape
    count = peers * height
    shape = jax.ShapeDtypeStruct((count // parts, width), F32)
    return pl.pallas_call(
        functools.partial(cycle_kernel, index, parts),
        out_shape=(shape,) * parts,
        in_specs=[SMEM] + [HBM] * 3,
        out_specs=(HBM,) * parts,
        scratch_shapes=[
            pltpu.VMEM((count, width), BF),
            pltpu.VMEM((count, width), BF),
            pltpu.VMEM((peers, height, width), F32),
            pltpu.VMEM(table.shape, BF),
            pltpu.VMEM((parts,) + shape.shape, F32),
            pltpu.SemaphoreType.DMA((peers + 1 + parts,)),
        ],
        compiler_params=params(24),
        cost_estimate=cost(0),
        name="cycle_stage",
    )(ids, piece, table, after)


def axial_kernel(mp, parts, ids, radial, cyc, axial, *refs):
    ins = refs[:parts]
    table_ref, after, out, x, xh, xl, raw, table, made, sems = refs[parts:]
    del after
    kc, width = ins[0].shape
    rows = width // mp
    half = mp * kc
    count = parts * rows
    copies = fetch([*ins, table_ref], [raw.at[j] for j in range(parts)] + [table], sems)
    for j in range(parts):
        source = jnp.bitwise_xor(ids[1], j)
        at = pl.ds(pl.multiple_of(source * rows, rows), rows)
        copies[j].wait()
        for m in range(mp):
            hi, lo = split(raw[j, :, m * rows : (m + 1) * rows])
            x[m * kc : (m + 1) * kc, at] = hi
            x[half + m * kc : half + (m + 1) * kc, at] = lo
    copies[parts].wait()
    mine = cyc[pl.ds(pl.multiple_of(ids[1] * kc, kc), kc), :]
    base = axial[...] + mine
    value = stacked3(x, table[0:count, :], table[count:, :])
    for m in range(mp):
        part = slice(m * kc, (m + 1) * kc)
        hi, lo = split(value[part] / (base + radial[ids[0] * mp + m]))
        xh[part, :] = hi
        xl[part, :] = lo
    made[...] = stacked3(table, xh[...], xl[...], True)
    copy = pltpu.make_async_copy(made, out, sems.at[parts + 1])
    copy.start()
    copy.wait()


def axial_stage(ids, radial, cyc, axial, pieces, table, mp, after):
    parts = len(pieces)
    kc, width = pieces[0].shape
    count = width // mp * parts
    return pl.pallas_call(
        functools.partial(axial_kernel, mp, parts),
        out_shape=jax.ShapeDtypeStruct((count, mp * kc), F32),
        in_specs=[SMEM, SMEM, VMEM, VMEM] + [HBM] * (parts + 2),
        out_specs=HBM,
        scratch_shapes=[
            pltpu.VMEM((2 * mp * kc, count), BF),
            pltpu.VMEM((mp * kc, count), BF),
            pltpu.VMEM((mp * kc, count), BF),
            pltpu.VMEM((parts, kc, width), F32),
            pltpu.VMEM(table.shape, BF),
            pltpu.VMEM((count, mp * kc), F32),
            pltpu.SemaphoreType.DMA((parts + 2,)),
        ],
        compiler_params=params(24),
        cost_estimate=cost(0),
        name="axial_stage",
    )(ids, radial, cyc, axial, *pieces, table, after)


def return_kernel(comp, mp, parts, peers, piece, *refs):
    out, x, y, raw, table, weave, kernel, made, sems = refs[-9:]
    _, few, width = piece.shape
    kc = width // mp
    count = table.shape[1]
    depth, span = kernel.shape[0] // 2, kernel.shape[1]
    half = mp * peers * few
    groups = count * mp // LANES
    copies = fetch((piece, *refs[:3]), (raw, table, weave, kernel), sems)
    copies[0].wait()
    for p in range(parts):
        for q in range(peers):
            for m in range(mp):
                row = (m * peers + q) * few
                hi, lo = split(raw[p * peers + q, :, m * kc : (m + 1) * kc])
                x[row : row + few, p * kc : (p + 1) * kc] = hi
                x[half + row : half + row + few, p * kc : (p + 1) * kc] = lo
    for copy in copies[1:]:
        copy.wait()
    value = split(stacked3(x, table[0:count, :], table[count:, :]))
    rows = peers * few
    for t in range(count // LANES):
        columns = slice(t * LANES, (t + 1) * LANES)
        for part, first in zip(value, (0, groups * few), strict=True):
            gathered = jnp.concatenate(
                [part[m * rows : (m + 1) * rows, columns] for m in range(mp)], axis=1
            )
            woven = dot(gathered, weave[...]).astype(BF)
            for g in range(mp):
                for q in range(peers):
                    row = first + (t * mp + g) * few
                    y[row : row + few, q * LANES : (q + 1) * LANES] = woven[
                        q * few : (q + 1) * few, g * LANES : (g + 1) * LANES
                    ]
    result = stacked3(y, kernel[0:depth, :], kernel[depth:, :])
    for g in range(groups):
        made[:, g * span : (g + 1) * span] = result[g * few : (g + 1) * few, :]
    copy = pltpu.make_async_copy(made, out.at[comp], sems.at[4])
    copy.start()
    copy.wait()


def return_stage(comp, piece, table, weave, back, mp, parts, carried):
    devices, few, width = piece.shape
    peers = devices // parts
    count = table.shape[1]
    depth, span = back.shape[0] // 2, back.shape[1]
    groups = count * mp // LANES
    extra = [] if carried is None else [carried]
    return pl.pallas_call(
        functools.partial(return_kernel, comp, mp, parts, peers),
        out_shape=jax.ShapeDtypeStruct((3, few, groups * span), F32),
        in_specs=[HBM] * (4 + len(extra)),
        out_specs=HBM,
        scratch_shapes=[
            pltpu.VMEM((2 * mp * peers * few, count), BF),
            pltpu.VMEM((2 * groups * few, depth), BF),
            pltpu.VMEM(piece.shape, F32),
            pltpu.VMEM(table.shape, BF),
            pltpu.VMEM(weave.shape, BF),
            pltpu.VMEM(back.shape, BF),
            pltpu.VMEM((few, groups * span), F32),
            pltpu.SemaphoreType.DMA((5,)),
        ],
        input_output_aliases={4: 0} if extra else {},
        compiler_params=params(32),
        cost_estimate=cost(0),
        name="return_stage",
    )(piece, table, weave, back, *extra)


def across(block, axis):
    return lax.all_to_all(block, axis, split_axis=0, concat_axis=0, tiled=True)


def swap(pieces, axis):
    count = len(pieces)
    return [pieces[0]] + [
        lax.ppermute(pieces[d], axis, [(i, i ^ d) for i in range(count)]) for d in range(1, count)
    ]


ORDER = (
    ("stencil", (0,)),
    ("stencil", (1, 2)),
    ("cycle", 0),
    ("tables", None),
    ("axial", 0),
    ("cycle", 1),
    ("axial", 1),
    ("cycle", 2),
    ("return", 0),
    ("axial", 2),
    ("return", 1),
    ("return", 2),
)


def body(
    displace,
    load,
    history,
    stiffen,
    modulus,
    radial_slope,
    radial_basis,
    axial_eig,
    cycle_eig,
    radial_eig,
):
    parts = lax.axis_size("ax")
    peers = lax.axis_size("circ")
    mp = R // peers
    rows, flat = stiffen.shape
    count_a = parts * rows
    count_c = peers * flat // R
    me = lax.axis_index("circ").astype(jnp.int32)
    pe = lax.axis_index("ax").astype(jnp.int32)
    ids = jnp.stack([me, pe])

    upward, downward, leftward, rightward = pack(displace, history, stiffen)
    ahead = [(i, i + 1) for i in range(parts - 1)]
    back_ahead = [(j, i) for i, j in ahead]
    around = [(i, (i + 1) % peers) for i in range(peers)]
    back_around = [(j, i) for i, j in around]
    bottom = lax.ppermute(upward, "ax", back_ahead)
    top = lax.ppermute(downward, "ax", ahead)
    right = lax.ppermute(leftward, "circ", back_around)
    left = lax.ppermute(rightward, "circ", around)
    to_left, to_right = corners(top, bottom)
    right_corner = lax.ppermute(to_left, "circ", back_around)
    left_corner = lax.ppermute(to_right, "circ", around)
    front = front_tables(radial_slope, radial_basis, mp)
    halos = (top, bottom, left, left_corner, right, right_corner)

    cycle_table_stack = host_split(host_cycle(count_c))
    axial_table_stack = host_split(host_axial(count_a))
    weave = host_weave(mp)
    cyc = cycle_eig[:, None]
    axial = axial_eig[None, :]

    lines = [None] * 3
    out, after = None, ids
    for kind, i in ORDER:
        if kind == "stencil":
            after = stencil(
                i, mp, peers, modulus, displace, load, history, stiffen, halos, front, after
            )
            block = across(after, "circ")
            for index, comp in enumerate(i):
                lines[comp] = (index, block)
        elif kind == "tables":
            after = back = back_tables(radial_basis, mp, peers, after)
        elif kind == "cycle":
            index, block = lines[i]
            sent = cycle_stage(index, ids, block, cycle_table_stack, parts, after)
            after = sent[0]
            lines[i] = swap(list(sent), "ax")
        elif kind == "axial":
            after = axial_stage(
                ids, radial_eig, cyc, axial, lines[i], axial_table_stack, mp, after
            )
            block = after.reshape(parts * peers, rows // peers, -1)
            lines[i] = across(block, ("ax", "circ"))
        else:
            out = return_stage(i, lines[i], cycle_table_stack, weave, back, mp, parts, out)
            after = out
    return out


def tiled(mesh):
    parts, peers = mesh.shape["ax"], mesh.shape["circ"]
    rows, flat = NA // parts, NC // peers * R
    return (
        parts & (parts - 1) == 0
        and peers & (peers - 1) == 0
        and R == 32
        and R % peers == 0
        and peers * (R // peers) * 8 == 8 * R
        and rows % LANES == 0
        and (NC // parts) % LANES == 0
        and flat % (2 * LANES) == 0
        and (NC // peers) % 16 == 0
        and (rows // peers) % 16 == 0
    )


def solution(mesh):
    return jax.shard_map(
        body if tiled(mesh) else plain_body,
        mesh=mesh,
        in_specs=(
            P(None, "ax", "circ"),
            P(None, "ax", "circ"),
            P(None, "ax", "circ"),
            P("ax", "circ"),
            P(),
            P(),
            P(),
            P(),
            P(),
            P(),
        ),
        out_specs=P(None, ("ax", "circ"), None),
        check_vma=False,
    )
```

```python
import math

import functools

import jax
import jax.numpy as jnp
import ml_dtypes
import numpy as np
from jax import lax
from jax.experimental import pallas as pl
from jax.experimental.pallas import tpu as pltpu
from jax.sharding import PartitionSpec as P

NA = 512
NC = 512
R = 32


def with_halo(block, sides, width, periodic):
    for axis, dim in sides:
        count = lax.axis_size(axis)
        forward = [(i, i + 1) for i in range(count - 1)]
        if periodic:
            forward.append((count - 1, 0))
        backward = [(target, source) for source, target in forward]
        low = lax.ppermute(
            lax.slice_in_dim(block, block.shape[dim] - width, None, axis=dim), axis, forward
        )
        high = lax.ppermute(lax.slice_in_dim(block, 0, width, axis=dim), axis, backward)
        block = jnp.concatenate([low, block, high], axis=dim)
    return block


def cycle_table(count):
    col = jnp.arange(count, dtype=jnp.int32)[:, None]
    mode = jnp.arange(count, dtype=jnp.int32)[None, :]
    half = count // 2
    folded = jnp.where(mode <= half, mode, mode - half)
    shift = jnp.where(mode <= half, 0.0, 0.5 * math.pi).astype(jnp.float32)
    scale_ends = jnp.where(
        (mode == 0) | (mode == half), math.sqrt(1.0 / count), math.sqrt(2.0 / count)
    ).astype(jnp.float32)
    phase = (col * folded % count).astype(jnp.float32) * (2.0 * math.pi / count)
    return jnp.cos(phase - shift) * scale_ends


def axial_table(rows, count):
    first = (rows + 1)[:, None]
    mode = jnp.arange(count, dtype=jnp.int32)[None, :] + 1
    phase = (first * mode % (2 * (count + 1))).astype(jnp.float32) * (math.pi / (count + 1))
    return jnp.sin(phase) * math.sqrt(2.0 / (count + 1))


def extend(field):
    rows = with_halo(field, (("ax", 1),), 1, False)
    return with_halo(rows, (("circ", 2),), R, True)


def cycle_parts(ext):
    span = ext.shape[2] - 2 * R
    left = ext[:, :, :span]
    middle = ext[:, :, R : R + span]
    right = ext[:, :, 2 * R :]
    return ((left + 4.0 * middle + right) / 6.0, (right - left) * 0.5)


def row_smooth(field):
    return (field[:, :-2] + 4.0 * field[:, 1:-1] + field[:, 2:]) / 6.0


def row_slope(field):
    return (field[:, 2:] - field[:, :-2]) * 0.5


def radial_mix(field, matrix, form):
    count, rows, flat = field.shape
    cube = field.reshape(count, rows, flat // R, R)
    mixed = jnp.einsum(form, cube, matrix, precision=lax.Precision.HIGHEST)
    return mixed.reshape(count, rows, flat)


def into_cycles(field):
    return lax.all_to_all(field, "circ", split_axis=1, concat_axis=2, tiled=True)


def cycle_forward(field, table, basis):
    count, rows, flat = field.shape
    cube = field.reshape(count * rows, NC, R)
    cube = jnp.einsum("bcr,ck->bkr", cube, table, precision=lax.Precision.HIGHEST)
    cube = jnp.einsum("bkr,rm->bkm", cube, basis, precision=lax.Precision.HIGHEST)
    return cube.reshape(count, rows, flat)


def cycle_inverse(field, table, basis):
    count, rows, flat = field.shape
    cube = field.reshape(count * rows, NC, R)
    cube = jnp.einsum("bkm,rm->bkr", cube, basis, precision=lax.Precision.HIGHEST)
    cube = jnp.einsum("bkr,ck->bcr", cube, table, precision=lax.Precision.HIGHEST)
    return cube.reshape(count, rows, flat)


def axial_solve(lines, forward_table, inverse_table, weights):
    modes = jnp.einsum("pk,cps->cks", forward_table, lines, precision=lax.Precision.HIGHEST)
    return jnp.einsum(
        "ak,cks->cas", inverse_table, modes * weights[None], precision=lax.Precision.HIGHEST
    )


def plain_body(
    displace,
    load,
    history,
    stiffen,
    modulus,
    radial_slope,
    radial_basis,
    axial_eig,
    cycle_eig,
    radial_eig,
):
    ext = extend(displace)
    cycle_v, cycle_d = cycle_parts(ext)
    smooth_v = row_smooth(cycle_v)
    radial_part = radial_mix(smooth_v, radial_slope, "iacq,rq->iacr")
    grads = jnp.concatenate([row_slope(cycle_v), row_smooth(cycle_d), radial_part], axis=0)
    mixed = jnp.einsum("mn,nac->mac", modulus, grads, precision=lax.Precision.HIGHEST)
    stress = (1.0 + stiffen)[None] * mixed + history
    ext_stress = extend(stress)
    first_v, unused_d = cycle_parts(ext_stress[0:3])
    unused_v, second_d = cycle_parts(ext_stress[3:6])
    third_v, unused_e = cycle_parts(ext_stress[6:9])
    third = radial_mix(row_smooth(third_v), radial_slope, "iacr,rq->iacq")
    pull = -row_slope(first_v) - row_smooth(second_d) + third
    resid = load - pull
    a_dev = displace.shape[1]
    flat_dev = displace.shape[2]
    n_ax = lax.axis_size("ax")
    n_circ = lax.axis_size("circ")
    piece = flat_dev // n_ax
    rows_cycle = a_dev // n_circ
    table_cycle = cycle_table(NC)
    spec = cycle_forward(into_cycles(resid), table_cycle, radial_basis)
    start = lax.axis_index("circ") * flat_dev + lax.axis_index("ax") * piece
    index_flat = start + jnp.arange(piece, dtype=jnp.int32)
    denom = (
        axial_eig[:, None]
        + jnp.take(cycle_eig, index_flat // R)[None, :]
        + jnp.take(radial_eig, index_flat % R)[None, :]
    )
    weights = 1.0 / denom
    natural_rows = jnp.arange(NA, dtype=jnp.int32)
    inverse_table = axial_table(natural_rows, NA)
    cube = spec.reshape(3, rows_cycle, n_circ, flat_dev)
    lines = lax.all_to_all(
        lax.all_to_all(cube, "ax", split_axis=3, concat_axis=1, tiled=True),
        "circ",
        split_axis=2,
        concat_axis=1,
        tiled=True,
    ).reshape(3, NA, piece)
    group = n_ax * rows_cycle
    outer = natural_rows // group
    inner = natural_rows % group
    source_rows = inner // rows_cycle * a_dev + outer * rows_cycle + inner % rows_cycle
    forward_table = axial_table(source_rows, NA)
    solved = axial_solve(lines, forward_table, inverse_table, weights)
    cycles_back = lax.all_to_all(
        lax.all_to_all(solved, "ax", split_axis=1, concat_axis=2, tiled=True),
        "circ",
        split_axis=1,
        concat_axis=2,
        tiled=True,
    )
    return cycle_inverse(cycles_back, table_cycle, radial_basis)


BF = jnp.bfloat16
F32 = jnp.float32
VMEM = pl.BlockSpec(memory_space=pltpu.VMEM)
SMEM = pl.BlockSpec(memory_space=pltpu.SMEM)
HBM = pl.BlockSpec(memory_space=pltpu.HBM)
HALO = 8
PAD = 8
HALF = 64
LANES = 128


def params(mebibytes=60):
    return pltpu.CompilerParams(vmem_limit_bytes=mebibytes << 20)


def cost(microseconds):
    return pl.CostEstimate(flops=1, bytes_accessed=int(microseconds * 3.6e6) + 1, transcendentals=0)


def split(x):
    hi = x.astype(BF)
    return hi, (x - hi.astype(F32)).astype(BF)


def dot(a, b, transposed=False):
    dims = (((1,), (1 if transposed else 0,)), ((), ()))
    return lax.dot_general(a, b, dims, preferred_element_type=F32)


def dot3(ah, al, bh, bl, transposed=False):
    return dot(ah, bh, transposed) + (dot(ah, bl, transposed) + dot(al, bh, transposed))


def stacked3(both, bh, bl, transposed=False):
    rows = both.shape[0] // 2
    upper = dot(both[...], bh, transposed)
    return upper[:rows] + (upper[rows:] + dot(both[0:rows, :], bl, transposed))


def exact(a, b, transposed=False):
    dims = (((1,), (1 if transposed else 0,)), ((), ()))
    return lax.dot_general(
        a, b, dims, precision=lax.Precision.HIGHEST, preferred_element_type=F32
    )


def host_split(table):
    hi = table.astype(np.float32).astype(ml_dtypes.bfloat16)
    lo = (table - hi.astype(np.float64)).astype(np.float32).astype(ml_dtypes.bfloat16)
    return jnp.asarray(np.concatenate([hi, lo], axis=0))


def host_cycle(count):
    col = np.arange(count)[None, :]
    mode = np.arange(count)[:, None]
    half = count // 2
    folded = np.where(mode <= half, mode, mode - half)
    phase = 2.0 * np.pi * ((col * folded) % count) / count
    scale = np.where((mode == 0) | (mode == half), math.sqrt(1.0 / count), math.sqrt(2.0 / count))
    return np.where(mode <= half, np.cos(phase), np.sin(phase)) * scale


def host_axial(count):
    first = np.arange(1, count + 1)
    phase = np.pi * (np.outer(first, first) % (2 * (count + 1))) / (count + 1)
    return np.sin(phase) * math.sqrt(2.0 / (count + 1))


def host_weave(mp):
    table = np.zeros((mp * LANES, mp * LANES), np.float32)
    for m in range(mp):
        for c in range(LANES):
            table[m * LANES + c, c * mp + m] = 1.0
    return jnp.asarray(table.astype(ml_dtypes.bfloat16))


def iota(shape, dim):
    return lax.broadcasted_iota(jnp.int32, shape, dim)


def onehot(condition):
    return jnp.where(condition, 1.0, 0.0).astype(F32)


def write_split(hi_ref, lo_ref, value):
    hi, lo = split(value)
    hi_ref[...] = hi
    lo_ref[...] = lo


def fetch(sources, targets, sems):
    copies = [
        pltpu.make_async_copy(source, target, sems.at[k])
        for k, (source, target) in enumerate(zip(sources, targets, strict=True))
    ]
    for copy in copies:
        copy.start()
    return copies


def write_stack(ref, value):
    rows = value.shape[0]
    hi, lo = split(value)
    ref[0:rows, :] = hi
    ref[rows:, :] = lo


def fetch(sources, targets, sems):
    copies = [
        pltpu.make_async_copy(source, target, sems.at[k])
        for k, (source, target) in enumerate(zip(sources, targets, strict=True))
    ]
    for copy in copies:
        copy.start()
    return copies


def front_tables_kernel(mp, slope_ref, basis_ref, *refs):
    outs, made, sems = refs[:6], refs[6:12], refs[12]
    krh, krl, kbh, kbl, kwh, kwl = made
    slope = slope_ref[...]
    basis = basis_ref[...]
    side = LANES
    row = iota((side, R), 0)
    col = iota((side, R), 1)
    pick = onehot(row % R == col)
    mask = iota((side, side), 0) // R == iota((side, side), 1) // R
    value = exact(exact(pick, slope, True), pick, True)
    write_split(krh, krl, jnp.where(mask, value * (1.0 / 36.0), 0.0))
    side = 8 * R
    row = iota((side, R), 0)
    col = iota((side, R), 1)
    pick = onehot(row % R == col)
    block = mp * 8
    mode = onehot(row // block * mp + (row % block) // 8 == col)
    mask = iota((side, side), 0) % 8 == iota((side, side), 1) // R
    value = exact(exact(mode, basis, True), pick, True)
    write_split(kbh, kbl, jnp.where(mask, value, 0.0))
    both = exact(slope, basis)
    value = exact(exact(mode, both, True), pick, True)
    write_split(kwh, kwl, jnp.where(mask, value * (-1.0 / 36.0), 0.0))
    for copy in fetch(made, outs, sems):
        copy.wait()


def front_tables(slope, basis, mp):
    one = jax.ShapeDtypeStruct((LANES, LANES), BF)
    two = jax.ShapeDtypeStruct((8 * R, 8 * R), BF)
    return pl.pallas_call(
        functools.partial(front_tables_kernel, mp),
        out_shape=(one, one, two, two, two, two),
        in_specs=[VMEM, VMEM],
        out_specs=(HBM,) * 6,
        scratch_shapes=[pltpu.VMEM(x.shape, BF) for x in (one, one, two, two, two, two)]
        + [pltpu.SemaphoreType.DMA((6,))],
        compiler_params=params(),
        name="front_tables",
    )(slope, basis)


def back_tables_kernel(mp, basis_ref, after, out, made, sem):
    del after
    rows, cols = made.shape[0] // 2, made.shape[1]
    row = iota((rows, R), 0)
    col = iota((rows, R), 1)
    mode = onehot(row // HALF * mp + row % mp == col)
    pick = onehot(iota((cols, R), 0) % R == iota((cols, R), 1))
    value = exact(exact(mode, basis_ref[...], True), pick, True)
    mask = (iota((rows, cols), 0) % HALF) // mp == iota((rows, cols), 1) // R
    write_stack(made, jnp.where(mask, value, 0.0))
    copy = pltpu.make_async_copy(made, out, sem)
    copy.start()
    copy.wait()


def back_tables(basis, mp, peers, after):
    shape = jax.ShapeDtypeStruct((2 * peers * HALF, HALF // mp * R), BF)
    return pl.pallas_call(
        functools.partial(back_tables_kernel, mp),
        out_shape=shape,
        in_specs=[VMEM, HBM],
        out_specs=HBM,
        scratch_shapes=[pltpu.VMEM(shape.shape, BF), pltpu.SemaphoreType.DMA],
        compiler_params=params(24),
        name="back_tables",
    )(basis, after)


def pack_columns(out, lane, wide, slim, pieces):
    for tile in range(4):
        value = None
        for index, piece in enumerate(pieces):
            at = 64 * index if index < 3 else 96 + 32 * index
            if at // LANES == tile:
                shift = (at - (wide if index < 3 else slim)) % LANES
                moved = pltpu.roll(piece, shift, 1) if shift else piece
                value = moved if value is None else jnp.where(lane >= at % LANES, moved, value)
        out[:, tile * LANES : (tile + 1) * LANES] = value


def pack_kernel(
    displace, history, stiffen, up_ref, down_ref, left_ref, right_ref, d, h, s, dc, hc, sc, sems
):
    rows, flat = stiffen.shape
    sources, targets = [], []
    for k, at in enumerate((slice(0, 8), slice(rows - 8, rows))):
        sources += [displace.at[:, at, :], history.at[:, at, :], stiffen.at[at, :]]
        targets += [d.at[k], h.at[k], s.at[k]]
    for k, at in enumerate((slice(0, LANES), slice(flat - LANES, flat))):
        sources += [displace.at[:, :, at], history.at[:, :, at], stiffen.at[:, at]]
        targets += [dc.at[k], hc.at[k], sc.at[k]]
    copies = fetch(sources, targets, sems)
    for copy in copies[:6]:
        copy.wait()
    for k, first, last, out in ((0, 0, 0, up_ref), (1, 6, 7, down_ref)):
        for i in range(3):
            out[2 * i : 2 * i + 2, :] = d[k, i, first : first + 2, :]
        for n in range(9):
            out[6 + n : 7 + n, :] = h[k, n, last : last + 1, :]
        out[15:16, :] = 1.0 + s[k, last : last + 1, :]
    for copy in copies[6:]:
        copy.wait()
    lane = iota((rows, LANES), 1)
    for k, out, wide, slim in ((0, left_ref, 0, 0), (1, right_ref, LANES - 2 * R, LANES - R)):
        pieces = [dc[k, i] for i in range(3)] + [hc[k, n] for n in range(9)] + [1.0 + sc[k]]
        pack_columns(out, lane, wide, slim, pieces)


def pack(displace, history, stiffen):
    rows, flat = stiffen.shape
    row = jax.ShapeDtypeStruct((16, flat), F32)
    column = jax.ShapeDtypeStruct((rows, 4 * LANES), F32)
    return pl.pallas_call(
        pack_kernel,
        out_shape=(row, row, column, column),
        in_specs=[HBM] * 3,
        out_specs=(VMEM,) * 4,
        scratch_shapes=[
            pltpu.VMEM((2, 3, 8, flat), F32),
            pltpu.VMEM((2, 9, 8, flat), F32),
            pltpu.VMEM((2, 8, flat), F32),
            pltpu.VMEM((2, 3, rows, LANES), F32),
            pltpu.VMEM((2, 9, rows, LANES), F32),
            pltpu.VMEM((2, rows, LANES), F32),
            pltpu.SemaphoreType.DMA((12,)),
        ],
        compiler_params=params(60),
        cost_estimate=cost(0),
        name="pack",
    )(displace, history, stiffen)


def corners_kernel(top, bottom, after, left_ref, right_ref, tall):
    del after
    flat = top.shape[1]
    lane = iota((HALO, LANES), 1)
    tall[...] = jnp.zeros_like(tall)
    for out, at, wide, slim in (
        (left_ref, slice(0, LANES), 0, 0),
        (right_ref, slice(flat - LANES, flat), LANES - 2 * R, LANES - R),
    ):
        pieces = []
        for index in range(13):
            first, count = (2 * index, 2) if index < 3 else (3 + index, 1)
            tall[index, 0:count, :] = bottom[first : first + count, at]
            tall[index, HALO - count : HALO, :] = top[first : first + count, at]
            pieces.append(tall[index])
        pack_columns(out, lane, wide, slim, pieces)


def corners(top, bottom, after):
    shape = jax.ShapeDtypeStruct((HALO, 4 * LANES), F32)
    return pl.pallas_call(
        corners_kernel,
        out_shape=(shape, shape),
        in_specs=[VMEM] * 2 + [HBM],
        out_specs=(VMEM, VMEM),
        scratch_shapes=[pltpu.VMEM((13, HALO, LANES), F32)],
        compiler_params=params(),
        cost_estimate=cost(0),
        name="corners",
    )(top, bottom, after)


def stencil_kernel(
    comps,
    mp,
    peers,
    modulus,
    displace,
    load,
    history,
    stiffen,
    top,
    bottom,
    left,
    left_corner,
    right,
    right_corner,
    *rest,
):
    n = len(comps)
    out, xd, hx, sx, ld, st, sums, diffs, made, krh, krl, kbh, kbl, kwh, kwl, sems = rest[7:]
    rows, flat = stiffen.shape
    tall = rows + HALO
    tiles = flat // LANES
    entries = [comp + 3 * k for comp in comps for k in range(3)]
    center = (slice(0, rows), slice(0, flat))

    def displace_copy(i, t):
        return pltpu.make_async_copy(
            displace.at[i, :, t * LANES : (t + 1) * LANES],
            xd.at[i, t, PAD : PAD + rows, :],
            sems.at[i * tiles + t],
        )

    moves = [displace_copy(i, t) for t in range(tiles) for i in range(3)]
    base = 3 * tiles
    late = [pltpu.make_async_copy(stiffen, sx.at[center], sems.at[base])]
    late += [
        pltpu.make_async_copy(history.at[m], hx.at[(k,) + center], sems.at[base + 1 + k])
        for k, m in enumerate(entries)
    ]
    final = [
        pltpu.make_async_copy(load.at[comp], ld.at[k], sems.at[base + 1 + 3 * n + k])
        for k, comp in enumerate(comps)
    ]
    tables = [
        pltpu.make_async_copy(source, target, sems.at[base + 1 + 5 * n + k])
        for k, (source, target) in enumerate(
            zip(rest[:6], (krh, krl, kbh, kbl, kwh, kwl), strict=True)
        )
    ]
    late += tables[:2]
    final += tables[2:]
    for copy in moves + late + final:
        copy.start()
    left = (left, left_corner)
    right = (right, right_corner)
    lane = iota((tall, LANES), 1)
    short = iota((rows, LANES), 1)

    def tile_of(refs, at, target):
        part = slice(at // LANES * LANES, (at // LANES + 1) * LANES)
        value = jnp.concatenate([ref[:, part] for ref in refs], axis=0)
        shift = (target - at) % LANES
        return pltpu.roll(value, shift, 1) if shift else value

    for i in range(3):
        tile = jnp.where(lane < 64, tile_of(right, 64 * i, 0), tile_of(left, 64 * i, 64))
        xd[i, tiles, PAD : PAD + tall, :] = tile
        xd[i, tiles, PAD - 1 : PAD, :] = tile[tall - 1 : tall]
        xd[i, tiles, PAD + tall : PAD + tall + 1, :] = tile[0:1]
        for t in range(tiles):
            part = slice(t * LANES, (t + 1) * LANES)
            above = top[2 * i : 2 * i + 2, part]
            xd[i, t, PAD + rows : PAD + rows + 2, :] = bottom[2 * i : 2 * i + 2, part]
            xd[i, t, PAD + tall - 2 : PAD + tall, :] = above
            xd[i, t, PAD - 1 : PAD, :] = above[1:2]
    zeros = jnp.zeros((HALO, flat), F32)
    for k, m in enumerate(entries):
        at = 192 + 32 * m
        hx[k, rows:tall, 0:flat] = zeros
        hx[k, rows : rows + 1, 0:flat] = bottom[6 + m : 7 + m, :]
        hx[k, tall - 1 : tall, 0:flat] = top[6 + m : 7 + m, :]
        hx[k, :, flat:] = jnp.where(lane < 64, tile_of(right, at, 0), tile_of(left, at, 96))
    sx[rows:tall, 0:flat] = zeros
    sx[rows : rows + 1, 0:flat] = bottom[15:16, :] - 1.0
    sx[tall - 1 : tall, 0:flat] = top[15:16, :] - 1.0
    sx[:, flat:] = jnp.where(lane < 64, tile_of(right, 480, 0), tile_of(left, 480, 96)) - 1.0

    def lanes(t):
        return pl.ds(pl.multiple_of(t * LANES, LANES), LANES)

    def previous(t):
        return lax.rem(t + tiles, tiles + 1)

    def following(t):
        return lax.rem(t + 1, tiles + 1)

    def lower(ref, k, t, height, mask):
        mixed = jnp.where(
            mask >= LANES - R, ref[k, previous(t), 0:height, :], ref[k, t, 0:height, :]
        )
        return pltpu.roll(mixed, R, 1)

    def higher(ref, k, t, height, mask):
        mixed = jnp.where(mask < R, ref[k, following(t), 0:height, :], ref[k, t, 0:height, :])
        return pltpu.roll(mixed, LANES - R, 1)

    for copy in moves:
        copy.wait()

    def rows_step(t, carry):
        for i in range(3):
            xd[i, t, PAD + tall : PAD + tall + 1, :] = xd[i, t, PAD : PAD + 1, :]
            above = xd[i, t, PAD - 1 : PAD - 1 + tall, :]
            below = xd[i, t, PAD + 1 : PAD + 1 + tall, :]
            total = above + 4.0 * xd[i, t, PAD : PAD + tall, :] + below
            change = below - above
            sums[i, t] = total
            diffs[i, t] = change
        return carry

    lax.fori_loop(0, tiles + 1, rows_step, 0, unroll=True)
    for copy in late:
        copy.wait()

    def stress_step(t, carry):
        total = [None] * len(entries)
        for i in range(3):
            low = lower(sums, i, t, tall, lane)
            high = higher(sums, i, t, tall, lane)
            second = high - low
            both = low + high + 4.0 * sums[i, t]
            low = lower(diffs, i, t, tall, lane)
            high = higher(diffs, i, t, tall, lane)
            first = low + high + 4.0 * diffs[i, t]
            bh, bl = split(both)
            third = dot3(bh, bl, krh[...], krl[...])
            for k, m in enumerate(entries):
                part = (
                    (modulus[m, i] * (1.0 / 12.0)) * first
                    + (modulus[m, 3 + i] * (1.0 / 12.0)) * second
                    + modulus[m, 6 + i] * third
                )
                total[k] = part if total[k] is None else total[k] + part
        factor = 1.0 + sx[:, lanes(t)]
        for k in range(len(entries)):
            value = factor * total[k] + hx[k, :, lanes(t)]
            st[k, t, PAD : PAD + tall, :] = value
            st[k, t, PAD - 1 : PAD, :] = value[tall - 1 : tall]
        return carry

    lax.fori_loop(0, tiles + 1, stress_step, 0, unroll=True)
    for copy in final:
        copy.wait()

    sent = []
    for index in range(n):
        first_entry = 3 * index
        message = made.at[index]

        def pull_rows(t, carry):
            def around(k):
                field = first_entry + k
                return (
                    st[field, t, PAD - 1 : PAD - 1 + rows, :],
                    st[field, t, PAD : PAD + rows, :],
                    st[field, t, PAD + 1 : PAD + 1 + rows, :],
                )

            above, _, below = around(0)
            p = below - above
            above, now, below = around(1)
            q = above + 4.0 * now + below
            above, now, below = around(2)
            w = above + 4.0 * now + below
            sums[0, t, 0:rows, :] = p - q
            sums[1, t, 0:rows, :] = p + q
            sums[2, t, 0:rows, :] = w
            return carry

        lax.fori_loop(0, tiles + 1, pull_rows, 0, unroll=True)

        def message_step(s, carry):
            us, ws = [], []
            for half in range(2):
                t = 2 * s + half
                pull = 2.0 * (sums[0, t, 0:rows, :] + sums[1, t, 0:rows, :])
                pull = pull + lower(sums, 0, t, rows, short) + higher(sums, 1, t, rows, short)
                us.append(ld[index, :, lanes(t)] + pull * (1.0 / 12.0))
                w = 4.0 * sums[2, t, 0:rows, :]
                ws.append(w + lower(sums, 2, t, rows, short) + higher(sums, 2, t, rows, short))
            uh, ul = split(jnp.concatenate(us, axis=1))
            wh, wl = split(jnp.concatenate(ws, axis=1))
            value = dot3(kbh[...], kbl[...], uh, ul, True)
            value = value + dot3(kwh[...], kwl[...], wh, wl, True)
            here = pl.ds(pl.multiple_of(s * 8, 8), 8)
            for peer in range(peers):
                for m in range(mp):
                    row = (peer * mp + m) * 8
                    message[peer, here, m * rows : (m + 1) * rows] = value[row : row + 8, :]
            return carry

        lax.fori_loop(0, tiles // 2, message_step, 0, unroll=True)
        sent += [pltpu.make_async_copy(message, out.at[:, index], sems.at[base + 1 + 4 * n + index])]
        sent[-1].start()
    for copy in sent:
        copy.wait()


def stencil(comps, mp, peers, modulus, displace, load, history, stiffen, halos, tables, after):
    rows, flat = stiffen.shape
    tall = rows + HALO
    wide = flat + LANES
    tiles = flat // LANES
    n = len(comps)
    block = (flat // R, mp * rows)
    return pl.pallas_call(
        functools.partial(stencil_kernel, comps, mp, peers),
        out_shape=jax.ShapeDtypeStruct((peers, n) + block, F32),
        in_specs=[SMEM] + [HBM] * 4 + [VMEM] * 6 + [HBM] * 7,
        out_specs=HBM,
        scratch_shapes=[
            pltpu.VMEM((3, tiles + 1, PAD + tall + HALO, LANES), F32),
            pltpu.VMEM((3 * n, tall, wide), F32),
            pltpu.VMEM((tall, wide), F32),
            pltpu.VMEM((n, rows, flat), F32),
            pltpu.VMEM((3 * n, tiles + 1, PAD + tall, LANES), F32),
            pltpu.VMEM((3, tiles + 1, tall, LANES), F32),
            pltpu.VMEM((3, tiles + 1, tall, LANES), F32),
            pltpu.VMEM((n, peers) + block, F32),
            *(pltpu.VMEM(table.shape, BF) for table in tables),
            pltpu.SemaphoreType.DMA((3 * tiles + 7 + 5 * n,)),
        ],
        compiler_params=params(),
        cost_estimate=cost(13 + 8 * n),
        name="stencil",
    )(modulus, displace, load, history, stiffen, *halos, *tables, after)


def cycle_kernel(index, parts, ids, piece, table_ref, after, *refs):
    del after
    outs = refs[:parts]
    xh, xl, raw, table, made, sems = refs[parts:]
    peers, _, height, _ = piece.shape
    copies = fetch(
        [piece.at[j, index] for j in range(peers)] + [table_ref],
        [raw.at[j] for j in range(peers)] + [table],
        sems,
    )
    for j in range(peers):
        copies[j].wait()
        at = slice(j * height, (j + 1) * height)
        hi, lo = split(raw[j])
        xh[at, :] = hi
        xl[at, :] = lo
    copies[peers].wait()
    value = stacked3(table, xh[...], xl[...])
    block = outs[0].shape[0]
    for b in range(parts):
        made[jnp.bitwise_xor(ids[1], b)] = value[b * block : (b + 1) * block]
    sent = fetch([made.at[d] for d in range(parts)], outs, sems.at[pl.ds(peers + 1, parts)])
    for copy in sent:
        copy.wait()


def cycle_stage(index, ids, piece, table, parts, after):
    peers, _, height, width = piece.shape
    count = peers * height
    shape = jax.ShapeDtypeStruct((count // parts, width), F32)
    return pl.pallas_call(
        functools.partial(cycle_kernel, index, parts),
        out_shape=(shape,) * parts,
        in_specs=[SMEM] + [HBM] * 3,
        out_specs=(HBM,) * parts,
        scratch_shapes=[
            pltpu.VMEM((count, width), BF),
            pltpu.VMEM((count, width), BF),
            pltpu.VMEM((peers, height, width), F32),
            pltpu.VMEM(table.shape, BF),
            pltpu.VMEM((parts,) + shape.shape, F32),
            pltpu.SemaphoreType.DMA((peers + 1 + parts,)),
        ],
        compiler_params=params(24),
        cost_estimate=cost(0),
        name="cycle_stage",
    )(ids, piece, table, after)


def axial_kernel(mp, parts, ids, radial, cyc, axial, *refs):
    ins = refs[:parts]
    table_ref, after, out, x, xh, xl, raw, table, made, sems = refs[parts:]
    del after
    kc, width = ins[0].shape
    rows = width // mp
    half = mp * kc
    count = parts * rows
    copies = fetch([*ins, table_ref], [raw.at[j] for j in range(parts)] + [table], sems)
    for j in range(parts):
        source = jnp.bitwise_xor(ids[1], j)
        at = pl.ds(pl.multiple_of(source * rows, rows), rows)
        copies[j].wait()
        for m in range(mp):
            hi, lo = split(raw[j, :, m * rows : (m + 1) * rows])
            x[m * kc : (m + 1) * kc, at] = hi
            x[half + m * kc : half + (m + 1) * kc, at] = lo
    copies[parts].wait()
    mine = cyc[pl.ds(pl.multiple_of(ids[1] * kc, kc), kc), :]
    base = axial[...] + mine
    value = stacked3(x, table[0:count, :], table[count:, :])
    for m in range(mp):
        part = slice(m * kc, (m + 1) * kc)
        hi, lo = split(value[part] / (base + radial[ids[0] * mp + m]))
        xh[part, :] = hi
        xl[part, :] = lo
    made[...] = stacked3(table, xh[...], xl[...], True)
    copy = pltpu.make_async_copy(made, out, sems.at[parts + 1])
    copy.start()
    copy.wait()


def axial_stage(ids, radial, cyc, axial, pieces, table, mp, after):
    parts = len(pieces)
    kc, width = pieces[0].shape
    count = width // mp * parts
    return pl.pallas_call(
        functools.partial(axial_kernel, mp, parts),
        out_shape=jax.ShapeDtypeStruct((count, mp * kc), F32),
        in_specs=[SMEM, SMEM, VMEM, VMEM] + [HBM] * (parts + 2),
        out_specs=HBM,
        scratch_shapes=[
            pltpu.VMEM((2 * mp * kc, count), BF),
            pltpu.VMEM((mp * kc, count), BF),
            pltpu.VMEM((mp * kc, count), BF),
            pltpu.VMEM((parts, kc, width), F32),
            pltpu.VMEM(table.shape, BF),
            pltpu.VMEM((count, mp * kc), F32),
            pltpu.SemaphoreType.DMA((parts + 2,)),
        ],
        compiler_params=params(24),
        cost_estimate=cost(0),
        name="axial_stage",
    )(ids, radial, cyc, axial, *pieces, table, after)


def return_kernel(comp, mp, parts, peers, piece, *refs):
    out, x, y, raw, table, weave, kernel, made, sems = refs[-9:]
    _, few, width = piece.shape
    kc = width // mp
    count = table.shape[1]
    depth, span = kernel.shape[0] // 2, kernel.shape[1]
    half = mp * peers * few
    groups = count * mp // HALF
    copies = fetch((piece, *refs[:3]), (raw, table, weave, kernel), sems)
    copies[0].wait()
    for p in range(parts):
        for q in range(peers):
            for m in range(mp):
                row = (m * peers + q) * few
                hi, lo = split(raw[p * peers + q, :, m * kc : (m + 1) * kc])
                x[row : row + few, p * kc : (p + 1) * kc] = hi
                x[half + row : half + row + few, p * kc : (p + 1) * kc] = lo
    for copy in copies[1:]:
        copy.wait()
    value = split(stacked3(x, table[0:count, :], table[count:, :]))
    rows = peers * few
    front = iota((few, LANES), 1) < HALF
    for t in range(count // LANES):
        columns = slice(t * LANES, (t + 1) * LANES)
        for part, first in zip(value, (0, groups * few), strict=True):
            gathered = jnp.concatenate(
                [part[m * rows : (m + 1) * rows, columns] for m in range(mp)], axis=1
            )
            woven = dot(gathered, weave[...])
            for g in range(mp):
                block = woven[:, g * LANES : (g + 1) * LANES]
                turned = pltpu.roll(block, HALF, 1)
                row = first + 2 * (t * mp + g) * few
                for q in range(0, peers, 2):
                    one = slice(q * few, (q + 1) * few)
                    two = slice((q + 1) * few, (q + 2) * few)
                    to = slice(q * HALF, q * HALF + LANES)
                    y[row : row + few, to] = jnp.where(front, block[one], turned[two]).astype(BF)
                    y[row + few : row + 2 * few, to] = jnp.where(
                        front, turned[one], block[two]
                    ).astype(BF)
    result = stacked3(y, kernel[0:depth, :], kernel[depth:, :])
    for g in range(groups):
        made[:, g * span : (g + 1) * span] = result[g * few : (g + 1) * few, :]
    copy = pltpu.make_async_copy(made, out.at[comp], sems.at[4])
    copy.start()
    copy.wait()


def return_stage(comp, piece, table, weave, back, mp, parts, carried):
    devices, few, width = piece.shape
    peers = devices // parts
    count = table.shape[1]
    depth, span = back.shape[0] // 2, back.shape[1]
    groups = count * mp // HALF
    extra = [] if carried is None else [carried]
    return pl.pallas_call(
        functools.partial(return_kernel, comp, mp, parts, peers),
        out_shape=jax.ShapeDtypeStruct((3, few, groups * span), F32),
        in_specs=[HBM] * (4 + len(extra)),
        out_specs=HBM,
        scratch_shapes=[
            pltpu.VMEM((2 * mp * peers * few, count), BF),
            pltpu.VMEM((2 * groups * few, depth), BF),
            pltpu.VMEM(piece.shape, F32),
            pltpu.VMEM(table.shape, BF),
            pltpu.VMEM(weave.shape, BF),
            pltpu.VMEM(back.shape, BF),
            pltpu.VMEM((few, groups * span), F32),
            pltpu.SemaphoreType.DMA((5,)),
        ],
        input_output_aliases={4: 0} if extra else {},
        compiler_params=params(32),
        cost_estimate=cost(0),
        name="return_stage",
    )(piece, table, weave, back, *extra)


def across(block, axis):
    return lax.all_to_all(block, axis, split_axis=0, concat_axis=0, tiled=True)


def swap(pieces, axis):
    count = len(pieces)
    return [pieces[0]] + [
        lax.ppermute(pieces[d], axis, [(i, i ^ d) for i in range(count)]) for d in range(1, count)
    ]


ORDER = (
    ("stencil", (0,)),
    ("stencil", (1, 2)),
    ("cycle", 0),
    ("tables", None),
    ("axial", 0),
    ("cycle", 1),
    ("axial", 1),
    ("cycle", 2),
    ("return", 0),
    ("axial", 2),
    ("return", 1),
    ("return", 2),
)


def body(
    displace,
    load,
    history,
    stiffen,
    modulus,
    radial_slope,
    radial_basis,
    axial_eig,
    cycle_eig,
    radial_eig,
):
    parts = lax.axis_size("ax")
    peers = lax.axis_size("circ")
    mp = R // peers
    rows, flat = stiffen.shape
    count_a = parts * rows
    count_c = peers * flat // R
    me = lax.axis_index("circ").astype(jnp.int32)
    pe = lax.axis_index("ax").astype(jnp.int32)
    ids = jnp.stack([me, pe])

    upward, downward, leftward, rightward = pack(displace, history, stiffen)
    ahead = [(i, i + 1) for i in range(parts - 1)]
    back_ahead = [(j, i) for i, j in ahead]
    around = [(i, (i + 1) % peers) for i in range(peers)]
    back_around = [(j, i) for i, j in around]
    bottom = lax.ppermute(upward, "ax", back_ahead)
    top = lax.ppermute(downward, "ax", ahead)
    right = lax.ppermute(leftward, "circ", back_around)
    left = lax.ppermute(rightward, "circ", around)
    front = front_tables(radial_slope, radial_basis, mp)
    to_left, to_right = corners(top, bottom, front[0])
    right_corner = lax.ppermute(to_left, "circ", back_around)
    left_corner = lax.ppermute(to_right, "circ", around)
    halos = (top, bottom, left, left_corner, right, right_corner)

    cycle_table_stack = host_split(host_cycle(count_c))
    axial_table_stack = host_split(host_axial(count_a))
    weave = host_weave(mp)
    cyc = cycle_eig[:, None]
    axial = axial_eig[None, :]

    lines = [None] * 3
    out, after = None, ids
    for kind, i in ORDER:
        if kind == "stencil":
            after = stencil(
                i, mp, peers, modulus, displace, load, history, stiffen, halos, front, after
            )
            block = across(after, "circ")
            for index, comp in enumerate(i):
                lines[comp] = (index, block)
        elif kind == "tables":
            after = back = back_tables(radial_basis, mp, peers, after)
        elif kind == "cycle":
            index, block = lines[i]
            sent = cycle_stage(index, ids, block, cycle_table_stack, parts, after)
            after = sent[0]
            lines[i] = swap(list(sent), "ax")
        elif kind == "axial":
            after = axial_stage(
                ids, radial_eig, cyc, axial, lines[i], axial_table_stack, mp, after
            )
            block = after.reshape(parts * peers, rows // peers, -1)
            lines[i] = across(block, ("ax", "circ"))
        else:
            out = return_stage(i, lines[i], cycle_table_stack, weave, back, mp, parts, out)
            after = out
    return out


def tiled(mesh):
    parts, peers = mesh.shape["ax"], mesh.shape["circ"]
    rows, flat = NA // parts, NC // peers * R
    return (
        parts & (parts - 1) == 0
        and peers & (peers - 1) == 0
        and R == 32
        and R % peers == 0
        and peers * (R // peers) * 8 == 8 * R
        and rows % LANES == 0
        and (NC // parts) % LANES == 0
        and flat % (2 * LANES) == 0
        and (NC // peers) % 16 == 0
        and (rows // peers) % 16 == 0
        and HALF % (R // peers) == 0
        and peers % 2 == 0
    )


def solution(mesh):
    return jax.shard_map(
        body if tiled(mesh) else plain_body,
        mesh=mesh,
        in_specs=(
            P(None, "ax", "circ"),
            P(None, "ax", "circ"),
            P(None, "ax", "circ"),
            P("ax", "circ"),
            P(),
            P(),
            P(),
            P(),
            P(),
            P(),
        ),
        out_specs=P(None, ("ax", "circ"), None),
        check_vma=False,
    )
```

```python
import math

import functools

import jax
import jax.numpy as jnp
import ml_dtypes
import numpy as np
from jax import lax
from jax.experimental import pallas as pl
from jax.experimental.pallas import tpu as pltpu
from jax.sharding import PartitionSpec as P

NA = 512
NC = 512
R = 32


def with_halo(block, sides, width, periodic):
    for axis, dim in sides:
        count = lax.axis_size(axis)
        forward = [(i, i + 1) for i in range(count - 1)]
        if periodic:
            forward.append((count - 1, 0))
        backward = [(target, source) for source, target in forward]
        low = lax.ppermute(
            lax.slice_in_dim(block, block.shape[dim] - width, None, axis=dim), axis, forward
        )
        high = lax.ppermute(lax.slice_in_dim(block, 0, width, axis=dim), axis, backward)
        block = jnp.concatenate([low, block, high], axis=dim)
    return block


def cycle_table(count):
    col = jnp.arange(count, dtype=jnp.int32)[:, None]
    mode = jnp.arange(count, dtype=jnp.int32)[None, :]
    half = count // 2
    folded = jnp.where(mode <= half, mode, mode - half)
    shift = jnp.where(mode <= half, 0.0, 0.5 * math.pi).astype(jnp.float32)
    scale_ends = jnp.where(
        (mode == 0) | (mode == half), math.sqrt(1.0 / count), math.sqrt(2.0 / count)
    ).astype(jnp.float32)
    phase = (col * folded % count).astype(jnp.float32) * (2.0 * math.pi / count)
    return jnp.cos(phase - shift) * scale_ends


def axial_table(rows, count):
    first = (rows + 1)[:, None]
    mode = jnp.arange(count, dtype=jnp.int32)[None, :] + 1
    phase = (first * mode % (2 * (count + 1))).astype(jnp.float32) * (math.pi / (count + 1))
    return jnp.sin(phase) * math.sqrt(2.0 / (count + 1))


def extend(field):
    rows = with_halo(field, (("ax", 1),), 1, False)
    return with_halo(rows, (("circ", 2),), R, True)


def cycle_parts(ext):
    span = ext.shape[2] - 2 * R
    left = ext[:, :, :span]
    middle = ext[:, :, R : R + span]
    right = ext[:, :, 2 * R :]
    return ((left + 4.0 * middle + right) / 6.0, (right - left) * 0.5)


def row_smooth(field):
    return (field[:, :-2] + 4.0 * field[:, 1:-1] + field[:, 2:]) / 6.0


def row_slope(field):
    return (field[:, 2:] - field[:, :-2]) * 0.5


def radial_mix(field, matrix, form):
    count, rows, flat = field.shape
    cube = field.reshape(count, rows, flat // R, R)
    mixed = jnp.einsum(form, cube, matrix, precision=lax.Precision.HIGHEST)
    return mixed.reshape(count, rows, flat)


def into_cycles(field):
    return lax.all_to_all(field, "circ", split_axis=1, concat_axis=2, tiled=True)


def cycle_forward(field, table, basis):
    count, rows, flat = field.shape
    cube = field.reshape(count * rows, NC, R)
    cube = jnp.einsum("bcr,ck->bkr", cube, table, precision=lax.Precision.HIGHEST)
    cube = jnp.einsum("bkr,rm->bkm", cube, basis, precision=lax.Precision.HIGHEST)
    return cube.reshape(count, rows, flat)


def cycle_inverse(field, table, basis):
    count, rows, flat = field.shape
    cube = field.reshape(count * rows, NC, R)
    cube = jnp.einsum("bkm,rm->bkr", cube, basis, precision=lax.Precision.HIGHEST)
    cube = jnp.einsum("bkr,ck->bcr", cube, table, precision=lax.Precision.HIGHEST)
    return cube.reshape(count, rows, flat)


def axial_solve(lines, forward_table, inverse_table, weights):
    modes = jnp.einsum("pk,cps->cks", forward_table, lines, precision=lax.Precision.HIGHEST)
    return jnp.einsum(
        "ak,cks->cas", inverse_table, modes * weights[None], precision=lax.Precision.HIGHEST
    )


def plain_body(
    displace,
    load,
    history,
    stiffen,
    modulus,
    radial_slope,
    radial_basis,
    axial_eig,
    cycle_eig,
    radial_eig,
):
    ext = extend(displace)
    cycle_v, cycle_d = cycle_parts(ext)
    smooth_v = row_smooth(cycle_v)
    radial_part = radial_mix(smooth_v, radial_slope, "iacq,rq->iacr")
    grads = jnp.concatenate([row_slope(cycle_v), row_smooth(cycle_d), radial_part], axis=0)
    mixed = jnp.einsum("mn,nac->mac", modulus, grads, precision=lax.Precision.HIGHEST)
    stress = (1.0 + stiffen)[None] * mixed + history
    ext_stress = extend(stress)
    first_v, unused_d = cycle_parts(ext_stress[0:3])
    unused_v, second_d = cycle_parts(ext_stress[3:6])
    third_v, unused_e = cycle_parts(ext_stress[6:9])
    third = radial_mix(row_smooth(third_v), radial_slope, "iacr,rq->iacq")
    pull = -row_slope(first_v) - row_smooth(second_d) + third
    resid = load - pull
    a_dev = displace.shape[1]
    flat_dev = displace.shape[2]
    n_ax = lax.axis_size("ax")
    n_circ = lax.axis_size("circ")
    piece = flat_dev // n_ax
    rows_cycle = a_dev // n_circ
    table_cycle = cycle_table(NC)
    spec = cycle_forward(into_cycles(resid), table_cycle, radial_basis)
    start = lax.axis_index("circ") * flat_dev + lax.axis_index("ax") * piece
    index_flat = start + jnp.arange(piece, dtype=jnp.int32)
    denom = (
        axial_eig[:, None]
        + jnp.take(cycle_eig, index_flat // R)[None, :]
        + jnp.take(radial_eig, index_flat % R)[None, :]
    )
    weights = 1.0 / denom
    natural_rows = jnp.arange(NA, dtype=jnp.int32)
    inverse_table = axial_table(natural_rows, NA)
    cube = spec.reshape(3, rows_cycle, n_circ, flat_dev)
    lines = lax.all_to_all(
        lax.all_to_all(cube, "ax", split_axis=3, concat_axis=1, tiled=True),
        "circ",
        split_axis=2,
        concat_axis=1,
        tiled=True,
    ).reshape(3, NA, piece)
    group = n_ax * rows_cycle
    outer = natural_rows // group
    inner = natural_rows % group
    source_rows = inner // rows_cycle * a_dev + outer * rows_cycle + inner % rows_cycle
    forward_table = axial_table(source_rows, NA)
    solved = axial_solve(lines, forward_table, inverse_table, weights)
    cycles_back = lax.all_to_all(
        lax.all_to_all(solved, "ax", split_axis=1, concat_axis=2, tiled=True),
        "circ",
        split_axis=1,
        concat_axis=2,
        tiled=True,
    )
    return cycle_inverse(cycles_back, table_cycle, radial_basis)


BF = jnp.bfloat16
F32 = jnp.float32
VMEM = pl.BlockSpec(memory_space=pltpu.VMEM)
SMEM = pl.BlockSpec(memory_space=pltpu.SMEM)
HBM = pl.BlockSpec(memory_space=pltpu.HBM)
HALO = 8
PAD = 8
HALF = 64
LANES = 128


def params(mebibytes=60):
    return pltpu.CompilerParams(vmem_limit_bytes=mebibytes << 20)


def cost(microseconds):
    return pl.CostEstimate(flops=1, bytes_accessed=int(microseconds * 3.6e6) + 1, transcendentals=0)


def split(x):
    hi = x.astype(BF)
    return hi, (x - hi.astype(F32)).astype(BF)


def dot(a, b, transposed=False):
    dims = (((1,), (1 if transposed else 0,)), ((), ()))
    return lax.dot_general(a, b, dims, preferred_element_type=F32)


def dot3(ah, al, bh, bl, transposed=False):
    return dot(ah, bh, transposed) + (dot(ah, bl, transposed) + dot(al, bh, transposed))


def stacked3(both, bh, bl, transposed=False):
    rows = both.shape[0] // 2
    upper = dot(both[...], bh, transposed)
    return upper[:rows] + (upper[rows:] + dot(both[0:rows, :], bl, transposed))


def exact(a, b, transposed=False):
    dims = (((1,), (1 if transposed else 0,)), ((), ()))
    return lax.dot_general(
        a, b, dims, precision=lax.Precision.HIGHEST, preferred_element_type=F32
    )


def host_split(table):
    hi = table.astype(np.float32).astype(ml_dtypes.bfloat16)
    lo = (table - hi.astype(np.float64)).astype(np.float32).astype(ml_dtypes.bfloat16)
    return jnp.asarray(np.concatenate([hi, lo], axis=0))


def host_cycle(count):
    col = np.arange(count)[None, :]
    mode = np.arange(count)[:, None]
    half = count // 2
    folded = np.where(mode <= half, mode, mode - half)
    phase = 2.0 * np.pi * ((col * folded) % count) / count
    scale = np.where((mode == 0) | (mode == half), math.sqrt(1.0 / count), math.sqrt(2.0 / count))
    return np.where(mode <= half, np.cos(phase), np.sin(phase)) * scale


def host_axial(count):
    first = np.arange(1, count + 1)
    phase = np.pi * (np.outer(first, first) % (2 * (count + 1))) / (count + 1)
    return np.sin(phase) * math.sqrt(2.0 / (count + 1))


def host_weave(mp):
    table = np.zeros((mp * LANES, mp * LANES), np.float32)
    for m in range(mp):
        for c in range(LANES):
            table[m * LANES + c, c * mp + m] = 1.0
    return jnp.asarray(table.astype(ml_dtypes.bfloat16))


def iota(shape, dim):
    return lax.broadcasted_iota(jnp.int32, shape, dim)


def onehot(condition):
    return jnp.where(condition, 1.0, 0.0).astype(F32)


def write_split(hi_ref, lo_ref, value):
    hi, lo = split(value)
    hi_ref[...] = hi
    lo_ref[...] = lo


def fetch(sources, targets, sems):
    copies = [
        pltpu.make_async_copy(source, target, sems.at[k])
        for k, (source, target) in enumerate(zip(sources, targets, strict=True))
    ]
    for copy in copies:
        copy.start()
    return copies


def write_stack(ref, value):
    rows = value.shape[0]
    hi, lo = split(value)
    ref[0:rows, :] = hi
    ref[rows:, :] = lo


def fetch(sources, targets, sems):
    copies = [
        pltpu.make_async_copy(source, target, sems.at[k])
        for k, (source, target) in enumerate(zip(sources, targets, strict=True))
    ]
    for copy in copies:
        copy.start()
    return copies


def front_tables_kernel(mp, slope_ref, basis_ref, *refs):
    outs, made, sems = refs[:6], refs[6:12], refs[12]
    krh, krl, kbh, kbl, kwh, kwl = made
    slope = slope_ref[...]
    basis = basis_ref[...]
    side = LANES
    row = iota((side, R), 0)
    col = iota((side, R), 1)
    pick = onehot(row % R == col)
    mask = iota((side, side), 0) // R == iota((side, side), 1) // R
    value = exact(exact(pick, slope, True), pick, True)
    write_split(krh, krl, jnp.where(mask, value * (1.0 / 36.0), 0.0))
    side = 8 * R
    row = iota((side, R), 0)
    col = iota((side, R), 1)
    pick = onehot(row % R == col)
    block = mp * 8
    mode = onehot(row // block * mp + (row % block) // 8 == col)
    mask = iota((side, side), 0) % 8 == iota((side, side), 1) // R
    value = exact(exact(mode, basis, True), pick, True)
    write_split(kbh, kbl, jnp.where(mask, value, 0.0))
    both = exact(slope, basis)
    value = exact(exact(mode, both, True), pick, True)
    write_split(kwh, kwl, jnp.where(mask, value * (-1.0 / 36.0), 0.0))
    for copy in fetch(made, outs, sems):
        copy.wait()


def front_tables(slope, basis, mp):
    one = jax.ShapeDtypeStruct((LANES, LANES), BF)
    two = jax.ShapeDtypeStruct((8 * R, 8 * R), BF)
    return pl.pallas_call(
        functools.partial(front_tables_kernel, mp),
        out_shape=(one, one, two, two, two, two),
        in_specs=[VMEM, VMEM],
        out_specs=(HBM,) * 6,
        scratch_shapes=[pltpu.VMEM(x.shape, BF) for x in (one, one, two, two, two, two)]
        + [pltpu.SemaphoreType.DMA((6,))],
        compiler_params=params(),
        name="front_tables",
    )(slope, basis)


def back_tables_kernel(mp, basis_ref, after, out, made, sem):
    del after
    rows, cols = made.shape[0] // 2, made.shape[1]
    row = iota((rows, R), 0)
    col = iota((rows, R), 1)
    mode = onehot(row // HALF * mp + row % mp == col)
    pick = onehot(iota((cols, R), 0) % R == iota((cols, R), 1))
    value = exact(exact(mode, basis_ref[...], True), pick, True)
    mask = (iota((rows, cols), 0) % HALF) // mp == iota((rows, cols), 1) // R
    write_stack(made, jnp.where(mask, value, 0.0))
    copy = pltpu.make_async_copy(made, out, sem)
    copy.start()
    copy.wait()


def back_tables(basis, mp, peers, after):
    shape = jax.ShapeDtypeStruct((2 * peers * HALF, HALF // mp * R), BF)
    return pl.pallas_call(
        functools.partial(back_tables_kernel, mp),
        out_shape=shape,
        in_specs=[VMEM, HBM],
        out_specs=HBM,
        scratch_shapes=[pltpu.VMEM(shape.shape, BF), pltpu.SemaphoreType.DMA],
        compiler_params=params(24),
        name="back_tables",
    )(basis, after)


def pack_columns(out, lane, wide, slim, pieces):
    for tile in range(4):
        value = None
        for index, piece in enumerate(pieces):
            at = 64 * index if index < 3 else 96 + 32 * index
            if at // LANES == tile:
                shift = (at - (wide if index < 3 else slim)) % LANES
                moved = pltpu.roll(piece, shift, 1) if shift else piece
                value = moved if value is None else jnp.where(lane >= at % LANES, moved, value)
        out[:, tile * LANES : (tile + 1) * LANES] = value


def pack_kernel(
    displace, history, stiffen, up_ref, down_ref, left_ref, right_ref, d, h, s, dc, hc, sc, sems
):
    rows, flat = stiffen.shape
    sources, targets = [], []
    for k, at in enumerate((slice(0, 8), slice(rows - 8, rows))):
        sources += [displace.at[:, at, :], history.at[:, at, :], stiffen.at[at, :]]
        targets += [d.at[k], h.at[k], s.at[k]]
    for k, at in enumerate((slice(0, LANES), slice(flat - LANES, flat))):
        sources += [displace.at[:, :, at], history.at[:, :, at], stiffen.at[:, at]]
        targets += [dc.at[k], hc.at[k], sc.at[k]]
    copies = fetch(sources, targets, sems)
    for copy in copies[:6]:
        copy.wait()
    for k, first, last, out in ((0, 0, 0, up_ref), (1, 6, 7, down_ref)):
        for i in range(3):
            out[2 * i : 2 * i + 2, :] = d[k, i, first : first + 2, :]
        for n in range(9):
            out[6 + n : 7 + n, :] = h[k, n, last : last + 1, :]
        out[15:16, :] = 1.0 + s[k, last : last + 1, :]
    for copy in copies[6:]:
        copy.wait()
    lane = iota((rows, LANES), 1)
    for k, out, wide, slim in ((0, left_ref, 0, 0), (1, right_ref, LANES - 2 * R, LANES - R)):
        pieces = [dc[k, i] for i in range(3)] + [hc[k, n] for n in range(9)] + [1.0 + sc[k]]
        pack_columns(out, lane, wide, slim, pieces)


def pack(displace, history, stiffen):
    rows, flat = stiffen.shape
    row = jax.ShapeDtypeStruct((16, flat), F32)
    column = jax.ShapeDtypeStruct((rows, 4 * LANES), F32)
    return pl.pallas_call(
        pack_kernel,
        out_shape=(row, row, column, column),
        in_specs=[HBM] * 3,
        out_specs=(VMEM,) * 4,
        scratch_shapes=[
            pltpu.VMEM((2, 3, 8, flat), F32),
            pltpu.VMEM((2, 9, 8, flat), F32),
            pltpu.VMEM((2, 8, flat), F32),
            pltpu.VMEM((2, 3, rows, LANES), F32),
            pltpu.VMEM((2, 9, rows, LANES), F32),
            pltpu.VMEM((2, rows, LANES), F32),
            pltpu.SemaphoreType.DMA((12,)),
        ],
        compiler_params=params(60),
        cost_estimate=cost(0),
        name="pack",
    )(displace, history, stiffen)


def corners_kernel(top, bottom, after, left_ref, right_ref, tall):
    del after
    flat = top.shape[1]
    lane = iota((HALO, LANES), 1)
    tall[...] = jnp.zeros_like(tall)
    for out, at, wide, slim in (
        (left_ref, slice(0, LANES), 0, 0),
        (right_ref, slice(flat - LANES, flat), LANES - 2 * R, LANES - R),
    ):
        pieces = []
        for index in range(13):
            first, count = (2 * index, 2) if index < 3 else (3 + index, 1)
            tall[index, 0:count, :] = bottom[first : first + count, at]
            tall[index, HALO - count : HALO, :] = top[first : first + count, at]
            pieces.append(tall[index])
        pack_columns(out, lane, wide, slim, pieces)


def corners(top, bottom, after):
    shape = jax.ShapeDtypeStruct((HALO, 4 * LANES), F32)
    return pl.pallas_call(
        corners_kernel,
        out_shape=(shape, shape),
        in_specs=[VMEM] * 2 + [HBM],
        out_specs=(VMEM, VMEM),
        scratch_shapes=[pltpu.VMEM((13, HALO, LANES), F32)],
        compiler_params=params(),
        cost_estimate=cost(0),
        name="corners",
    )(top, bottom, after)


def stencil_kernel(
    comps,
    mp,
    peers,
    modulus,
    displace,
    load,
    history,
    stiffen,
    top,
    bottom,
    left,
    left_corner,
    right,
    right_corner,
    *rest,
):
    n = len(comps)
    out, xd, hx, sx, ld, st, sums, diffs, made, krh, krl, kbh, kbl, kwh, kwl, sems = rest[7:]
    rows, flat = stiffen.shape
    tall = rows + HALO
    tiles = flat // LANES
    entries = [comp + 3 * k for comp in comps for k in range(3)]
    center = (slice(0, rows), slice(0, flat))

    def displace_copy(i, t):
        return pltpu.make_async_copy(
            displace.at[i, :, t * LANES : (t + 1) * LANES],
            xd.at[i, t, PAD : PAD + rows, :],
            sems.at[i * tiles + t],
        )

    moves = [displace_copy(i, t) for t in range(tiles) for i in range(3)]
    base = 3 * tiles
    late = [pltpu.make_async_copy(stiffen, sx.at[center], sems.at[base])]
    late += [
        pltpu.make_async_copy(history.at[m], hx.at[(k,) + center], sems.at[base + 1 + k])
        for k, m in enumerate(entries)
    ]
    final = [
        pltpu.make_async_copy(load.at[comp], ld.at[k], sems.at[base + 1 + 3 * n + k])
        for k, comp in enumerate(comps)
    ]
    tables = [
        pltpu.make_async_copy(source, target, sems.at[base + 1 + 5 * n + k])
        for k, (source, target) in enumerate(
            zip(rest[:6], (krh, krl, kbh, kbl, kwh, kwl), strict=True)
        )
    ]
    late += tables[:2]
    final += tables[2:]
    for copy in moves + late + final:
        copy.start()
    left = (left, left_corner)
    right = (right, right_corner)
    lane = iota((tall, LANES), 1)
    short = iota((rows, LANES), 1)

    def tile_of(refs, at, target):
        part = slice(at // LANES * LANES, (at // LANES + 1) * LANES)
        value = jnp.concatenate([ref[:, part] for ref in refs], axis=0)
        shift = (target - at) % LANES
        return pltpu.roll(value, shift, 1) if shift else value

    for i in range(3):
        tile = jnp.where(lane < 64, tile_of(right, 64 * i, 0), tile_of(left, 64 * i, 64))
        xd[i, tiles, PAD : PAD + tall, :] = tile
        xd[i, tiles, PAD - 1 : PAD, :] = tile[tall - 1 : tall]
        xd[i, tiles, PAD + tall : PAD + tall + 1, :] = tile[0:1]
        for t in range(tiles):
            part = slice(t * LANES, (t + 1) * LANES)
            above = top[2 * i : 2 * i + 2, part]
            xd[i, t, PAD + rows : PAD + rows + 2, :] = bottom[2 * i : 2 * i + 2, part]
            xd[i, t, PAD + tall - 2 : PAD + tall, :] = above
            xd[i, t, PAD - 1 : PAD, :] = above[1:2]
    zeros = jnp.zeros((HALO, flat), F32)
    for k, m in enumerate(entries):
        at = 192 + 32 * m
        hx[k, rows:tall, 0:flat] = zeros
        hx[k, rows : rows + 1, 0:flat] = bottom[6 + m : 7 + m, :]
        hx[k, tall - 1 : tall, 0:flat] = top[6 + m : 7 + m, :]
        hx[k, :, flat:] = jnp.where(lane < 64, tile_of(right, at, 0), tile_of(left, at, 96))
    sx[rows:tall, 0:flat] = zeros
    sx[rows : rows + 1, 0:flat] = bottom[15:16, :] - 1.0
    sx[tall - 1 : tall, 0:flat] = top[15:16, :] - 1.0
    sx[:, flat:] = jnp.where(lane < 64, tile_of(right, 480, 0), tile_of(left, 480, 96)) - 1.0

    def lanes(t):
        return pl.ds(pl.multiple_of(t * LANES, LANES), LANES)

    def previous(t):
        return lax.rem(t + tiles, tiles + 1)

    def following(t):
        return lax.rem(t + 1, tiles + 1)

    def lower(ref, k, t, height, mask):
        mixed = jnp.where(
            mask >= LANES - R, ref[k, previous(t), 0:height, :], ref[k, t, 0:height, :]
        )
        return pltpu.roll(mixed, R, 1)

    def higher(ref, k, t, height, mask):
        mixed = jnp.where(mask < R, ref[k, following(t), 0:height, :], ref[k, t, 0:height, :])
        return pltpu.roll(mixed, LANES - R, 1)

    for copy in moves:
        copy.wait()

    def rows_step(t, carry):
        for i in range(3):
            xd[i, t, PAD + tall : PAD + tall + 1, :] = xd[i, t, PAD : PAD + 1, :]
            above = xd[i, t, PAD - 1 : PAD - 1 + tall, :]
            below = xd[i, t, PAD + 1 : PAD + 1 + tall, :]
            total = above + 4.0 * xd[i, t, PAD : PAD + tall, :] + below
            change = below - above
            sums[i, t] = total
            diffs[i, t] = change
        return carry

    lax.fori_loop(0, tiles + 1, rows_step, 0)
    for copy in late:
        copy.wait()

    def stress_step(t, carry):
        total = [None] * len(entries)
        for i in range(3):
            low = lower(sums, i, t, tall, lane)
            high = higher(sums, i, t, tall, lane)
            second = high - low
            both = low + high + 4.0 * sums[i, t]
            low = lower(diffs, i, t, tall, lane)
            high = higher(diffs, i, t, tall, lane)
            first = low + high + 4.0 * diffs[i, t]
            bh, bl = split(both)
            third = dot3(bh, bl, krh[...], krl[...])
            for k, m in enumerate(entries):
                part = (
                    (modulus[m, i] * (1.0 / 12.0)) * first
                    + (modulus[m, 3 + i] * (1.0 / 12.0)) * second
                    + modulus[m, 6 + i] * third
                )
                total[k] = part if total[k] is None else total[k] + part
        factor = 1.0 + sx[:, lanes(t)]
        for k in range(len(entries)):
            value = factor * total[k] + hx[k, :, lanes(t)]
            st[k, t, PAD : PAD + tall, :] = value
            st[k, t, PAD - 1 : PAD, :] = value[tall - 1 : tall]
        return carry

    def stress_steps(s, carry):
        stress_step(2 * s + 0, carry)
        stress_step(2 * s + 1, carry)
        return carry

    if n == 1:
        lax.fori_loop(0, tiles + 1, stress_step, 0, unroll=True)
    else:
        lax.fori_loop(0, tiles // 2, stress_steps, 0)
        stress_step(tiles, 0)
    for copy in final:
        copy.wait()

    sent = []
    for index in range(n):
        first_entry = 3 * index
        message = made.at[index]

        def pull_rows(t, carry):
            def around(k):
                field = first_entry + k
                return (
                    st[field, t, PAD - 1 : PAD - 1 + rows, :],
                    st[field, t, PAD : PAD + rows, :],
                    st[field, t, PAD + 1 : PAD + 1 + rows, :],
                )

            above, _, below = around(0)
            p = below - above
            above, now, below = around(1)
            q = above + 4.0 * now + below
            above, now, below = around(2)
            w = above + 4.0 * now + below
            sums[0, t, 0:rows, :] = p - q
            sums[1, t, 0:rows, :] = p + q
            sums[2, t, 0:rows, :] = w
            return carry

        lax.fori_loop(0, tiles + 1, pull_rows, 0)

        def message_step(s, carry):
            us, ws = [], []
            for half in range(2):
                t = 2 * s + half
                pull = 2.0 * (sums[0, t, 0:rows, :] + sums[1, t, 0:rows, :])
                pull = pull + lower(sums, 0, t, rows, short) + higher(sums, 1, t, rows, short)
                us.append(ld[index, :, lanes(t)] + pull * (1.0 / 12.0))
                w = 4.0 * sums[2, t, 0:rows, :]
                ws.append(w + lower(sums, 2, t, rows, short) + higher(sums, 2, t, rows, short))
            uh, ul = split(jnp.concatenate(us, axis=1))
            wh, wl = split(jnp.concatenate(ws, axis=1))
            value = dot3(kbh[...], kbl[...], uh, ul, True)
            value = value + dot3(kwh[...], kwl[...], wh, wl, True)
            here = pl.ds(pl.multiple_of(s * 8, 8), 8)
            for peer in range(peers):
                for m in range(mp):
                    row = (peer * mp + m) * 8
                    message[peer, here, m * rows : (m + 1) * rows] = value[row : row + 8, :]
            return carry

        def message_pair(s, carry):
            message_step(2 * s, carry)
            return message_step(2 * s + 1, carry)

        if n == 1:
            lax.fori_loop(0, tiles // 2, message_step, 0, unroll=True)
        else:
            lax.fori_loop(0, tiles // 4, message_pair, 0)
        sent += [pltpu.make_async_copy(message, out.at[:, index], sems.at[base + 1 + 4 * n + index])]
        sent[-1].start()
    for copy in sent:
        copy.wait()


def stencil(comps, mp, peers, modulus, displace, load, history, stiffen, halos, tables, after):
    rows, flat = stiffen.shape
    tall = rows + HALO
    wide = flat + LANES
    tiles = flat // LANES
    n = len(comps)
    block = (flat // R, mp * rows)
    return pl.pallas_call(
        functools.partial(stencil_kernel, comps, mp, peers),
        out_shape=jax.ShapeDtypeStruct((peers, n) + block, F32),
        in_specs=[SMEM] + [HBM] * 4 + [VMEM] * 6 + [HBM] * 7,
        out_specs=HBM,
        scratch_shapes=[
            pltpu.VMEM((3, tiles + 1, PAD + tall + HALO, LANES), F32),
            pltpu.VMEM((3 * n, tall, wide), F32),
            pltpu.VMEM((tall, wide), F32),
            pltpu.VMEM((n, rows, flat), F32),
            pltpu.VMEM((3 * n, tiles + 1, PAD + tall, LANES), F32),
            pltpu.VMEM((3, tiles + 1, tall, LANES), F32),
            pltpu.VMEM((3, tiles + 1, tall, LANES), F32),
            pltpu.VMEM((n, peers) + block, F32),
            *(pltpu.VMEM(table.shape, BF) for table in tables),
            pltpu.SemaphoreType.DMA((3 * tiles + 7 + 5 * n,)),
        ],
        compiler_params=params(),
        cost_estimate=cost(13 + 8 * n),
        name="stencil",
    )(modulus, displace, load, history, stiffen, *halos, *tables, after)


def cycle_kernel(index, parts, ids, piece, table_ref, after, *refs):
    del after
    outs = refs[:parts]
    xh, xl, raw, table, made, sems = refs[parts:]
    peers, _, height, _ = piece.shape
    copies = fetch(
        [piece.at[j, index] for j in range(peers)] + [table_ref],
        [raw.at[j] for j in range(peers)] + [table],
        sems,
    )
    for j in range(peers):
        copies[j].wait()
        at = slice(j * height, (j + 1) * height)
        hi, lo = split(raw[j])
        xh[at, :] = hi
        xl[at, :] = lo
    copies[peers].wait()
    value = stacked3(table, xh[...], xl[...])
    block = outs[0].shape[0]
    for b in range(parts):
        made[jnp.bitwise_xor(ids[1], b)] = value[b * block : (b + 1) * block]
    sent = fetch([made.at[d] for d in range(parts)], outs, sems.at[pl.ds(peers + 1, parts)])
    for copy in sent:
        copy.wait()


def cycle_stage(index, ids, piece, table, parts, after):
    peers, _, height, width = piece.shape
    count = peers * height
    shape = jax.ShapeDtypeStruct((count // parts, width), F32)
    return pl.pallas_call(
        functools.partial(cycle_kernel, index, parts),
        out_shape=(shape,) * parts,
        in_specs=[SMEM] + [HBM] * 3,
        out_specs=(HBM,) * parts,
        scratch_shapes=[
            pltpu.VMEM((count, width), BF),
            pltpu.VMEM((count, width), BF),
            pltpu.VMEM((peers, height, width), F32),
            pltpu.VMEM(table.shape, BF),
            pltpu.VMEM((parts,) + shape.shape, F32),
            pltpu.SemaphoreType.DMA((peers + 1 + parts,)),
        ],
        compiler_params=params(24),
        cost_estimate=cost(0),
        name="cycle_stage",
    )(ids, piece, table, after)


def axial_kernel(mp, parts, ids, radial, cyc, axial, *refs):
    ins = refs[:parts]
    table_ref, after, out, x, xh, xl, raw, table, made, sems = refs[parts:]
    del after
    kc, width = ins[0].shape
    rows = width // mp
    half = mp * kc
    count = parts * rows
    copies = fetch([*ins, table_ref], [raw.at[j] for j in range(parts)] + [table], sems)
    for j in range(parts):
        source = jnp.bitwise_xor(ids[1], j)
        at = pl.ds(pl.multiple_of(source * rows, rows), rows)
        copies[j].wait()
        for m in range(mp):
            hi, lo = split(raw[j, :, m * rows : (m + 1) * rows])
            x[m * kc : (m + 1) * kc, at] = hi
            x[half + m * kc : half + (m + 1) * kc, at] = lo
    copies[parts].wait()
    mine = cyc[pl.ds(pl.multiple_of(ids[1] * kc, kc), kc), :]
    base = axial[...] + mine
    value = stacked3(x, table[0:count, :], table[count:, :])
    for m in range(mp):
        part = slice(m * kc, (m + 1) * kc)
        hi, lo = split(value[part] / (base + radial[ids[0] * mp + m]))
        xh[part, :] = hi
        xl[part, :] = lo
    made[...] = stacked3(table, xh[...], xl[...], True)
    copy = pltpu.make_async_copy(made, out, sems.at[parts + 1])
    copy.start()
    copy.wait()


def axial_stage(ids, radial, cyc, axial, pieces, table, mp, after):
    parts = len(pieces)
    kc, width = pieces[0].shape
    count = width // mp * parts
    return pl.pallas_call(
        functools.partial(axial_kernel, mp, parts),
        out_shape=jax.ShapeDtypeStruct((count, mp * kc), F32),
        in_specs=[SMEM, SMEM, VMEM, VMEM] + [HBM] * (parts + 2),
        out_specs=HBM,
        scratch_shapes=[
            pltpu.VMEM((2 * mp * kc, count), BF),
            pltpu.VMEM((mp * kc, count), BF),
            pltpu.VMEM((mp * kc, count), BF),
            pltpu.VMEM((parts, kc, width), F32),
            pltpu.VMEM(table.shape, BF),
            pltpu.VMEM((count, mp * kc), F32),
            pltpu.SemaphoreType.DMA((parts + 2,)),
        ],
        compiler_params=params(24),
        cost_estimate=cost(0),
        name="axial_stage",
    )(ids, radial, cyc, axial, *pieces, table, after)


def return_kernel(comp, mp, parts, peers, piece, *refs):
    out, x, y, raw, table, weave, kernel, made, sems = refs[-9:]
    _, few, width = piece.shape
    kc = width // mp
    count = table.shape[1]
    depth, span = kernel.shape[0] // 2, kernel.shape[1]
    half = mp * peers * few
    groups = count * mp // HALF
    copies = fetch((piece, *refs[:3]), (raw, table, weave, kernel), sems)
    copies[0].wait()
    for p in range(parts):
        for q in range(peers):
            for m in range(mp):
                row = (m * peers + q) * few
                hi, lo = split(raw[p * peers + q, :, m * kc : (m + 1) * kc])
                x[row : row + few, p * kc : (p + 1) * kc] = hi
                x[half + row : half + row + few, p * kc : (p + 1) * kc] = lo
    for copy in copies[1:]:
        copy.wait()
    value = split(stacked3(x, table[0:count, :], table[count:, :]))
    rows = peers * few
    front = iota((few, LANES), 1) < HALF
    for t in range(count // LANES):
        columns = slice(t * LANES, (t + 1) * LANES)
        for part, first in zip(value, (0, groups * few), strict=True):
            gathered = jnp.concatenate(
                [part[m * rows : (m + 1) * rows, columns] for m in range(mp)], axis=1
            )
            woven = dot(gathered, weave[...])
            for g in range(mp):
                block = woven[:, g * LANES : (g + 1) * LANES]
                turned = pltpu.roll(block, HALF, 1)
                row = first + 2 * (t * mp + g) * few
                for q in range(0, peers, 2):
                    one = slice(q * few, (q + 1) * few)
                    two = slice((q + 1) * few, (q + 2) * few)
                    to = slice(q * HALF, q * HALF + LANES)
                    y[row : row + few, to] = jnp.where(front, block[one], turned[two]).astype(BF)
                    y[row + few : row + 2 * few, to] = jnp.where(
                        front, turned[one], block[two]
                    ).astype(BF)
    result = stacked3(y, kernel[0:depth, :], kernel[depth:, :])
    for g in range(groups):
        made[:, g * span : (g + 1) * span] = result[g * few : (g + 1) * few, :]
    copy = pltpu.make_async_copy(made, out.at[comp], sems.at[4])
    copy.start()
    copy.wait()


def return_stage(comp, piece, table, weave, back, mp, parts, carried):
    devices, few, width = piece.shape
    peers = devices // parts
    count = table.shape[1]
    depth, span = back.shape[0] // 2, back.shape[1]
    groups = count * mp // HALF
    extra = [] if carried is None else [carried]
    return pl.pallas_call(
        functools.partial(return_kernel, comp, mp, parts, peers),
        out_shape=jax.ShapeDtypeStruct((3, few, groups * span), F32),
        in_specs=[HBM] * (4 + len(extra)),
        out_specs=HBM,
        scratch_shapes=[
            pltpu.VMEM((2 * mp * peers * few, count), BF),
            pltpu.VMEM((2 * groups * few, depth), BF),
            pltpu.VMEM(piece.shape, F32),
            pltpu.VMEM(table.shape, BF),
            pltpu.VMEM(weave.shape, BF),
            pltpu.VMEM(back.shape, BF),
            pltpu.VMEM((few, groups * span), F32),
            pltpu.SemaphoreType.DMA((5,)),
        ],
        input_output_aliases={4: 0} if extra else {},
        compiler_params=params(32),
        cost_estimate=cost(0),
        name="return_stage",
    )(piece, table, weave, back, *extra)


def across(block, axis):
    return lax.all_to_all(block, axis, split_axis=0, concat_axis=0, tiled=True)


def swap(pieces, axis):
    count = len(pieces)
    return [pieces[0]] + [
        lax.ppermute(pieces[d], axis, [(i, i ^ d) for i in range(count)]) for d in range(1, count)
    ]


ORDER = (
    ("stencil", (0,)),
    ("stencil", (1, 2)),
    ("cycle", 0),
    ("tables", None),
    ("axial", 0),
    ("cycle", 1),
    ("axial", 1),
    ("cycle", 2),
    ("return", 0),
    ("axial", 2),
    ("return", 1),
    ("return", 2),
)


def body(
    displace,
    load,
    history,
    stiffen,
    modulus,
    radial_slope,
    radial_basis,
    axial_eig,
    cycle_eig,
    radial_eig,
):
    parts = lax.axis_size("ax")
    peers = lax.axis_size("circ")
    mp = R // peers
    rows, flat = stiffen.shape
    count_a = parts * rows
    count_c = peers * flat // R
    me = lax.axis_index("circ").astype(jnp.int32)
    pe = lax.axis_index("ax").astype(jnp.int32)
    ids = jnp.stack([me, pe])

    upward, downward, leftward, rightward = pack(displace, history, stiffen)
    ahead = [(i, i + 1) for i in range(parts - 1)]
    back_ahead = [(j, i) for i, j in ahead]
    around = [(i, (i + 1) % peers) for i in range(peers)]
    back_around = [(j, i) for i, j in around]
    bottom = lax.ppermute(upward, "ax", back_ahead)
    top = lax.ppermute(downward, "ax", ahead)
    right = lax.ppermute(leftward, "circ", back_around)
    left = lax.ppermute(rightward, "circ", around)
    front = front_tables(radial_slope, radial_basis, mp)
    to_left, to_right = corners(top, bottom, front[0])
    right_corner = lax.ppermute(to_left, "circ", back_around)
    left_corner = lax.ppermute(to_right, "circ", around)
    halos = (top, bottom, left, left_corner, right, right_corner)

    cycle_table_stack = host_split(host_cycle(count_c))
    axial_table_stack = host_split(host_axial(count_a))
    weave = host_weave(mp)
    cyc = cycle_eig[:, None]
    axial = axial_eig[None, :]

    lines = [None] * 3
    out, after = None, ids
    for kind, i in ORDER:
        if kind == "stencil":
            after = stencil(
                i, mp, peers, modulus, displace, load, history, stiffen, halos, front, after
            )
            block = across(after, "circ")
            for index, comp in enumerate(i):
                lines[comp] = (index, block)
        elif kind == "tables":
            after = back = back_tables(radial_basis, mp, peers, after)
        elif kind == "cycle":
            index, block = lines[i]
            sent = cycle_stage(index, ids, block, cycle_table_stack, parts, after)
            after = sent[0]
            lines[i] = swap(list(sent), "ax")
        elif kind == "axial":
            after = axial_stage(
                ids, radial_eig, cyc, axial, lines[i], axial_table_stack, mp, after
            )
            block = after.reshape(parts * peers, rows // peers, -1)
            lines[i] = across(block, ("ax", "circ"))
        else:
            out = return_stage(i, lines[i], cycle_table_stack, weave, back, mp, parts, out)
            after = out
    return out


def tiled(mesh):
    parts, peers = mesh.shape["ax"], mesh.shape["circ"]
    rows, flat = NA // parts, NC // peers * R
    return (
        parts & (parts - 1) == 0
        and peers & (peers - 1) == 0
        and R == 32
        and R % peers == 0
        and peers * (R // peers) * 8 == 8 * R
        and rows % LANES == 0
        and (NC // parts) % LANES == 0
        and flat % (2 * LANES) == 0
        and (NC // peers) % 16 == 0
        and (rows // peers) % 16 == 0
        and HALF % (R // peers) == 0
        and peers % 2 == 0
    )


def solution(mesh):
    return jax.shard_map(
        body if tiled(mesh) else plain_body,
        mesh=mesh,
        in_specs=(
            P(None, "ax", "circ"),
            P(None, "ax", "circ"),
            P(None, "ax", "circ"),
            P("ax", "circ"),
            P(),
            P(),
            P(),
            P(),
            P(),
            P(),
        ),
        out_specs=P(None, ("ax", "circ"), None),
        check_vma=False,
    )
```

```python
import math

import functools

import jax
import jax.numpy as jnp
import ml_dtypes
import numpy as np
from jax import lax
from jax.experimental import pallas as pl
from jax.experimental.pallas import tpu as pltpu
from jax.sharding import PartitionSpec as P

NA = 512
NC = 512
R = 32


def with_halo(block, sides, width, periodic):
    for axis, dim in sides:
        count = lax.axis_size(axis)
        forward = [(i, i + 1) for i in range(count - 1)]
        if periodic:
            forward.append((count - 1, 0))
        backward = [(target, source) for source, target in forward]
        low = lax.ppermute(
            lax.slice_in_dim(block, block.shape[dim] - width, None, axis=dim), axis, forward
        )
        high = lax.ppermute(lax.slice_in_dim(block, 0, width, axis=dim), axis, backward)
        block = jnp.concatenate([low, block, high], axis=dim)
    return block


def cycle_table(count):
    col = jnp.arange(count, dtype=jnp.int32)[:, None]
    mode = jnp.arange(count, dtype=jnp.int32)[None, :]
    half = count // 2
    folded = jnp.where(mode <= half, mode, mode - half)
    shift = jnp.where(mode <= half, 0.0, 0.5 * math.pi).astype(jnp.float32)
    scale_ends = jnp.where(
        (mode == 0) | (mode == half), math.sqrt(1.0 / count), math.sqrt(2.0 / count)
    ).astype(jnp.float32)
    phase = (col * folded % count).astype(jnp.float32) * (2.0 * math.pi / count)
    return jnp.cos(phase - shift) * scale_ends


def axial_table(rows, count):
    first = (rows + 1)[:, None]
    mode = jnp.arange(count, dtype=jnp.int32)[None, :] + 1
    phase = (first * mode % (2 * (count + 1))).astype(jnp.float32) * (math.pi / (count + 1))
    return jnp.sin(phase) * math.sqrt(2.0 / (count + 1))


def extend(field):
    rows = with_halo(field, (("ax", 1),), 1, False)
    return with_halo(rows, (("circ", 2),), R, True)


def cycle_parts(ext):
    span = ext.shape[2] - 2 * R
    left = ext[:, :, :span]
    middle = ext[:, :, R : R + span]
    right = ext[:, :, 2 * R :]
    return ((left + 4.0 * middle + right) / 6.0, (right - left) * 0.5)


def row_smooth(field):
    return (field[:, :-2] + 4.0 * field[:, 1:-1] + field[:, 2:]) / 6.0


def row_slope(field):
    return (field[:, 2:] - field[:, :-2]) * 0.5


def radial_mix(field, matrix, form):
    count, rows, flat = field.shape
    cube = field.reshape(count, rows, flat // R, R)
    mixed = jnp.einsum(form, cube, matrix, precision=lax.Precision.HIGHEST)
    return mixed.reshape(count, rows, flat)


def into_cycles(field):
    return lax.all_to_all(field, "circ", split_axis=1, concat_axis=2, tiled=True)


def cycle_forward(field, table, basis):
    count, rows, flat = field.shape
    cube = field.reshape(count * rows, NC, R)
    cube = jnp.einsum("bcr,ck->bkr", cube, table, precision=lax.Precision.HIGHEST)
    cube = jnp.einsum("bkr,rm->bkm", cube, basis, precision=lax.Precision.HIGHEST)
    return cube.reshape(count, rows, flat)


def cycle_inverse(field, table, basis):
    count, rows, flat = field.shape
    cube = field.reshape(count * rows, NC, R)
    cube = jnp.einsum("bkm,rm->bkr", cube, basis, precision=lax.Precision.HIGHEST)
    cube = jnp.einsum("bkr,ck->bcr", cube, table, precision=lax.Precision.HIGHEST)
    return cube.reshape(count, rows, flat)


def axial_solve(lines, forward_table, inverse_table, weights):
    modes = jnp.einsum("pk,cps->cks", forward_table, lines, precision=lax.Precision.HIGHEST)
    return jnp.einsum(
        "ak,cks->cas", inverse_table, modes * weights[None], precision=lax.Precision.HIGHEST
    )


def plain_body(
    displace,
    load,
    history,
    stiffen,
    modulus,
    radial_slope,
    radial_basis,
    axial_eig,
    cycle_eig,
    radial_eig,
):
    ext = extend(displace)
    cycle_v, cycle_d = cycle_parts(ext)
    smooth_v = row_smooth(cycle_v)
    radial_part = radial_mix(smooth_v, radial_slope, "iacq,rq->iacr")
    grads = jnp.concatenate([row_slope(cycle_v), row_smooth(cycle_d), radial_part], axis=0)
    mixed = jnp.einsum("mn,nac->mac", modulus, grads, precision=lax.Precision.HIGHEST)
    stress = (1.0 + stiffen)[None] * mixed + history
    ext_stress = extend(stress)
    first_v, unused_d = cycle_parts(ext_stress[0:3])
    unused_v, second_d = cycle_parts(ext_stress[3:6])
    third_v, unused_e = cycle_parts(ext_stress[6:9])
    third = radial_mix(row_smooth(third_v), radial_slope, "iacr,rq->iacq")
    pull = -row_slope(first_v) - row_smooth(second_d) + third
    resid = load - pull
    a_dev = displace.shape[1]
    flat_dev = displace.shape[2]
    n_ax = lax.axis_size("ax")
    n_circ = lax.axis_size("circ")
    piece = flat_dev // n_ax
    rows_cycle = a_dev // n_circ
    table_cycle = cycle_table(NC)
    spec = cycle_forward(into_cycles(resid), table_cycle, radial_basis)
    start = lax.axis_index("circ") * flat_dev + lax.axis_index("ax") * piece
    index_flat = start + jnp.arange(piece, dtype=jnp.int32)
    denom = (
        axial_eig[:, None]
        + jnp.take(cycle_eig, index_flat // R)[None, :]
        + jnp.take(radial_eig, index_flat % R)[None, :]
    )
    weights = 1.0 / denom
    natural_rows = jnp.arange(NA, dtype=jnp.int32)
    inverse_table = axial_table(natural_rows, NA)
    cube = spec.reshape(3, rows_cycle, n_circ, flat_dev)
    lines = lax.all_to_all(
        lax.all_to_all(cube, "ax", split_axis=3, concat_axis=1, tiled=True),
        "circ",
        split_axis=2,
        concat_axis=1,
        tiled=True,
    ).reshape(3, NA, piece)
    group = n_ax * rows_cycle
    outer = natural_rows // group
    inner = natural_rows % group
    source_rows = inner // rows_cycle * a_dev + outer * rows_cycle + inner % rows_cycle
    forward_table = axial_table(source_rows, NA)
    solved = axial_solve(lines, forward_table, inverse_table, weights)
    cycles_back = lax.all_to_all(
        lax.all_to_all(solved, "ax", split_axis=1, concat_axis=2, tiled=True),
        "circ",
        split_axis=1,
        concat_axis=2,
        tiled=True,
    )
    return cycle_inverse(cycles_back, table_cycle, radial_basis)


BF = jnp.bfloat16
F32 = jnp.float32
VMEM = pl.BlockSpec(memory_space=pltpu.VMEM)
SMEM = pl.BlockSpec(memory_space=pltpu.SMEM)
HBM = pl.BlockSpec(memory_space=pltpu.HBM)
HALO = 8
PAD = 8
HALF = 64
LANES = 128


def params(mebibytes=60):
    return pltpu.CompilerParams(vmem_limit_bytes=mebibytes << 20)


def cost(microseconds):
    return pl.CostEstimate(flops=1, bytes_accessed=int(microseconds * 3.6e6) + 1, transcendentals=0)


def split(x):
    hi = x.astype(BF)
    return hi, (x - hi.astype(F32)).astype(BF)


def dot(a, b, transposed=False):
    dims = (((1,), (1 if transposed else 0,)), ((), ()))
    return lax.dot_general(a, b, dims, preferred_element_type=F32)


def dot3(ah, al, bh, bl, transposed=False):
    return dot(ah, bh, transposed) + (dot(ah, bl, transposed) + dot(al, bh, transposed))


def stacked3(both, bh, bl, transposed=False):
    rows = both.shape[0] // 2
    upper = dot(both[...], bh, transposed)
    return upper[:rows] + (upper[rows:] + dot(both[0:rows, :], bl, transposed))


def exact(a, b, transposed=False):
    dims = (((1,), (1 if transposed else 0,)), ((), ()))
    return lax.dot_general(
        a, b, dims, precision=lax.Precision.HIGHEST, preferred_element_type=F32
    )


def host_split(table):
    hi = table.astype(np.float32).astype(ml_dtypes.bfloat16)
    lo = (table - hi.astype(np.float64)).astype(np.float32).astype(ml_dtypes.bfloat16)
    return jnp.asarray(np.concatenate([hi, lo], axis=0))


def host_cycle(count):
    col = np.arange(count)[None, :]
    mode = np.arange(count)[:, None]
    half = count // 2
    folded = np.where(mode <= half, mode, mode - half)
    phase = 2.0 * np.pi * ((col * folded) % count) / count
    scale = np.where((mode == 0) | (mode == half), math.sqrt(1.0 / count), math.sqrt(2.0 / count))
    return np.where(mode <= half, np.cos(phase), np.sin(phase)) * scale


def host_axial(count):
    first = np.arange(1, count + 1)
    phase = np.pi * (np.outer(first, first) % (2 * (count + 1))) / (count + 1)
    return np.sin(phase) * math.sqrt(2.0 / (count + 1))


def host_weave(mp):
    table = np.zeros((mp * LANES, mp * LANES), np.float32)
    for m in range(mp):
        for c in range(LANES):
            table[m * LANES + c, c * mp + m] = 1.0
    return jnp.asarray(table.astype(ml_dtypes.bfloat16))


def iota(shape, dim):
    return lax.broadcasted_iota(jnp.int32, shape, dim)


def onehot(condition):
    return jnp.where(condition, 1.0, 0.0).astype(F32)


def write_split(hi_ref, lo_ref, value):
    hi, lo = split(value)
    hi_ref[...] = hi
    lo_ref[...] = lo


def fetch(sources, targets, sems):
    copies = [
        pltpu.make_async_copy(source, target, sems.at[k])
        for k, (source, target) in enumerate(zip(sources, targets, strict=True))
    ]
    for copy in copies:
        copy.start()
    return copies


def write_stack(ref, value):
    rows = value.shape[0]
    hi, lo = split(value)
    ref[0:rows, :] = hi
    ref[rows:, :] = lo


def fetch(sources, targets, sems):
    copies = [
        pltpu.make_async_copy(source, target, sems.at[k])
        for k, (source, target) in enumerate(zip(sources, targets, strict=True))
    ]
    for copy in copies:
        copy.start()
    return copies


def front_tables_kernel(mp, slope_ref, basis_ref, *refs):
    outs, made, sems = refs[:6], refs[6:12], refs[12]
    krh, krl, kbh, kbl, kwh, kwl = made
    slope = slope_ref[...]
    basis = basis_ref[...]
    side = LANES
    row = iota((side, R), 0)
    col = iota((side, R), 1)
    pick = onehot(row % R == col)
    mask = iota((side, side), 0) // R == iota((side, side), 1) // R
    value = exact(exact(pick, slope, True), pick, True)
    write_split(krh, krl, jnp.where(mask, value * (1.0 / 36.0), 0.0))
    side = 8 * R
    row = iota((side, R), 0)
    col = iota((side, R), 1)
    pick = onehot(row % R == col)
    block = mp * 8
    mode = onehot(row // block * mp + (row % block) // 8 == col)
    mask = iota((side, side), 0) % 8 == iota((side, side), 1) // R
    value = exact(exact(mode, basis, True), pick, True)
    write_split(kbh, kbl, jnp.where(mask, value, 0.0))
    both = exact(slope, basis)
    value = exact(exact(mode, both, True), pick, True)
    write_split(kwh, kwl, jnp.where(mask, value * (-1.0 / 36.0), 0.0))
    for copy in fetch(made, outs, sems):
        copy.wait()


def front_tables(slope, basis, mp):
    one = jax.ShapeDtypeStruct((LANES, LANES), BF)
    two = jax.ShapeDtypeStruct((8 * R, 8 * R), BF)
    return pl.pallas_call(
        functools.partial(front_tables_kernel, mp),
        out_shape=(one, one, two, two, two, two),
        in_specs=[VMEM, VMEM],
        out_specs=(HBM,) * 6,
        scratch_shapes=[pltpu.VMEM(x.shape, BF) for x in (one, one, two, two, two, two)]
        + [pltpu.SemaphoreType.DMA((6,))],
        compiler_params=params(),
        name="front_tables",
    )(slope, basis)


def back_tables_kernel(mp, basis_ref, after, out, made, sem):
    del after
    rows, cols = made.shape[0] // 2, made.shape[1]
    row = iota((rows, R), 0)
    col = iota((rows, R), 1)
    mode = onehot(row // HALF * mp + row % mp == col)
    pick = onehot(iota((cols, R), 0) % R == iota((cols, R), 1))
    value = exact(exact(mode, basis_ref[...], True), pick, True)
    mask = (iota((rows, cols), 0) % HALF) // mp == iota((rows, cols), 1) // R
    write_stack(made, jnp.where(mask, value, 0.0))
    copy = pltpu.make_async_copy(made, out, sem)
    copy.start()
    copy.wait()


def back_tables(basis, mp, peers, after):
    shape = jax.ShapeDtypeStruct((2 * peers * HALF, HALF // mp * R), BF)
    return pl.pallas_call(
        functools.partial(back_tables_kernel, mp),
        out_shape=shape,
        in_specs=[VMEM, HBM],
        out_specs=HBM,
        scratch_shapes=[pltpu.VMEM(shape.shape, BF), pltpu.SemaphoreType.DMA],
        compiler_params=params(24),
        name="back_tables",
    )(basis, after)


def pack_columns(out, lane, wide, slim, pieces):
    for tile in range(4):
        value = None
        for index, piece in enumerate(pieces):
            at = 64 * index if index < 3 else 96 + 32 * index
            if at // LANES == tile:
                shift = (at - (wide if index < 3 else slim)) % LANES
                moved = pltpu.roll(piece, shift, 1) if shift else piece
                value = moved if value is None else jnp.where(lane >= at % LANES, moved, value)
        out[:, tile * LANES : (tile + 1) * LANES] = value


def pack_kernel(
    displace, history, stiffen, up_ref, down_ref, left_ref, right_ref, d, h, s, dc, hc, sc, sems
):
    rows, flat = stiffen.shape
    sources, targets = [], []
    for k, at in enumerate((slice(0, 8), slice(rows - 8, rows))):
        sources += [displace.at[:, at, :], history.at[:, at, :], stiffen.at[at, :]]
        targets += [d.at[k], h.at[k], s.at[k]]
    for k, at in enumerate((slice(0, LANES), slice(flat - LANES, flat))):
        sources += [displace.at[:, :, at], history.at[:, :, at], stiffen.at[:, at]]
        targets += [dc.at[k], hc.at[k], sc.at[k]]
    copies = fetch(sources, targets, sems)
    for copy in copies[:6]:
        copy.wait()
    for k, first, last, out in ((0, 0, 0, up_ref), (1, 6, 7, down_ref)):
        for i in range(3):
            out[2 * i : 2 * i + 2, :] = d[k, i, first : first + 2, :]
        for n in range(9):
            out[6 + n : 7 + n, :] = h[k, n, last : last + 1, :]
        out[15:16, :] = 1.0 + s[k, last : last + 1, :]
    for copy in copies[6:]:
        copy.wait()
    lane = iota((rows, LANES), 1)
    for k, out, wide, slim in ((0, left_ref, 0, 0), (1, right_ref, LANES - 2 * R, LANES - R)):
        pieces = [dc[k, i] for i in range(3)] + [hc[k, n] for n in range(9)] + [1.0 + sc[k]]
        pack_columns(out, lane, wide, slim, pieces)


def pack(displace, history, stiffen):
    rows, flat = stiffen.shape
    row = jax.ShapeDtypeStruct((16, flat), F32)
    column = jax.ShapeDtypeStruct((rows, 4 * LANES), F32)
    return pl.pallas_call(
        pack_kernel,
        out_shape=(row, row, column, column),
        in_specs=[HBM] * 3,
        out_specs=(VMEM,) * 4,
        scratch_shapes=[
            pltpu.VMEM((2, 3, 8, flat), F32),
            pltpu.VMEM((2, 9, 8, flat), F32),
            pltpu.VMEM((2, 8, flat), F32),
            pltpu.VMEM((2, 3, rows, LANES), F32),
            pltpu.VMEM((2, 9, rows, LANES), F32),
            pltpu.VMEM((2, rows, LANES), F32),
            pltpu.SemaphoreType.DMA((12,)),
        ],
        compiler_params=params(60),
        cost_estimate=cost(0),
        name="pack",
    )(displace, history, stiffen)


def corners_kernel(top, bottom, after, left_ref, right_ref, tall):
    del after
    flat = top.shape[1]
    lane = iota((HALO, LANES), 1)
    tall[...] = jnp.zeros_like(tall)
    for out, at, wide, slim in (
        (left_ref, slice(0, LANES), 0, 0),
        (right_ref, slice(flat - LANES, flat), LANES - 2 * R, LANES - R),
    ):
        pieces = []
        for index in range(13):
            first, count = (2 * index, 2) if index < 3 else (3 + index, 1)
            tall[index, 0:count, :] = bottom[first : first + count, at]
            tall[index, HALO - count : HALO, :] = top[first : first + count, at]
            pieces.append(tall[index])
        pack_columns(out, lane, wide, slim, pieces)


def corners(top, bottom, after):
    shape = jax.ShapeDtypeStruct((HALO, 4 * LANES), F32)
    return pl.pallas_call(
        corners_kernel,
        out_shape=(shape, shape),
        in_specs=[VMEM] * 2 + [HBM],
        out_specs=(VMEM, VMEM),
        scratch_shapes=[pltpu.VMEM((13, HALO, LANES), F32)],
        compiler_params=params(),
        cost_estimate=cost(0),
        name="corners",
    )(top, bottom, after)


def stencil_kernel(
    comps,
    mp,
    peers,
    modulus,
    displace,
    load,
    history,
    stiffen,
    top,
    bottom,
    left,
    left_corner,
    right,
    right_corner,
    *rest,
):
    n = len(comps)
    outs = rest[7 : 7 + n]
    xd, hx, sx, ld, st, sums, diffs, made, krh, krl, kbh, kbl, kwh, kwl, sems = rest[7 + n :]
    rows, flat = stiffen.shape
    tall = rows + HALO
    tiles = flat // LANES
    entries = [comp + 3 * k for comp in comps for k in range(3)]
    center = (slice(0, rows), slice(0, flat))

    def displace_copy(i, t):
        return pltpu.make_async_copy(
            displace.at[i, :, t * LANES : (t + 1) * LANES],
            xd.at[i, t, PAD : PAD + rows, :],
            sems.at[i * tiles + t],
        )

    moves = [displace_copy(i, t) for t in range(tiles) for i in range(3)]
    base = 3 * tiles
    late = [pltpu.make_async_copy(stiffen, sx.at[center], sems.at[base])]
    late += [
        pltpu.make_async_copy(history.at[m], hx.at[(k,) + center], sems.at[base + 1 + k])
        for k, m in enumerate(entries)
    ]
    final = [
        pltpu.make_async_copy(load.at[comp], ld.at[k], sems.at[base + 1 + 3 * n + k])
        for k, comp in enumerate(comps)
    ]
    tables = [
        pltpu.make_async_copy(source, target, sems.at[base + 1 + 5 * n + k])
        for k, (source, target) in enumerate(
            zip(rest[:6], (krh, krl, kbh, kbl, kwh, kwl), strict=True)
        )
    ]
    late += tables[:2]
    final += tables[2:]
    for copy in moves + late + final:
        copy.start()
    left = (left, left_corner)
    right = (right, right_corner)
    lane = iota((tall, LANES), 1)
    short = iota((rows, LANES), 1)

    def tile_of(refs, at, target):
        part = slice(at // LANES * LANES, (at // LANES + 1) * LANES)
        value = jnp.concatenate([ref[:, part] for ref in refs], axis=0)
        shift = (target - at) % LANES
        return pltpu.roll(value, shift, 1) if shift else value

    for i in range(3):
        tile = jnp.where(lane < 64, tile_of(right, 64 * i, 0), tile_of(left, 64 * i, 64))
        xd[i, tiles, PAD : PAD + tall, :] = tile
        xd[i, tiles, PAD - 1 : PAD, :] = tile[tall - 1 : tall]
        xd[i, tiles, PAD + tall : PAD + tall + 1, :] = tile[0:1]
        for t in range(tiles):
            part = slice(t * LANES, (t + 1) * LANES)
            above = top[2 * i : 2 * i + 2, part]
            xd[i, t, PAD + rows : PAD + rows + 2, :] = bottom[2 * i : 2 * i + 2, part]
            xd[i, t, PAD + tall - 2 : PAD + tall, :] = above
            xd[i, t, PAD - 1 : PAD, :] = above[1:2]
    zeros = jnp.zeros((HALO, flat), F32)
    for k, m in enumerate(entries):
        at = 192 + 32 * m
        hx[k, rows:tall, 0:flat] = zeros
        hx[k, rows : rows + 1, 0:flat] = bottom[6 + m : 7 + m, :]
        hx[k, tall - 1 : tall, 0:flat] = top[6 + m : 7 + m, :]
        hx[k, :, flat:] = jnp.where(lane < 64, tile_of(right, at, 0), tile_of(left, at, 96))
    sx[rows:tall, 0:flat] = zeros
    sx[rows : rows + 1, 0:flat] = bottom[15:16, :] - 1.0
    sx[tall - 1 : tall, 0:flat] = top[15:16, :] - 1.0
    sx[:, flat:] = jnp.where(lane < 64, tile_of(right, 480, 0), tile_of(left, 480, 96)) - 1.0

    def lanes(t):
        return pl.ds(pl.multiple_of(t * LANES, LANES), LANES)

    def previous(t):
        return lax.rem(t + tiles, tiles + 1)

    def following(t):
        return lax.rem(t + 1, tiles + 1)

    def lower(ref, k, t, height, mask):
        mixed = jnp.where(
            mask >= LANES - R, ref[k, previous(t), 0:height, :], ref[k, t, 0:height, :]
        )
        return pltpu.roll(mixed, R, 1)

    def higher(ref, k, t, height, mask):
        mixed = jnp.where(mask < R, ref[k, following(t), 0:height, :], ref[k, t, 0:height, :])
        return pltpu.roll(mixed, LANES - R, 1)

    for copy in moves:
        copy.wait()

    def rows_step(t, carry):
        for i in range(3):
            xd[i, t, PAD + tall : PAD + tall + 1, :] = xd[i, t, PAD : PAD + 1, :]
            above = xd[i, t, PAD - 1 : PAD - 1 + tall, :]
            below = xd[i, t, PAD + 1 : PAD + 1 + tall, :]
            total = above + 4.0 * xd[i, t, PAD : PAD + tall, :] + below
            change = below - above
            sums[i, t] = total
            diffs[i, t] = change
        return carry

    lax.fori_loop(0, tiles + 1, rows_step, 0)
    for copy in late:
        copy.wait()

    def stress_step(t, carry):
        total = [None] * len(entries)
        for i in range(3):
            low = lower(sums, i, t, tall, lane)
            high = higher(sums, i, t, tall, lane)
            second = high - low
            both = low + high + 4.0 * sums[i, t]
            low = lower(diffs, i, t, tall, lane)
            high = higher(diffs, i, t, tall, lane)
            first = low + high + 4.0 * diffs[i, t]
            bh, bl = split(both)
            third = dot3(bh, bl, krh[...], krl[...])
            for k, m in enumerate(entries):
                part = (
                    (modulus[m, i] * (1.0 / 12.0)) * first
                    + (modulus[m, 3 + i] * (1.0 / 12.0)) * second
                    + modulus[m, 6 + i] * third
                )
                total[k] = part if total[k] is None else total[k] + part
        factor = 1.0 + sx[:, lanes(t)]
        for k in range(len(entries)):
            value = factor * total[k] + hx[k, :, lanes(t)]
            st[k, t, PAD : PAD + tall, :] = value
            st[k, t, PAD - 1 : PAD, :] = value[tall - 1 : tall]
        return carry

    def stress_steps(s, carry):
        stress_step(2 * s + 0, carry)
        stress_step(2 * s + 1, carry)
        return carry

    if n == 1:
        lax.fori_loop(0, tiles + 1, stress_step, 0, unroll=True)
    else:
        lax.fori_loop(0, tiles // 2, stress_steps, 0)
        stress_step(tiles, 0)
    for copy in final:
        copy.wait()

    sent = []
    for index in range(n):
        first_entry = 3 * index
        message = made.at[index]

        def pull_rows(t, carry):
            def around(k):
                field = first_entry + k
                return (
                    st[field, t, PAD - 1 : PAD - 1 + rows, :],
                    st[field, t, PAD : PAD + rows, :],
                    st[field, t, PAD + 1 : PAD + 1 + rows, :],
                )

            above, _, below = around(0)
            p = below - above
            above, now, below = around(1)
            q = above + 4.0 * now + below
            above, now, below = around(2)
            w = above + 4.0 * now + below
            sums[0, t, 0:rows, :] = p - q
            sums[1, t, 0:rows, :] = p + q
            sums[2, t, 0:rows, :] = w
            return carry

        lax.fori_loop(0, tiles + 1, pull_rows, 0)

        def message_step(s, carry):
            us, ws = [], []
            for half in range(2):
                t = 2 * s + half
                pull = 2.0 * (sums[0, t, 0:rows, :] + sums[1, t, 0:rows, :])
                pull = pull + lower(sums, 0, t, rows, short) + higher(sums, 1, t, rows, short)
                us.append(ld[index, :, lanes(t)] + pull * (1.0 / 12.0))
                w = 4.0 * sums[2, t, 0:rows, :]
                ws.append(w + lower(sums, 2, t, rows, short) + higher(sums, 2, t, rows, short))
            uh, ul = split(jnp.concatenate(us, axis=1))
            wh, wl = split(jnp.concatenate(ws, axis=1))
            value = dot3(kbh[...], kbl[...], uh, ul, True)
            value = value + dot3(kwh[...], kwl[...], wh, wl, True)
            here = pl.ds(pl.multiple_of(s * 8, 8), 8)
            for peer in range(peers):
                for m in range(mp):
                    row = (peer * mp + m) * 8
                    message[peer, here, m * rows : (m + 1) * rows] = value[row : row + 8, :]
            return carry

        def message_pair(s, carry):
            message_step(2 * s, carry)
            return message_step(2 * s + 1, carry)

        if n == 1:
            lax.fori_loop(0, tiles // 2, message_step, 0, unroll=True)
        else:
            lax.fori_loop(0, tiles // 4, message_pair, 0)
        sent += [pltpu.make_async_copy(message, outs[index], sems.at[base + 1 + 4 * n + index])]
        sent[-1].start()
    for copy in sent:
        copy.wait()


def stencil(comps, mp, peers, modulus, displace, load, history, stiffen, halos, tables, after):
    rows, flat = stiffen.shape
    tall = rows + HALO
    wide = flat + LANES
    tiles = flat // LANES
    n = len(comps)
    block = (flat // R, mp * rows)
    return pl.pallas_call(
        functools.partial(stencil_kernel, comps, mp, peers),
        out_shape=(jax.ShapeDtypeStruct((peers,) + block, F32),) * n,
        in_specs=[SMEM] + [HBM] * 4 + [VMEM] * 6 + [HBM] * 7,
        out_specs=(HBM,) * n,
        scratch_shapes=[
            pltpu.VMEM((3, tiles + 1, PAD + tall + HALO, LANES), F32),
            pltpu.VMEM((3 * n, tall, wide), F32),
            pltpu.VMEM((tall, wide), F32),
            pltpu.VMEM((n, rows, flat), F32),
            pltpu.VMEM((3 * n, tiles + 1, PAD + tall, LANES), F32),
            pltpu.VMEM((3, tiles + 1, tall, LANES), F32),
            pltpu.VMEM((3, tiles + 1, tall, LANES), F32),
            pltpu.VMEM((n, peers) + block, F32),
            *(pltpu.VMEM(table.shape, BF) for table in tables),
            pltpu.SemaphoreType.DMA((3 * tiles + 7 + 5 * n,)),
        ],
        compiler_params=params(),
        cost_estimate=cost(13 + 8 * n),
        name="stencil",
    )(modulus, displace, load, history, stiffen, *halos, *tables, after)


def cycle_kernel(parts, ids, piece, table_ref, after, *refs):
    del after
    outs = refs[:parts]
    xh, xl, raw, table, made, sems = refs[parts:]
    peers, height, _ = piece.shape
    copies = fetch(
        [piece.at[j] for j in range(peers)] + [table_ref],
        [raw.at[j] for j in range(peers)] + [table],
        sems,
    )
    for j in range(peers):
        copies[j].wait()
        at = slice(j * height, (j + 1) * height)
        hi, lo = split(raw[j])
        xh[at, :] = hi
        xl[at, :] = lo
    copies[peers].wait()
    value = stacked3(table, xh[...], xl[...])
    block = outs[0].shape[0]
    for b in range(parts):
        made[jnp.bitwise_xor(ids[1], b)] = value[b * block : (b + 1) * block]
    sent = fetch([made.at[d] for d in range(parts)], outs, sems.at[pl.ds(peers + 1, parts)])
    for copy in sent:
        copy.wait()


def cycle_stage(ids, piece, table, parts, after):
    peers, height, width = piece.shape
    count = peers * height
    shape = jax.ShapeDtypeStruct((count // parts, width), F32)
    return pl.pallas_call(
        functools.partial(cycle_kernel, parts),
        out_shape=(shape,) * parts,
        in_specs=[SMEM] + [HBM] * 3,
        out_specs=(HBM,) * parts,
        scratch_shapes=[
            pltpu.VMEM((count, width), BF),
            pltpu.VMEM((count, width), BF),
            pltpu.VMEM((peers, height, width), F32),
            pltpu.VMEM(table.shape, BF),
            pltpu.VMEM((parts,) + shape.shape, F32),
            pltpu.SemaphoreType.DMA((peers + 1 + parts,)),
        ],
        compiler_params=params(24),
        cost_estimate=cost(0),
        name="cycle_stage",
    )(ids, piece, table, after)


def axial_kernel(slot, mp, parts, ids, radial, cyc, axial, *refs):
    ins = refs[:parts]
    table_ref = refs[parts]
    out, x, xh, xl, raw, table, made, sems = refs[-8:]
    kc, width = ins[0].shape
    rows = width // mp
    half = mp * kc
    count = parts * rows
    copies = fetch([*ins, table_ref], [raw.at[j] for j in range(parts)] + [table], sems)
    for j in range(parts):
        source = jnp.bitwise_xor(ids[1], j)
        at = pl.ds(pl.multiple_of(source * rows, rows), rows)
        copies[j].wait()
        for m in range(mp):
            hi, lo = split(raw[j, :, m * rows : (m + 1) * rows])
            x[m * kc : (m + 1) * kc, at] = hi
            x[half + m * kc : half + (m + 1) * kc, at] = lo
    copies[parts].wait()
    mine = cyc[pl.ds(pl.multiple_of(ids[1] * kc, kc), kc), :]
    base = axial[...] + mine
    value = stacked3(x, table[0:count, :], table[count:, :])
    for m in range(mp):
        part = slice(m * kc, (m + 1) * kc)
        hi, lo = split(value[part] / (base + radial[ids[0] * mp + m]))
        xh[part, :] = hi
        xl[part, :] = lo
    made[...] = stacked3(table, xh[...], xl[...], True).reshape(made.shape)
    copy = pltpu.make_async_copy(made, out.at[:, slot], sems.at[parts + 1])
    copy.start()
    copy.wait()


def axial_stage(slot, slots, ids, radial, cyc, axial, pieces, table, mp, devices, after, carried):
    parts = len(pieces)
    kc, width = pieces[0].shape
    count = width // mp * parts
    extra = [] if carried is None else [carried]
    return pl.pallas_call(
        functools.partial(axial_kernel, slot, mp, parts),
        out_shape=jax.ShapeDtypeStruct((devices, slots, count // devices, mp * kc), F32),
        in_specs=[SMEM, SMEM, VMEM, VMEM] + [HBM] * (parts + 2 + len(extra)),
        out_specs=HBM,
        scratch_shapes=[
            pltpu.VMEM((2 * mp * kc, count), BF),
            pltpu.VMEM((mp * kc, count), BF),
            pltpu.VMEM((mp * kc, count), BF),
            pltpu.VMEM((parts, kc, width), F32),
            pltpu.VMEM(table.shape, BF),
            pltpu.VMEM((devices, count // devices, mp * kc), F32),
            pltpu.SemaphoreType.DMA((parts + 2,)),
        ],
        input_output_aliases={parts + 6: 0} if extra else {},
        compiler_params=params(24),
        cost_estimate=cost(0),
        name="axial_stage",
    )(ids, radial, cyc, axial, *pieces, table, after, *extra)


def return_kernel(slot, comp, mp, parts, peers, piece, *refs):
    out, x, y, raw, table, weave, kernel, made, sems = refs[-9:]
    _, _, few, width = piece.shape
    kc = width // mp
    count = table.shape[1]
    depth, span = kernel.shape[0] // 2, kernel.shape[1]
    half = mp * peers * few
    groups = count * mp // HALF
    copies = fetch((piece.at[:, slot], *refs[:3]), (raw, table, weave, kernel), sems)
    copies[0].wait()
    for p in range(parts):
        for q in range(peers):
            for m in range(mp):
                row = (m * peers + q) * few
                hi, lo = split(raw[p * peers + q, :, m * kc : (m + 1) * kc])
                x[row : row + few, p * kc : (p + 1) * kc] = hi
                x[half + row : half + row + few, p * kc : (p + 1) * kc] = lo
    for copy in copies[1:]:
        copy.wait()
    value = split(stacked3(x, table[0:count, :], table[count:, :]))
    rows = peers * few
    front = iota((few, LANES), 1) < HALF
    for t in range(count // LANES):
        columns = slice(t * LANES, (t + 1) * LANES)
        for part, first in zip(value, (0, groups * few), strict=True):
            gathered = jnp.concatenate(
                [part[m * rows : (m + 1) * rows, columns] for m in range(mp)], axis=1
            )
            woven = dot(gathered, weave[...])
            for g in range(mp):
                block = woven[:, g * LANES : (g + 1) * LANES]
                turned = pltpu.roll(block, HALF, 1)
                row = first + 2 * (t * mp + g) * few
                for q in range(0, peers, 2):
                    one = slice(q * few, (q + 1) * few)
                    two = slice((q + 1) * few, (q + 2) * few)
                    to = slice(q * HALF, q * HALF + LANES)
                    y[row : row + few, to] = jnp.where(front, block[one], turned[two]).astype(BF)
                    y[row + few : row + 2 * few, to] = jnp.where(
                        front, turned[one], block[two]
                    ).astype(BF)
    result = stacked3(y, kernel[0:depth, :], kernel[depth:, :])
    for g in range(groups):
        made[:, g * span : (g + 1) * span] = result[g * few : (g + 1) * few, :]
    copy = pltpu.make_async_copy(made, out.at[comp], sems.at[4])
    copy.start()
    copy.wait()


def return_stage(slot, comp, piece, table, weave, back, mp, parts, carried):
    devices, _, few, width = piece.shape
    peers = devices // parts
    count = table.shape[1]
    depth, span = back.shape[0] // 2, back.shape[1]
    groups = count * mp // HALF
    extra = [] if carried is None else [carried]
    return pl.pallas_call(
        functools.partial(return_kernel, slot, comp, mp, parts, peers),
        out_shape=jax.ShapeDtypeStruct((3, few, groups * span), F32),
        in_specs=[HBM] * (4 + len(extra)),
        out_specs=HBM,
        scratch_shapes=[
            pltpu.VMEM((2 * mp * peers * few, count), BF),
            pltpu.VMEM((2 * groups * few, depth), BF),
            pltpu.VMEM((devices, few, width), F32),
            pltpu.VMEM(table.shape, BF),
            pltpu.VMEM(weave.shape, BF),
            pltpu.VMEM(back.shape, BF),
            pltpu.VMEM((few, groups * span), F32),
            pltpu.SemaphoreType.DMA((5,)),
        ],
        input_output_aliases={4: 0} if extra else {},
        compiler_params=params(32),
        cost_estimate=cost(0),
        name="return_stage",
    )(piece, table, weave, back, *extra)


def gate_kernel(block, after, out):
    del block, after, out


def gate(block, after):
    return pl.pallas_call(
        gate_kernel,
        out_shape=jax.ShapeDtypeStruct(block.shape, block.dtype),
        in_specs=[HBM, HBM],
        out_specs=HBM,
        input_output_aliases={0: 0},
        compiler_params=params(),
        cost_estimate=cost(0),
        name="gate",
    )(block, after)


def across(block, axis):
    return lax.all_to_all(block, axis, split_axis=0, concat_axis=0, tiled=True)


def swap(pieces, axis):
    count = len(pieces)
    return [pieces[0]] + [
        lax.ppermute(pieces[d], axis, [(i, i ^ d) for i in range(count)]) for d in range(1, count)
    ]


ORDER = (
    ("stencil", (0,)),
    ("forward", 0),
    ("stencil", (1, 2)),
    ("forward", 1),
    ("cycle", 0),
    ("tables", None),
    ("axial", 0),
    ("forward", 2),
    ("cycle", 1),
    ("axial", 1),
    ("backward", (0, 1)),
    ("cycle", 2),
    ("axial", 2),
    ("backward", (2,)),
    ("return", 0),
    ("return", 1),
    ("return", 2),
)


def body(
    displace,
    load,
    history,
    stiffen,
    modulus,
    radial_slope,
    radial_basis,
    axial_eig,
    cycle_eig,
    radial_eig,
):
    parts = lax.axis_size("ax")
    peers = lax.axis_size("circ")
    mp = R // peers
    rows, flat = stiffen.shape
    count_a = parts * rows
    count_c = peers * flat // R
    me = lax.axis_index("circ").astype(jnp.int32)
    pe = lax.axis_index("ax").astype(jnp.int32)
    ids = jnp.stack([me, pe])

    upward, downward, leftward, rightward = pack(displace, history, stiffen)
    ahead = [(i, i + 1) for i in range(parts - 1)]
    back_ahead = [(j, i) for i, j in ahead]
    around = [(i, (i + 1) % peers) for i in range(peers)]
    back_around = [(j, i) for i, j in around]
    bottom = lax.ppermute(upward, "ax", back_ahead)
    top = lax.ppermute(downward, "ax", ahead)
    right = lax.ppermute(leftward, "circ", back_around)
    left = lax.ppermute(rightward, "circ", around)
    front = front_tables(radial_slope, radial_basis, mp)
    to_left, to_right = corners(top, bottom, front[0])
    right_corner = lax.ppermute(to_left, "circ", back_around)
    left_corner = lax.ppermute(to_right, "circ", around)
    halos = (top, bottom, left, left_corner, right, right_corner)

    cycle_table_stack = host_split(host_cycle(count_c))
    axial_table_stack = host_split(host_axial(count_a))
    weave = host_weave(mp)
    cyc = cycle_eig[:, None]
    axial = axial_eig[None, :]

    lines = [None] * 3
    out, after, solved = None, ids, None
    for kind, i in ORDER:
        if kind == "stencil":
            blocks = stencil(
                i, mp, peers, modulus, displace, load, history, stiffen, halos, front, after
            )
            after = blocks[0]
            for comp, block in zip(i, blocks, strict=True):
                lines[comp] = block
        elif kind == "forward":
            lines[i] = across(lines[i] if i < 2 else gate(lines[i], after), "circ")
        elif kind == "tables":
            after = back = back_tables(radial_basis, mp, peers, after)
        elif kind == "cycle":
            sent = cycle_stage(ids, lines[i], cycle_table_stack, parts, after)
            after = sent[0]
            lines[i] = swap(list(sent), "ax")
        elif kind == "axial":
            slot, slots = (i, 2) if i < 2 else (0, 1)
            solved = after = axial_stage(
                slot,
                slots,
                ids,
                radial_eig,
                cyc,
                axial,
                lines[i],
                axial_table_stack,
                mp,
                parts * peers,
                after,
                solved if slot else None,
            )
        elif kind == "backward":
            block = across(solved, ("ax", "circ"))
            for slot, comp in enumerate(i):
                lines[comp] = (slot, block)
        else:
            slot, block = lines[i]
            out = return_stage(slot, i, block, cycle_table_stack, weave, back, mp, parts, out)
            after = out
    return out


def tiled(mesh):
    parts, peers = mesh.shape["ax"], mesh.shape["circ"]
    rows, flat = NA // parts, NC // peers * R
    return (
        parts & (parts - 1) == 0
        and peers & (peers - 1) == 0
        and R == 32
        and R % peers == 0
        and peers * (R // peers) * 8 == 8 * R
        and rows % LANES == 0
        and (NC // parts) % LANES == 0
        and flat % (2 * LANES) == 0
        and (NC // peers) % 16 == 0
        and (rows // peers) % 16 == 0
        and HALF % (R // peers) == 0
        and peers % 2 == 0
    )


def solution(mesh):
    return jax.shard_map(
        body if tiled(mesh) else plain_body,
        mesh=mesh,
        in_specs=(
            P(None, "ax", "circ"),
            P(None, "ax", "circ"),
            P(None, "ax", "circ"),
            P("ax", "circ"),
            P(),
            P(),
            P(),
            P(),
            P(),
            P(),
        ),
        out_specs=P(None, ("ax", "circ"), None),
        check_vma=False,
    )
```

```python
import math

import functools

import jax
import jax.numpy as jnp
import ml_dtypes
import numpy as np
from jax import lax
from jax.experimental import pallas as pl
from jax.experimental.pallas import tpu as pltpu
from jax.sharding import PartitionSpec as P

NA = 512
NC = 512
R = 32


def with_halo(block, sides, width, periodic):
    for axis, dim in sides:
        count = lax.axis_size(axis)
        forward = [(i, i + 1) for i in range(count - 1)]
        if periodic:
            forward.append((count - 1, 0))
        backward = [(target, source) for source, target in forward]
        low = lax.ppermute(
            lax.slice_in_dim(block, block.shape[dim] - width, None, axis=dim), axis, forward
        )
        high = lax.ppermute(lax.slice_in_dim(block, 0, width, axis=dim), axis, backward)
        block = jnp.concatenate([low, block, high], axis=dim)
    return block


def cycle_table(count):
    col = jnp.arange(count, dtype=jnp.int32)[:, None]
    mode = jnp.arange(count, dtype=jnp.int32)[None, :]
    half = count // 2
    folded = jnp.where(mode <= half, mode, mode - half)
    shift = jnp.where(mode <= half, 0.0, 0.5 * math.pi).astype(jnp.float32)
    scale_ends = jnp.where(
        (mode == 0) | (mode == half), math.sqrt(1.0 / count), math.sqrt(2.0 / count)
    ).astype(jnp.float32)
    phase = (col * folded % count).astype(jnp.float32) * (2.0 * math.pi / count)
    return jnp.cos(phase - shift) * scale_ends


def axial_table(rows, count):
    first = (rows + 1)[:, None]
    mode = jnp.arange(count, dtype=jnp.int32)[None, :] + 1
    phase = (first * mode % (2 * (count + 1))).astype(jnp.float32) * (math.pi / (count + 1))
    return jnp.sin(phase) * math.sqrt(2.0 / (count + 1))


def extend(field):
    rows = with_halo(field, (("ax", 1),), 1, False)
    return with_halo(rows, (("circ", 2),), R, True)


def cycle_parts(ext):
    span = ext.shape[2] - 2 * R
    left = ext[:, :, :span]
    middle = ext[:, :, R : R + span]
    right = ext[:, :, 2 * R :]
    return ((left + 4.0 * middle + right) / 6.0, (right - left) * 0.5)


def row_smooth(field):
    return (field[:, :-2] + 4.0 * field[:, 1:-1] + field[:, 2:]) / 6.0


def row_slope(field):
    return (field[:, 2:] - field[:, :-2]) * 0.5


def radial_mix(field, matrix, form):
    count, rows, flat = field.shape
    cube = field.reshape(count, rows, flat // R, R)
    mixed = jnp.einsum(form, cube, matrix, precision=lax.Precision.HIGHEST)
    return mixed.reshape(count, rows, flat)


def into_cycles(field):
    return lax.all_to_all(field, "circ", split_axis=1, concat_axis=2, tiled=True)


def cycle_forward(field, table, basis):
    count, rows, flat = field.shape
    cube = field.reshape(count * rows, NC, R)
    cube = jnp.einsum("bcr,ck->bkr", cube, table, precision=lax.Precision.HIGHEST)
    cube = jnp.einsum("bkr,rm->bkm", cube, basis, precision=lax.Precision.HIGHEST)
    return cube.reshape(count, rows, flat)


def cycle_inverse(field, table, basis):
    count, rows, flat = field.shape
    cube = field.reshape(count * rows, NC, R)
    cube = jnp.einsum("bkm,rm->bkr", cube, basis, precision=lax.Precision.HIGHEST)
    cube = jnp.einsum("bkr,ck->bcr", cube, table, precision=lax.Precision.HIGHEST)
    return cube.reshape(count, rows, flat)


def axial_solve(lines, forward_table, inverse_table, weights):
    modes = jnp.einsum("pk,cps->cks", forward_table, lines, precision=lax.Precision.HIGHEST)
    return jnp.einsum(
        "ak,cks->cas", inverse_table, modes * weights[None], precision=lax.Precision.HIGHEST
    )


def plain_body(
    displace,
    load,
    history,
    stiffen,
    modulus,
    radial_slope,
    radial_basis,
    axial_eig,
    cycle_eig,
    radial_eig,
):
    ext = extend(displace)
    cycle_v, cycle_d = cycle_parts(ext)
    smooth_v = row_smooth(cycle_v)
    radial_part = radial_mix(smooth_v, radial_slope, "iacq,rq->iacr")
    grads = jnp.concatenate([row_slope(cycle_v), row_smooth(cycle_d), radial_part], axis=0)
    mixed = jnp.einsum("mn,nac->mac", modulus, grads, precision=lax.Precision.HIGHEST)
    stress = (1.0 + stiffen)[None] * mixed + history
    ext_stress = extend(stress)
    first_v, unused_d = cycle_parts(ext_stress[0:3])
    unused_v, second_d = cycle_parts(ext_stress[3:6])
    third_v, unused_e = cycle_parts(ext_stress[6:9])
    third = radial_mix(row_smooth(third_v), radial_slope, "iacr,rq->iacq")
    pull = -row_slope(first_v) - row_smooth(second_d) + third
    resid = load - pull
    a_dev = displace.shape[1]
    flat_dev = displace.shape[2]
    n_ax = lax.axis_size("ax")
    n_circ = lax.axis_size("circ")
    piece = flat_dev // n_ax
    rows_cycle = a_dev // n_circ
    table_cycle = cycle_table(NC)
    spec = cycle_forward(into_cycles(resid), table_cycle, radial_basis)
    start = lax.axis_index("circ") * flat_dev + lax.axis_index("ax") * piece
    index_flat = start + jnp.arange(piece, dtype=jnp.int32)
    denom = (
        axial_eig[:, None]
        + jnp.take(cycle_eig, index_flat // R)[None, :]
        + jnp.take(radial_eig, index_flat % R)[None, :]
    )
    weights = 1.0 / denom
    natural_rows = jnp.arange(NA, dtype=jnp.int32)
    inverse_table = axial_table(natural_rows, NA)
    cube = spec.reshape(3, rows_cycle, n_circ, flat_dev)
    lines = lax.all_to_all(
        lax.all_to_all(cube, "ax", split_axis=3, concat_axis=1, tiled=True),
        "circ",
        split_axis=2,
        concat_axis=1,
        tiled=True,
    ).reshape(3, NA, piece)
    group = n_ax * rows_cycle
    outer = natural_rows // group
    inner = natural_rows % group
    source_rows = inner // rows_cycle * a_dev + outer * rows_cycle + inner % rows_cycle
    forward_table = axial_table(source_rows, NA)
    solved = axial_solve(lines, forward_table, inverse_table, weights)
    cycles_back = lax.all_to_all(
        lax.all_to_all(solved, "ax", split_axis=1, concat_axis=2, tiled=True),
        "circ",
        split_axis=1,
        concat_axis=2,
        tiled=True,
    )
    return cycle_inverse(cycles_back, table_cycle, radial_basis)


BF = jnp.bfloat16
F32 = jnp.float32
VMEM = pl.BlockSpec(memory_space=pltpu.VMEM)
SMEM = pl.BlockSpec(memory_space=pltpu.SMEM)
HBM = pl.BlockSpec(memory_space=pltpu.HBM)
HALO = 8
PAD = 8
HALF = 64
LANES = 128


def params(mebibytes=60):
    return pltpu.CompilerParams(vmem_limit_bytes=mebibytes << 20)


def cost(microseconds):
    return pl.CostEstimate(flops=1, bytes_accessed=int(microseconds * 3.6e6) + 1, transcendentals=0)


def split(x):
    hi = x.astype(BF)
    return hi, (x - hi.astype(F32)).astype(BF)


def dot(a, b, transposed=False):
    dims = (((1,), (1 if transposed else 0,)), ((), ()))
    return lax.dot_general(a, b, dims, preferred_element_type=F32)


def dot3(ah, al, bh, bl, transposed=False):
    return dot(ah, bh, transposed) + (dot(ah, bl, transposed) + dot(al, bh, transposed))


def stacked3(both, bh, bl, transposed=False):
    rows = both.shape[0] // 2
    upper = dot(both[...], bh, transposed)
    return upper[:rows] + (upper[rows:] + dot(both[0:rows, :], bl, transposed))


def exact(a, b, transposed=False):
    dims = (((1,), (1 if transposed else 0,)), ((), ()))
    return lax.dot_general(
        a, b, dims, precision=lax.Precision.HIGHEST, preferred_element_type=F32
    )


def host_split(table):
    hi = table.astype(np.float32).astype(ml_dtypes.bfloat16)
    lo = (table - hi.astype(np.float64)).astype(np.float32).astype(ml_dtypes.bfloat16)
    return jnp.asarray(np.concatenate([hi, lo], axis=0))


def host_cycle(count):
    col = np.arange(count)[None, :]
    mode = np.arange(count)[:, None]
    half = count // 2
    folded = np.where(mode <= half, mode, mode - half)
    phase = 2.0 * np.pi * ((col * folded) % count) / count
    scale = np.where((mode == 0) | (mode == half), math.sqrt(1.0 / count), math.sqrt(2.0 / count))
    return np.where(mode <= half, np.cos(phase), np.sin(phase)) * scale


def host_axial(count):
    first = np.arange(1, count + 1)
    phase = np.pi * (np.outer(first, first) % (2 * (count + 1))) / (count + 1)
    return np.sin(phase) * math.sqrt(2.0 / (count + 1))


def host_weave(mp):
    table = np.zeros((mp * LANES, mp * LANES), np.float32)
    for m in range(mp):
        for c in range(LANES):
            table[m * LANES + c, c * mp + m] = 1.0
    return jnp.asarray(table.astype(ml_dtypes.bfloat16))


def iota(shape, dim):
    return lax.broadcasted_iota(jnp.int32, shape, dim)


def onehot(condition):
    return jnp.where(condition, 1.0, 0.0).astype(F32)


def write_split(hi_ref, lo_ref, value):
    hi, lo = split(value)
    hi_ref[...] = hi
    lo_ref[...] = lo


def fetch(sources, targets, sems):
    copies = [
        pltpu.make_async_copy(source, target, sems.at[k])
        for k, (source, target) in enumerate(zip(sources, targets, strict=True))
    ]
    for copy in copies:
        copy.start()
    return copies


def write_stack(ref, value):
    rows = value.shape[0]
    hi, lo = split(value)
    ref[0:rows, :] = hi
    ref[rows:, :] = lo


def fetch(sources, targets, sems):
    copies = [
        pltpu.make_async_copy(source, target, sems.at[k])
        for k, (source, target) in enumerate(zip(sources, targets, strict=True))
    ]
    for copy in copies:
        copy.start()
    return copies


def front_tables_kernel(mp, slope_ref, basis_ref, *refs):
    outs, made, sems = refs[:6], refs[6:12], refs[12]
    krh, krl, kbh, kbl, kwh, kwl = made
    slope = slope_ref[...]
    basis = basis_ref[...]
    side = LANES
    row = iota((side, R), 0)
    col = iota((side, R), 1)
    pick = onehot(row % R == col)
    mask = iota((side, side), 0) // R == iota((side, side), 1) // R
    value = exact(exact(pick, slope, True), pick, True)
    write_split(krh, krl, jnp.where(mask, value * (1.0 / 36.0), 0.0))
    side = 8 * R
    row = iota((side, R), 0)
    col = iota((side, R), 1)
    pick = onehot(row % R == col)
    block = mp * 8
    mode = onehot(row // block * mp + (row % block) // 8 == col)
    mask = iota((side, side), 0) % 8 == iota((side, side), 1) // R
    value = exact(exact(mode, basis, True), pick, True)
    write_split(kbh, kbl, jnp.where(mask, value, 0.0))
    both = exact(slope, basis)
    value = exact(exact(mode, both, True), pick, True)
    write_split(kwh, kwl, jnp.where(mask, value * (-1.0 / 36.0), 0.0))
    for copy in fetch(made, outs, sems):
        copy.wait()


def front_tables(slope, basis, mp):
    one = jax.ShapeDtypeStruct((LANES, LANES), BF)
    two = jax.ShapeDtypeStruct((8 * R, 8 * R), BF)
    return pl.pallas_call(
        functools.partial(front_tables_kernel, mp),
        out_shape=(one, one, two, two, two, two),
        in_specs=[VMEM, VMEM],
        out_specs=(HBM,) * 6,
        scratch_shapes=[pltpu.VMEM(x.shape, BF) for x in (one, one, two, two, two, two)]
        + [pltpu.SemaphoreType.DMA((6,))],
        compiler_params=params(),
        name="front_tables",
    )(slope, basis)


def back_tables_kernel(mp, basis_ref, after, out, made, sem):
    del after
    rows, cols = made.shape[0] // 2, made.shape[1]
    row = iota((rows, R), 0)
    col = iota((rows, R), 1)
    mode = onehot(row // HALF * mp + row % mp == col)
    pick = onehot(iota((cols, R), 0) % R == iota((cols, R), 1))
    value = exact(exact(mode, basis_ref[...], True), pick, True)
    mask = (iota((rows, cols), 0) % HALF) // mp == iota((rows, cols), 1) // R
    write_stack(made, jnp.where(mask, value, 0.0))
    copy = pltpu.make_async_copy(made, out, sem)
    copy.start()
    copy.wait()


def back_tables(basis, mp, peers, after):
    shape = jax.ShapeDtypeStruct((2 * peers * HALF, HALF // mp * R), BF)
    return pl.pallas_call(
        functools.partial(back_tables_kernel, mp),
        out_shape=shape,
        in_specs=[VMEM, HBM],
        out_specs=HBM,
        scratch_shapes=[pltpu.VMEM(shape.shape, BF), pltpu.SemaphoreType.DMA],
        compiler_params=params(24),
        name="back_tables",
    )(basis, after)


def pack_columns(out, lane, wide, slim, pieces):
    for tile in range(4):
        value = None
        for index, piece in enumerate(pieces):
            at = 64 * index if index < 3 else 96 + 32 * index
            if at // LANES == tile:
                shift = (at - (wide if index < 3 else slim)) % LANES
                moved = pltpu.roll(piece, shift, 1) if shift else piece
                value = moved if value is None else jnp.where(lane >= at % LANES, moved, value)
        out[:, tile * LANES : (tile + 1) * LANES] = value


def pack_kernel(
    displace, history, stiffen, up_ref, down_ref, left_ref, right_ref, d, h, s, dc, hc, sc, sems
):
    rows, flat = stiffen.shape
    sources, targets = [], []
    for k, at in enumerate((slice(0, 8), slice(rows - 8, rows))):
        sources += [displace.at[:, at, :], history.at[:, at, :], stiffen.at[at, :]]
        targets += [d.at[k], h.at[k], s.at[k]]
    for k, at in enumerate((slice(0, LANES), slice(flat - LANES, flat))):
        sources += [displace.at[:, :, at], history.at[:, :, at], stiffen.at[:, at]]
        targets += [dc.at[k], hc.at[k], sc.at[k]]
    copies = fetch(sources, targets, sems)
    for copy in copies[:6]:
        copy.wait()
    for k, first, last, out in ((0, 0, 0, up_ref), (1, 6, 7, down_ref)):
        for i in range(3):
            out[2 * i : 2 * i + 2, :] = d[k, i, first : first + 2, :]
        for n in range(9):
            out[6 + n : 7 + n, :] = h[k, n, last : last + 1, :]
        out[15:16, :] = 1.0 + s[k, last : last + 1, :]
    for copy in copies[6:]:
        copy.wait()
    lane = iota((rows, LANES), 1)
    for k, out, wide, slim in ((0, left_ref, 0, 0), (1, right_ref, LANES - 2 * R, LANES - R)):
        pieces = [dc[k, i] for i in range(3)] + [hc[k, n] for n in range(9)] + [1.0 + sc[k]]
        pack_columns(out, lane, wide, slim, pieces)


def pack(displace, history, stiffen):
    rows, flat = stiffen.shape
    row = jax.ShapeDtypeStruct((16, flat), F32)
    column = jax.ShapeDtypeStruct((rows, 4 * LANES), F32)
    return pl.pallas_call(
        pack_kernel,
        out_shape=(row, row, column, column),
        in_specs=[HBM] * 3,
        out_specs=(VMEM,) * 4,
        scratch_shapes=[
            pltpu.VMEM((2, 3, 8, flat), F32),
            pltpu.VMEM((2, 9, 8, flat), F32),
            pltpu.VMEM((2, 8, flat), F32),
            pltpu.VMEM((2, 3, rows, LANES), F32),
            pltpu.VMEM((2, 9, rows, LANES), F32),
            pltpu.VMEM((2, rows, LANES), F32),
            pltpu.SemaphoreType.DMA((12,)),
        ],
        compiler_params=params(60),
        cost_estimate=cost(0),
        name="pack",
    )(displace, history, stiffen)


def corners_kernel(top, bottom, after, left_ref, right_ref, tall):
    del after
    flat = top.shape[1]
    lane = iota((HALO, LANES), 1)
    tall[...] = jnp.zeros_like(tall)
    for out, at, wide, slim in (
        (left_ref, slice(0, LANES), 0, 0),
        (right_ref, slice(flat - LANES, flat), LANES - 2 * R, LANES - R),
    ):
        pieces = []
        for index in range(13):
            first, count = (2 * index, 2) if index < 3 else (3 + index, 1)
            tall[index, 0:count, :] = bottom[first : first + count, at]
            tall[index, HALO - count : HALO, :] = top[first : first + count, at]
            pieces.append(tall[index])
        pack_columns(out, lane, wide, slim, pieces)


def corners(top, bottom, after):
    shape = jax.ShapeDtypeStruct((HALO, 4 * LANES), F32)
    return pl.pallas_call(
        corners_kernel,
        out_shape=(shape, shape),
        in_specs=[VMEM] * 2 + [HBM],
        out_specs=(VMEM, VMEM),
        scratch_shapes=[pltpu.VMEM((13, HALO, LANES), F32)],
        compiler_params=params(),
        cost_estimate=cost(0),
        name="corners",
    )(top, bottom, after)


def stencil_kernel(
    comps,
    mp,
    peers,
    modulus,
    displace,
    load,
    history,
    stiffen,
    top,
    bottom,
    left,
    left_corner,
    right,
    right_corner,
    *rest,
):
    n = len(comps)
    outs = rest[7 : 7 + n]
    xd, hx, sx, ld, st, sums, diffs, made, krh, krl, kbh, kbl, kwh, kwl, sems = rest[7 + n :]
    rows, flat = stiffen.shape
    tall = rows + HALO
    tiles = flat // LANES
    entries = [comp + 3 * k for comp in comps for k in range(3)]
    center = (slice(0, rows), slice(0, flat))

    def displace_copy(i, t):
        return pltpu.make_async_copy(
            displace.at[i, :, t * LANES : (t + 1) * LANES],
            xd.at[i, t, PAD : PAD + rows, :],
            sems.at[i * tiles + t],
        )

    moves = [displace_copy(i, t) for t in range(tiles) for i in range(3)]
    base = 3 * tiles
    late = [pltpu.make_async_copy(stiffen, sx.at[center], sems.at[base])]
    late += [
        pltpu.make_async_copy(history.at[m], hx.at[(k,) + center], sems.at[base + 1 + k])
        for k, m in enumerate(entries)
    ]
    final = [
        pltpu.make_async_copy(load.at[comp], ld.at[k], sems.at[base + 1 + 3 * n + k])
        for k, comp in enumerate(comps)
    ]
    tables = [
        pltpu.make_async_copy(source, target, sems.at[base + 1 + 5 * n + k])
        for k, (source, target) in enumerate(
            zip(rest[:6], (krh, krl, kbh, kbl, kwh, kwl), strict=True)
        )
    ]
    late += tables[:2]
    final += tables[2:]
    for copy in moves + late + final:
        copy.start()
    left = (left, left_corner)
    right = (right, right_corner)
    lane = iota((tall, LANES), 1)
    short = iota((rows, LANES), 1)

    def tile_of(refs, at, target):
        part = slice(at // LANES * LANES, (at // LANES + 1) * LANES)
        value = jnp.concatenate([ref[:, part] for ref in refs], axis=0)
        shift = (target - at) % LANES
        return pltpu.roll(value, shift, 1) if shift else value

    for i in range(3):
        tile = jnp.where(lane < 64, tile_of(right, 64 * i, 0), tile_of(left, 64 * i, 64))
        xd[i, tiles, PAD : PAD + tall, :] = tile
        xd[i, tiles, PAD - 1 : PAD, :] = tile[tall - 1 : tall]
        xd[i, tiles, PAD + tall : PAD + tall + 1, :] = tile[0:1]
        for t in range(tiles):
            part = slice(t * LANES, (t + 1) * LANES)
            above = top[2 * i : 2 * i + 2, part]
            xd[i, t, PAD + rows : PAD + rows + 2, :] = bottom[2 * i : 2 * i + 2, part]
            xd[i, t, PAD + tall - 2 : PAD + tall, :] = above
            xd[i, t, PAD - 1 : PAD, :] = above[1:2]
    zeros = jnp.zeros((HALO, flat), F32)
    for k, m in enumerate(entries):
        at = 192 + 32 * m
        hx[k, rows:tall, 0:flat] = zeros
        hx[k, rows : rows + 1, 0:flat] = bottom[6 + m : 7 + m, :]
        hx[k, tall - 1 : tall, 0:flat] = top[6 + m : 7 + m, :]
        hx[k, :, flat:] = jnp.where(lane < 64, tile_of(right, at, 0), tile_of(left, at, 96))
    sx[rows:tall, 0:flat] = zeros
    sx[rows : rows + 1, 0:flat] = bottom[15:16, :] - 1.0
    sx[tall - 1 : tall, 0:flat] = top[15:16, :] - 1.0
    sx[:, flat:] = jnp.where(lane < 64, tile_of(right, 480, 0), tile_of(left, 480, 96)) - 1.0

    def lanes(t):
        return pl.ds(pl.multiple_of(t * LANES, LANES), LANES)

    def previous(t):
        return lax.rem(t + tiles, tiles + 1)

    def following(t):
        return lax.rem(t + 1, tiles + 1)

    def lower(ref, k, t, height, mask):
        mixed = jnp.where(
            mask >= LANES - R, ref[k, previous(t), 0:height, :], ref[k, t, 0:height, :]
        )
        return pltpu.roll(mixed, R, 1)

    def higher(ref, k, t, height, mask):
        mixed = jnp.where(mask < R, ref[k, following(t), 0:height, :], ref[k, t, 0:height, :])
        return pltpu.roll(mixed, LANES - R, 1)

    for copy in moves:
        copy.wait()

    def rows_step(t, carry):
        for i in range(3):
            xd[i, t, PAD + tall : PAD + tall + 1, :] = xd[i, t, PAD : PAD + 1, :]
            above = xd[i, t, PAD - 1 : PAD - 1 + tall, :]
            below = xd[i, t, PAD + 1 : PAD + 1 + tall, :]
            total = above + 4.0 * xd[i, t, PAD : PAD + tall, :] + below
            change = below - above
            sums[i, t] = total
            diffs[i, t] = change
        return carry

    lax.fori_loop(0, tiles + 1, rows_step, 0)
    for copy in late:
        copy.wait()

    def stress_step(t, carry):
        total = [None] * len(entries)
        for i in range(3):
            low = lower(sums, i, t, tall, lane)
            high = higher(sums, i, t, tall, lane)
            second = high - low
            both = low + high + 4.0 * sums[i, t]
            low = lower(diffs, i, t, tall, lane)
            high = higher(diffs, i, t, tall, lane)
            first = low + high + 4.0 * diffs[i, t]
            bh, bl = split(both)
            third = dot3(bh, bl, krh[...], krl[...])
            for k, m in enumerate(entries):
                part = (
                    (modulus[m, i] * (1.0 / 12.0)) * first
                    + (modulus[m, 3 + i] * (1.0 / 12.0)) * second
                    + modulus[m, 6 + i] * third
                )
                total[k] = part if total[k] is None else total[k] + part
        factor = 1.0 + sx[:, lanes(t)]
        for k in range(len(entries)):
            value = factor * total[k] + hx[k, :, lanes(t)]
            st[k, t, PAD : PAD + tall, :] = value
            st[k, t, PAD - 1 : PAD, :] = value[tall - 1 : tall]
        return carry

    def stress_steps(s, carry):
        stress_step(2 * s + 0, carry)
        stress_step(2 * s + 1, carry)
        return carry

    if n == 1:
        lax.fori_loop(0, tiles + 1, stress_step, 0, unroll=True)
    else:
        lax.fori_loop(0, tiles // 2, stress_steps, 0)
        stress_step(tiles, 0)
    for copy in final:
        copy.wait()

    sent = []
    for index in range(n):
        first_entry = 3 * index
        message = made.at[index]

        def pull_rows(t, carry):
            def around(k):
                field = first_entry + k
                return (
                    st[field, t, PAD - 1 : PAD - 1 + rows, :],
                    st[field, t, PAD : PAD + rows, :],
                    st[field, t, PAD + 1 : PAD + 1 + rows, :],
                )

            above, _, below = around(0)
            p = below - above
            above, now, below = around(1)
            q = above + 4.0 * now + below
            above, now, below = around(2)
            w = above + 4.0 * now + below
            sums[0, t, 0:rows, :] = p - q
            sums[1, t, 0:rows, :] = p + q
            sums[2, t, 0:rows, :] = w
            return carry

        lax.fori_loop(0, tiles + 1, pull_rows, 0)

        def message_step(s, carry):
            us, ws = [], []
            for half in range(2):
                t = 2 * s + half
                pull = 2.0 * (sums[0, t, 0:rows, :] + sums[1, t, 0:rows, :])
                pull = pull + lower(sums, 0, t, rows, short) + higher(sums, 1, t, rows, short)
                us.append(ld[index, :, lanes(t)] + pull * (1.0 / 12.0))
                w = 4.0 * sums[2, t, 0:rows, :]
                ws.append(w + lower(sums, 2, t, rows, short) + higher(sums, 2, t, rows, short))
            uh, ul = split(jnp.concatenate(us, axis=1))
            wh, wl = split(jnp.concatenate(ws, axis=1))
            value = dot3(kbh[...], kbl[...], uh, ul, True)
            value = value + dot3(kwh[...], kwl[...], wh, wl, True)
            here = pl.ds(pl.multiple_of(s * 8, 8), 8)
            for peer in range(peers):
                for m in range(mp):
                    row = (peer * mp + m) * 8
                    message[peer, here, m * rows : (m + 1) * rows] = value[row : row + 8, :]
            return carry

        def message_pair(s, carry):
            message_step(2 * s, carry)
            return message_step(2 * s + 1, carry)

        if n == 1:
            lax.fori_loop(0, tiles // 2, message_step, 0, unroll=True)
        else:
            lax.fori_loop(0, tiles // 4, message_pair, 0)
        sent += [pltpu.make_async_copy(message, outs[index], sems.at[base + 1 + 4 * n + index])]
        sent[-1].start()
    for copy in sent:
        copy.wait()


def stencil(comps, mp, peers, modulus, displace, load, history, stiffen, halos, tables, after):
    rows, flat = stiffen.shape
    tall = rows + HALO
    wide = flat + LANES
    tiles = flat // LANES
    n = len(comps)
    block = (flat // R, mp * rows)
    return pl.pallas_call(
        functools.partial(stencil_kernel, comps, mp, peers),
        out_shape=(jax.ShapeDtypeStruct((peers,) + block, F32),) * n,
        in_specs=[SMEM] + [HBM] * 4 + [VMEM] * 6 + [HBM] * 7,
        out_specs=(HBM,) * n,
        scratch_shapes=[
            pltpu.VMEM((3, tiles + 1, PAD + tall + HALO, LANES), F32),
            pltpu.VMEM((3 * n, tall, wide), F32),
            pltpu.VMEM((tall, wide), F32),
            pltpu.VMEM((n, rows, flat), F32),
            pltpu.VMEM((3 * n, tiles + 1, PAD + tall, LANES), F32),
            pltpu.VMEM((3, tiles + 1, tall, LANES), F32),
            pltpu.VMEM((3, tiles + 1, tall, LANES), F32),
            pltpu.VMEM((n, peers) + block, F32),
            *(pltpu.VMEM(table.shape, BF) for table in tables),
            pltpu.SemaphoreType.DMA((3 * tiles + 7 + 5 * n,)),
        ],
        compiler_params=params(),
        cost_estimate=cost(13 + 8 * n),
        name="stencil",
    )(modulus, displace, load, history, stiffen, *halos, *tables, after)


def cycle_kernel(parts, ids, piece, table_ref, after, *refs):
    del after
    outs = refs[:parts]
    xh, xl, raw, table, made, sems = refs[parts:]
    peers, height, _ = piece.shape
    copies = fetch(
        [piece.at[j] for j in range(peers)] + [table_ref],
        [raw.at[j] for j in range(peers)] + [table],
        sems,
    )
    for j in range(peers):
        copies[j].wait()
        at = slice(j * height, (j + 1) * height)
        hi, lo = split(raw[j])
        xh[at, :] = hi
        xl[at, :] = lo
    copies[peers].wait()
    value = stacked3(table, xh[...], xl[...])
    block = outs[0].shape[0]
    for b in range(parts):
        made[jnp.bitwise_xor(ids[1], b)] = value[b * block : (b + 1) * block]
    sent = fetch([made.at[d] for d in range(parts)], outs, sems.at[pl.ds(peers + 1, parts)])
    for copy in sent:
        copy.wait()


def cycle_stage(ids, piece, table, parts, after):
    peers, height, width = piece.shape
    count = peers * height
    shape = jax.ShapeDtypeStruct((count // parts, width), F32)
    return pl.pallas_call(
        functools.partial(cycle_kernel, parts),
        out_shape=(shape,) * parts,
        in_specs=[SMEM] + [HBM] * 3,
        out_specs=(HBM,) * parts,
        scratch_shapes=[
            pltpu.VMEM((count, width), BF),
            pltpu.VMEM((count, width), BF),
            pltpu.VMEM((peers, height, width), F32),
            pltpu.VMEM(table.shape, BF),
            pltpu.VMEM((parts,) + shape.shape, F32),
            pltpu.SemaphoreType.DMA((peers + 1 + parts,)),
        ],
        compiler_params=params(24),
        cost_estimate=cost(0),
        name="cycle_stage",
    )(ids, piece, table, after)


def axial_kernel(slot, mp, parts, ids, radial, cyc, axial, *refs):
    ins = refs[:parts]
    table_ref = refs[parts]
    out, x, xh, xl, raw, table, made, sems = refs[-8:]
    kc, width = ins[0].shape
    rows = width // mp
    half = mp * kc
    count = parts * rows
    copies = fetch([*ins, table_ref], [raw.at[j] for j in range(parts)] + [table], sems)
    for j in range(parts):
        source = jnp.bitwise_xor(ids[1], j)
        at = pl.ds(pl.multiple_of(source * rows, rows), rows)
        copies[j].wait()
        for m in range(mp):
            hi, lo = split(raw[j, :, m * rows : (m + 1) * rows])
            x[m * kc : (m + 1) * kc, at] = hi
            x[half + m * kc : half + (m + 1) * kc, at] = lo
    copies[parts].wait()
    mine = cyc[pl.ds(pl.multiple_of(ids[1] * kc, kc), kc), :]
    base = axial[...] + mine
    value = stacked3(x, table[0:count, :], table[count:, :])
    for m in range(mp):
        part = slice(m * kc, (m + 1) * kc)
        hi, lo = split(value[part] / (base + radial[ids[0] * mp + m]))
        xh[part, :] = hi
        xl[part, :] = lo
    made[...] = stacked3(table, xh[...], xl[...], True).reshape(made.shape)
    copy = pltpu.make_async_copy(made, out.at[:, slot], sems.at[parts + 1])
    copy.start()
    copy.wait()


def axial_stage(slot, slots, ids, radial, cyc, axial, pieces, table, mp, devices, after, carried):
    parts = len(pieces)
    kc, width = pieces[0].shape
    count = width // mp * parts
    extra = [] if carried is None else [carried]
    return pl.pallas_call(
        functools.partial(axial_kernel, slot, mp, parts),
        out_shape=jax.ShapeDtypeStruct((devices, slots, count // devices, mp * kc), F32),
        in_specs=[SMEM, SMEM, VMEM, VMEM] + [HBM] * (parts + 2 + len(extra)),
        out_specs=HBM,
        scratch_shapes=[
            pltpu.VMEM((2 * mp * kc, count), BF),
            pltpu.VMEM((mp * kc, count), BF),
            pltpu.VMEM((mp * kc, count), BF),
            pltpu.VMEM((parts, kc, width), F32),
            pltpu.VMEM(table.shape, BF),
            pltpu.VMEM((devices, count // devices, mp * kc), F32),
            pltpu.SemaphoreType.DMA((parts + 2,)),
        ],
        input_output_aliases={parts + 6: 0} if extra else {},
        compiler_params=params(24),
        cost_estimate=cost(0),
        name="axial_stage",
    )(ids, radial, cyc, axial, *pieces, table, after, *extra)


def return_kernel(slot, comp, mp, parts, peers, piece, *refs):
    out, x, y, raw, table, weave, kernel, made, sems = refs[-9:]
    _, _, few, width = piece.shape
    kc = width // mp
    count = table.shape[1]
    depth, span = kernel.shape[0] // 2, kernel.shape[1]
    half = mp * peers * few
    groups = count * mp // HALF
    copies = fetch((piece.at[:, slot], *refs[:3]), (raw, table, weave, kernel), sems)
    copies[0].wait()
    for p in range(parts):
        for q in range(peers):
            for m in range(mp):
                row = (m * peers + q) * few
                hi, lo = split(raw[p * peers + q, :, m * kc : (m + 1) * kc])
                x[row : row + few, p * kc : (p + 1) * kc] = hi
                x[half + row : half + row + few, p * kc : (p + 1) * kc] = lo
    for copy in copies[1:]:
        copy.wait()
    value = split(stacked3(x, table[0:count, :], table[count:, :]))
    rows = peers * few
    front = iota((few, LANES), 1) < HALF
    for t in range(count // LANES):
        columns = slice(t * LANES, (t + 1) * LANES)
        for part, first in zip(value, (0, groups * few), strict=True):
            gathered = jnp.concatenate(
                [part[m * rows : (m + 1) * rows, columns] for m in range(mp)], axis=1
            )
            woven = dot(gathered, weave[...])
            for g in range(mp):
                block = woven[:, g * LANES : (g + 1) * LANES]
                turned = pltpu.roll(block, HALF, 1)
                row = first + 2 * (t * mp + g) * few
                for q in range(0, peers, 2):
                    one = slice(q * few, (q + 1) * few)
                    two = slice((q + 1) * few, (q + 2) * few)
                    to = slice(q * HALF, q * HALF + LANES)
                    y[row : row + few, to] = jnp.where(front, block[one], turned[two]).astype(BF)
                    y[row + few : row + 2 * few, to] = jnp.where(
                        front, turned[one], block[two]
                    ).astype(BF)
    result = stacked3(y, kernel[0:depth, :], kernel[depth:, :])
    for g in range(groups):
        made[:, g * span : (g + 1) * span] = result[g * few : (g + 1) * few, :]
    copy = pltpu.make_async_copy(made, out.at[comp], sems.at[4])
    copy.start()
    copy.wait()


def return_stage(slot, comp, piece, table, weave, back, mp, parts, carried):
    devices, _, few, width = piece.shape
    peers = devices // parts
    count = table.shape[1]
    depth, span = back.shape[0] // 2, back.shape[1]
    groups = count * mp // HALF
    extra = [] if carried is None else [carried]
    return pl.pallas_call(
        functools.partial(return_kernel, slot, comp, mp, parts, peers),
        out_shape=jax.ShapeDtypeStruct((3, few, groups * span), F32),
        in_specs=[HBM] * (4 + len(extra)),
        out_specs=HBM,
        scratch_shapes=[
            pltpu.VMEM((2 * mp * peers * few, count), BF),
            pltpu.VMEM((2 * groups * few, depth), BF),
            pltpu.VMEM((devices, few, width), F32),
            pltpu.VMEM(table.shape, BF),
            pltpu.VMEM(weave.shape, BF),
            pltpu.VMEM(back.shape, BF),
            pltpu.VMEM((few, groups * span), F32),
            pltpu.SemaphoreType.DMA((5,)),
        ],
        input_output_aliases={4: 0} if extra else {},
        compiler_params=params(32),
        cost_estimate=cost(0),
        name="return_stage",
    )(piece, table, weave, back, *extra)


def gate_kernel(*refs):
    del refs


def gate(block, *after):
    return pl.pallas_call(
        gate_kernel,
        out_shape=jax.ShapeDtypeStruct(block.shape, block.dtype),
        in_specs=[HBM] * (1 + len(after)),
        out_specs=HBM,
        input_output_aliases={0: 0},
        compiler_params=params(16),
        cost_estimate=cost(0),
        name="gate",
    )(block, *after)


def across(block, axis):
    return lax.all_to_all(block, axis, split_axis=0, concat_axis=0, tiled=True)


def swap(pieces, axis):
    count = len(pieces)
    return [pieces[0]] + [
        lax.ppermute(pieces[d], axis, [(i, i ^ d) for i in range(count)]) for d in range(1, count)
    ]


ORDER = (
    ("stencil", (0,)),
    ("forward", 0),
    ("stencil", (1, 2)),
    ("forward", 1),
    ("cycle", 0),
    ("tables", None),
    ("forward", 2),
    ("axial", 0),
    ("cycle", 1),
    ("axial", 1),
    ("backward", (0, 1)),
    ("cycle", 2),
    ("axial", 2),
    ("backward", (2,)),
    ("return", 0),
    ("return", 1),
    ("return", 2),
)


def body(
    displace,
    load,
    history,
    stiffen,
    modulus,
    radial_slope,
    radial_basis,
    axial_eig,
    cycle_eig,
    radial_eig,
):
    parts = lax.axis_size("ax")
    peers = lax.axis_size("circ")
    mp = R // peers
    rows, flat = stiffen.shape
    count_a = parts * rows
    count_c = peers * flat // R
    me = lax.axis_index("circ").astype(jnp.int32)
    pe = lax.axis_index("ax").astype(jnp.int32)
    ids = jnp.stack([me, pe])

    upward, downward, leftward, rightward = pack(displace, history, stiffen)
    ahead = [(i, i + 1) for i in range(parts - 1)]
    back_ahead = [(j, i) for i, j in ahead]
    around = [(i, (i + 1) % peers) for i in range(peers)]
    back_around = [(j, i) for i, j in around]
    bottom = lax.ppermute(upward, "ax", back_ahead)
    top = lax.ppermute(downward, "ax", ahead)
    right = lax.ppermute(leftward, "circ", back_around)
    left = lax.ppermute(rightward, "circ", around)
    front = front_tables(radial_slope, radial_basis, mp)
    to_left, to_right = corners(top, bottom, front[0])
    right_corner = lax.ppermute(to_left, "circ", back_around)
    left_corner = lax.ppermute(to_right, "circ", around)
    halos = (top, bottom, left, left_corner, right, right_corner)

    cycle_table_stack = host_split(host_cycle(count_c))
    axial_table_stack = host_split(host_axial(count_a))
    weave = host_weave(mp)
    cyc = cycle_eig[:, None]
    axial = axial_eig[None, :]

    lines = [None] * 3
    out, after, solved = None, ids, None
    for kind, i in ORDER:
        if kind == "stencil":
            blocks = stencil(
                i, mp, peers, modulus, displace, load, history, stiffen, halos, front, after
            )
            after = blocks[0]
            for comp, block in zip(i, blocks, strict=True):
                lines[comp] = block
        elif kind == "forward":
            lines[i] = across(lines[i] if i < 2 else gate(lines[i], *lines[0][1:]), "circ")
        elif kind == "tables":
            after = back = back_tables(radial_basis, mp, peers, after)
        elif kind == "cycle":
            sent = cycle_stage(ids, lines[i], cycle_table_stack, parts, after)
            after = sent[0]
            lines[i] = swap(list(sent), "ax")
        elif kind == "axial":
            slot, slots = (i, 2) if i < 2 else (0, 1)
            solved = after = axial_stage(
                slot,
                slots,
                ids,
                radial_eig,
                cyc,
                axial,
                lines[i],
                axial_table_stack,
                mp,
                parts * peers,
                after,
                solved if slot else None,
            )
        elif kind == "backward":
            block = across(solved, ("ax", "circ"))
            for slot, comp in enumerate(i):
                lines[comp] = (slot, block)
        else:
            slot, block = lines[i]
            out = return_stage(slot, i, block, cycle_table_stack, weave, back, mp, parts, out)
            after = out
    return out


def tiled(mesh):
    parts, peers = mesh.shape["ax"], mesh.shape["circ"]
    rows, flat = NA // parts, NC // peers * R
    return (
        parts & (parts - 1) == 0
        and peers & (peers - 1) == 0
        and R == 32
        and R % peers == 0
        and peers * (R // peers) * 8 == 8 * R
        and rows % LANES == 0
        and (NC // parts) % LANES == 0
        and flat % (2 * LANES) == 0
        and (NC // peers) % 16 == 0
        and (rows // peers) % 16 == 0
        and HALF % (R // peers) == 0
        and peers % 2 == 0
    )


def solution(mesh):
    return jax.shard_map(
        body if tiled(mesh) else plain_body,
        mesh=mesh,
        in_specs=(
            P(None, "ax", "circ"),
            P(None, "ax", "circ"),
            P(None, "ax", "circ"),
            P("ax", "circ"),
            P(),
            P(),
            P(),
            P(),
            P(),
            P(),
        ),
        out_specs=P(None, ("ax", "circ"), None),
        check_vma=False,
    )
```
